512 devices in a mesh: elem: 128 (over z, y, x_hi), mp: 4 (over x_lo, core).
Axes of the slice: x: 4 (x_hi: 2, x_lo: 2; x = x_hi * 2 + x_lo), y: 4, z: 16, core: 2. Of those that a mesh axis runs over, the one named last changes fastest.
Arguments:
- state_field: float32 [49, 1536, 128], P(None, 'elem'), may hold values from -6 to 6
- diffusion: float32 [128], replicated, may hold values from 0.01 to 0.05
- stretch_of_column: int32 [32, 1024], P(None, 'elem'), may hold values from -1 to 127, as said below
- w_in: bfloat16 [16, 512], replicated, may hold values from -1.5 to 1.5
- level_embed: bfloat16 [8, 512], replicated, may hold values from -6 to 6
- w_qkv: bfloat16 [3, 512, 512], P(None, None, 'mp'), may hold values from -0.25 to 0.25
- w_out: bfloat16 [512, 512], P('mp'), may hold values from -0.25 to 0.25
- w_up: bfloat16 [512, 2048], P(None, 'mp'), may hold values from -0.25 to 0.25
- w_down: bfloat16 [2048, 512], P('mp'), may hold values from -0.125 to 0.125
- w_read: float32 [512, 16], replicated, may hold values from -0.25 to 0.25
Outputs:
- new_state: float32 [49, 1536, 128], P(None, 'elem')
- tendency: float32 [32, 1024, 128], P(None, 'elem')
The draws below stay inside these ranges and needn't reach their ends.
Inputs may be any that keep to these rules, and one draw needn't show every extreme that they name: `stretch_of_column`: exactly 128 columns of the whole array name each stretch (batch); a column's results don't depend on which batch it is in. Within the columns of one index of elem no stretch is named more than 2 times, and some stretch exactly 2 times. How many columns of one index of elem name a stretch varies from 0 to 256 over the indices.
All inputs are finite; a program needn't handle non-finite values.
Results may differ from the reference program's by a relative error of at most 0.0042.
Values may be sent and summed in bfloat16 or wider, within the bound.
A program may use at most 64 MiB of HBM per device.

```python
import math
import jax
import jax.numpy as jnp
import numpy as np
from jax import lax

LEV = 8
NV = 16
WID = 512
HEADS = 8
FF = 2048
Y = 49
X = 1536
F = 128
PY = 32
PX = 1024
COLS_DEV = 256
STRETCHES = 128


def draw_stretch_of_column(key, part):
    key = jax.random.fold_in(key, 11)
    key_counts, key_labels, key_order = jax.random.split(key, 3)
    half_count = COLS_DEV // 2
    excess = jax.random.randint(key_counts, (STRETCHES // 2,), 0, half_count + 1)
    excess = excess.at[0].set(half_count)
    paired = jnp.concatenate([half_count + excess, half_count - excess]).astype(jnp.int32)
    labels = jax.random.permutation(key_labels, STRETCHES)
    counts = jnp.zeros((STRETCHES,), jnp.int32).at[labels].set(paired)
    starts = jnp.cumsum(counts) - counts
    order_keys = jax.random.split(key_order, STRETCHES)
    ordering = jax.vmap(lambda subkey: jax.random.permutation(subkey, COLS_DEV))(order_keys)
    cloudy = ordering < counts[:, None]
    ranks = jnp.cumsum(cloudy.astype(jnp.int32), axis=1) - 1
    stretch_ids = jnp.where(cloudy, (starts[:, None] + ranks) % STRETCHES, -1)
    stretch_ids = stretch_ids.reshape(STRETCHES, PY, PX // STRETCHES)
    return jnp.transpose(stretch_ids, (1, 0, 2)).reshape(PY, PX).astype(jnp.int32)


def block_scale(stream_key, extent, shards, low, high):
    loudness = 1.0
    for dim, blocks in shards:
        draws = jax.random.uniform(jax.random.fold_in(jax.random.fold_in(stream_key, 6), dim), (blocks,), jnp.float32, low / len(shards), high / len(shards))
        loudness = loudness * jnp.repeat(jnp.exp(draws), extent[dim] // blocks).reshape((-1,) + (1,) * (len(extent) - 1 - dim))
    return loudness


def noise(key, extent, scale, bound, cuts=(), kind=jnp.bfloat16):
    gain = block_scale(key, extent, cuts, -0.22, 0.18) if cuts else 1.0
    entries = jax.random.normal(key, extent, jnp.float32) * scale * gain
    return jnp.minimum(jnp.maximum(entries, -bound), bound).astype(kind)


def setup_inputs(seed: int = 0) -> dict:
    streams_of = jax.random.split(jax.random.key(seed), 11)
    state_field = noise(streams_of[0], (Y, X, F), 1.0, 6.0, ((1, 128),), jnp.float32)
    diffusion = jnp.clip(jnp.exp(jax.random.uniform(streams_of[1], (F,), jnp.float32, math.log(0.01), math.log(0.05))), 0.01, 0.05)
    stretch_of_column = draw_stretch_of_column(jax.random.fold_in(streams_of[10], 71), 0)
    w_in = noise(streams_of[3], (NV, WID), NV ** -0.5, 1.5)
    level_embed = noise(streams_of[4], (LEV, WID), 1.0, 6.0)
    w_qkv = noise(streams_of[5], (3, WID, WID), WID ** -0.5, 0.25, ((2, 4),))
    w_out = noise(streams_of[6], (WID, WID), WID ** -0.5, 0.25, ((0, 4),))
    w_up = noise(streams_of[7], (WID, FF), WID ** -0.5, 0.25, ((1, 4),))
    w_down = noise(streams_of[8], (FF, WID), FF ** -0.5, 0.125, ((0, 4),))
    w_read = noise(streams_of[9], (WID, NV), WID ** -0.5, 0.25, (), jnp.float32)
    return dict(state_field=state_field, diffusion=diffusion, stretch_of_column=stretch_of_column, w_in=w_in, level_embed=level_embed, w_qkv=w_qkv, w_out=w_out, w_up=w_up, w_down=w_down, w_read=w_read)


def basis_weight(points, index):
    return np.prod([points[index] - points[other] for other in range(4) if other != index])

def gll_tables():
    points = np.array([-1.0, -1.0 / math.sqrt(5.0), 1.0 / math.sqrt(5.0), 1.0])
    quadrature = np.array([1.0, 5.0, 5.0, 1.0]) / 6.0
    derivative = np.zeros((4, 4))
    for row_index in range(4):
        for col_index in range(4):
            if row_index == col_index:
                derivative[row_index, col_index] = sum((1.0 / (points[row_index] - points[other]) for other in range(4) if other != row_index))
            else:
                derivative[row_index, col_index] = basis_weight(points, row_index) / basis_weight(points, col_index) / (points[row_index] - points[col_index])
    remap = np.array([[0.375, 0.5, 0.125, 0.0], [0.0, 0.125, 0.5, 0.375]])
    return (derivative.astype(np.float32), quadrature.astype(np.float32), remap.astype(np.float32))

def elements(extended, cells_y, cells_x):
    node_rows = extended.shape[0]
    feature = extended.shape[2]
    inner_x = extended[:, :3 * cells_x].reshape(node_rows, cells_x, 3, feature)
    edge_x = extended[:, 3:3 * cells_x + 1:3][:, :, None]
    along_x = jnp.concatenate([inner_x, edge_x], axis=2)
    inner_y = along_x[:3 * cells_y].reshape(cells_y, 3, cells_x, 4, feature)
    edge_y = along_x[3:3 * cells_y + 1:3][:, None]
    return jnp.concatenate([inner_y, edge_y], axis=1)

def stiffness(nodal, derivative, quadrature):
    dmat = jnp.asarray(derivative)
    weight = jnp.asarray(quadrature)
    grad_x = jnp.einsum('ik,ybxkf->ybxif', dmat, nodal, precision=lax.Precision.HIGHEST)
    grad_y = jnp.einsum('jk,ykxaf->yjxaf', dmat, nodal, precision=lax.Precision.HIGHEST)
    weighted = dmat * weight[:, None]
    term_x = jnp.einsum('ia,ybxif->ybxaf', weighted, grad_x, precision=lax.Precision.HIGHEST)
    term_y = jnp.einsum('jb,yjxaf->ybxaf', weighted, grad_y, precision=lax.Precision.HIGHEST)
    return -(weight[None, :, None, None, None] * term_x + weight[None, None, None, :, None] * term_y)

def assemble_rows(stiff):
    cells_y, _, cells_x, _, feature = stiff.shape
    inner = stiff[:, :3].reshape(3 * cells_y, cells_x, 4, feature)
    inner = jnp.pad(inner, ((0, 1), (0, 0), (0, 0), (0, 0)))
    zero_part = jnp.zeros_like(stiff[:, 3])
    trailing = jnp.stack([zero_part, zero_part, stiff[:, 3]], axis=1).reshape(3 * cells_y, cells_x, 4, feature)
    trailing = jnp.pad(trailing, ((1, 0), (0, 0), (0, 0), (0, 0)))
    return inner + trailing

def node_mass(node_rows, node_cols):
    row_index = jnp.arange(node_rows)
    col_index = jnp.arange(node_cols)
    mass_y = jnp.where((row_index == 0) | (row_index == node_rows - 1), 1.0 / 6.0, jnp.where(row_index % 3 == 0, 1.0 / 3.0, 5.0 / 6.0))
    mass_x = jnp.where(col_index % 3 == 0, 1.0 / 3.0, 5.0 / 6.0)
    return (mass_y[:, None] * mass_x[None, :]).astype(jnp.float32)

def physics(columns, w_in, level_embed, w_qkv, w_out, w_up, w_down, w_read):
    count = columns.shape[0]
    nvar = w_in.shape[0]
    width = w_in.shape[1]
    levels = level_embed.shape[0]
    head_dim = width // HEADS
    per_level = columns.reshape(count * levels, nvar)
    embed = jnp.dot(per_level, w_in, preferred_element_type=jnp.float32).reshape(count, levels, width)
    embed = (embed + level_embed.astype(jnp.float32)[None]).reshape(count * levels, width)
    normed = (embed * lax.rsqrt(lax.optimization_barrier(jnp.mean(embed * embed, axis=-1, keepdims=True)) + 1e-05)).astype(jnp.bfloat16)
    query = jnp.dot(normed, w_qkv[0], preferred_element_type=jnp.float32).astype(jnp.bfloat16)
    keys = jnp.dot(normed, w_qkv[1], preferred_element_type=jnp.float32).astype(jnp.bfloat16)
    values = jnp.dot(normed, w_qkv[2], preferred_element_type=jnp.float32).astype(jnp.bfloat16)
    heads_count = w_qkv.shape[2] // head_dim
    query = query.reshape(count, levels, heads_count, head_dim).astype(jnp.float32)
    keys = keys.reshape(count, levels, heads_count, head_dim).astype(jnp.float32)
    values = values.reshape(count, levels, heads_count, head_dim).astype(jnp.float32)
    scores = jnp.einsum('nlhd,nmhd->nhlm', query, keys) * (1.0 / math.sqrt(head_dim))
    expo = jnp.exp(scores)
    prob = (expo / lax.optimization_barrier(jnp.sum(expo, axis=-1, keepdims=True))).astype(jnp.bfloat16)
    mixed = jnp.einsum('nhlm,nmhd->nlhd', prob.astype(jnp.float32), values).astype(jnp.bfloat16)
    mixed = mixed.reshape(count * levels, heads_count * head_dim)
    attended = jnp.dot(mixed, w_out, preferred_element_type=jnp.float32)
    hidden = jax.nn.gelu(jnp.dot(normed, w_up, preferred_element_type=jnp.float32), approximate=True).astype(jnp.bfloat16)
    processed = jnp.dot(hidden, w_down, preferred_element_type=jnp.float32)
    summed = embed + attended + processed
    return jnp.dot(summed, w_read, precision=lax.Precision.HIGHEST).reshape(count, levels * nvar)

def with_east(field):
    return jnp.concatenate([field, field[:, :1]], axis=1)

def reference(state_field, diffusion, stretch_of_column, w_in, level_embed, w_qkv, w_out, w_up, w_down, w_read):
    derivative, quadrature, remap = gll_tables()
    node_rows = state_field.shape[0]
    node_cols = state_field.shape[1]
    feature = state_field.shape[2]
    cells_y = (node_rows - 1) // 3
    cells_x = node_cols // 3
    stiff = stiffness(elements(with_east(state_field), cells_y, cells_x), derivative, quadrature)
    gathered = assemble_rows(stiff)
    inner_cols = gathered[:, :, :3].reshape(node_rows, node_cols, feature)
    zero_part = jnp.zeros_like(gathered[:, :, 3])
    trailing = jnp.stack([zero_part, zero_part, gathered[:, :, 3]], axis=2).reshape(node_rows, node_cols, feature)
    assembled = inner_cols + jnp.roll(trailing, 1, axis=1)
    new_state = state_field + diffusion * (assembled / node_mass(node_rows, node_cols)[:, :, None])
    fine = elements(with_east(new_state), cells_y, cells_x)
    remap_table = jnp.asarray(remap)
    columns = jnp.einsum('cb,da,ybxaf->ycxdf', remap_table, remap_table, fine, precision=lax.Precision.HIGHEST)
    columns = columns.reshape(4 * cells_y * cells_x, feature).astype(jnp.bfloat16)
    stretch_flat = stretch_of_column.reshape(-1)
    cloudy_total = STRETCHES * (COLS_DEV // 2)
    ordering = jnp.argsort((stretch_flat < 0).astype(jnp.int32), stable=True)[:cloudy_total].astype(jnp.int32)
    blocks = columns[ordering].reshape(STRETCHES, COLS_DEV // 2, feature)

    def run_block(block):
        return physics(block, w_in, level_embed, w_qkv, w_out, w_up, w_down, w_read)
    results = lax.map(run_block, blocks).reshape(cloudy_total, feature)
    tendency = jnp.zeros((columns.shape[0], feature), jnp.float32).at[ordering].set(results)
    return (new_state, tendency.reshape(2 * cells_y, 2 * cells_x, feature))
```

```python
import math

import jax
import jax.numpy as jnp
import numpy as np
from jax import lax
from jax.experimental import pallas as pl
from jax.experimental.pallas import tpu as pltpu
from jax.sharding import PartitionSpec as P

MESH = pl.DeviceIdType.MESH
F32 = jnp.float32
BF16 = jnp.bfloat16
HIGHEST = lax.Precision.HIGHEST

LEV = 8
NV = 16
F = 128
HEAD = 64
Y = 49
ROWS = 56
PAD = 8
CELLS = 64
TOK = LEV * CELLS
KU = 32


def stiffness_1d():
    points = np.array([-1.0, -1.0 / math.sqrt(5.0), 1.0 / math.sqrt(5.0), 1.0])
    weight = np.array([1.0, 5.0, 5.0, 1.0]) / 6.0
    basis = [np.prod([points[i] - points[o] for o in range(4) if o != i]) for i in range(4)]
    dmat = np.zeros((4, 4))
    for i in range(4):
        for k in range(4):
            if i == k:
                dmat[i, k] = sum(1.0 / (points[i] - points[o]) for o in range(4) if o != i)
            else:
                dmat[i, k] = basis[i] / basis[k] / (points[i] - points[k])
    return dmat.T @ (weight[:, None] * dmat)


KM = stiffness_1d()


def nt(a, b, precision=None):
    return lax.dot_general(a, b, (((1,), (1,)), ((), ())), precision=precision, preferred_element_type=F32)


def tn(a, b):
    return lax.dot_general(a, b, (((0,), (0,)), ((), ())), preferred_element_type=F32)


def nn(a, b):
    return jnp.dot(a, b, preferred_element_type=F32)


def iota(shape, dim):
    return lax.broadcasted_iota(jnp.int32, shape, dim)


def split2(x):
    high = x.astype(BF16)
    return high, (x - high.astype(F32)).astype(BF16)


def lane_turn(x, by):
    return x if by == 0 else jnp.concatenate([x[:, by:], x[:, :by]], axis=1)


def band_along_y(offset):
    y = iota((ROWS, F), 0)
    kind = y - 3 * ((y * 171) >> 9)
    out = jnp.zeros((ROWS, F), F32)
    if 0 <= offset + 1 < 4:
        out = jnp.where(kind == 1, F32(1.2 * KM[1, offset + 1]), out)
    if 0 <= offset + 2 < 4:
        out = jnp.where(kind == 2, F32(1.2 * KM[2, offset + 2]), out)
    corner = jnp.zeros((ROWS, F), F32)
    if offset >= 0:
        corner = corner + jnp.where(y < Y - 1, F32(KM[0, offset]), F32(0))
    if offset <= 0:
        corner = corner + jnp.where(y > 0, F32(KM[3, offset + 3]), F32(0))
    corner = corner * jnp.where((y == 0) | (y == Y - 1), F32(6), F32(3))
    out = jnp.where(kind == 0, corner, out)
    return jnp.where(y < Y, out, F32(0))


def kernel(
    elems, state, diff, stretch, w_in, lemb, w_qkv, w_out, w_up, w_down, w_read,
    new_out, tend_out,
    st, ext, cy, fresh, n12, f12, gsend, grecv, psend, precv,
    vdiff, vstretch, vin, vlev, vqkv, vwout, vup, vdown, vread,
    msg, natural, tbuf, tend,
    load_sem, out_sem, halo_send, halo_recv, msg_send, msg_recv, t_send, t_recv,
):
    me = lax.axis_index("elem")
    j = lax.axis_index("mp")
    east = lax.rem(me + 1, elems)
    west = lax.rem(me + elems - 1, elems)
    peers = (None, j + 1 - 2 * lax.rem(j, 2), lax.rem(j + 2, 4), 3 - j)

    loads = [
        pltpu.make_async_copy(src, dst, load_sem.at[i])
        for i, (src, dst) in enumerate(
            [
                (state, st), (diff, vdiff), (w_in, vin), (lemb, vlev), (w_read, vread),
                (w_qkv, vqkv), (w_up, vup), (w_out, vwout), (w_down, vdown), (stretch, vstretch),
            ]
        )
    ]
    for copy in loads:
        copy.start()

    barrier = pltpu.get_barrier_semaphore()
    for place in ({"elem": east}, {"elem": west}, {"mp": peers[1]}, {"mp": peers[2]}, {"mp": peers[3]}):
        pl.semaphore_signal(barrier, inc=1, device_id=place, device_id_type=MESH)

    for offset in range(-3, 4):
        cy[offset + 3] = band_along_y(offset)
    ext[:, :, 0:PAD, :] = jnp.zeros((4, 3, PAD, F), F32)
    ext[:, :, PAD + 48 : PAD + 64, :] = jnp.zeros((4, 3, 16, F), F32)

    def far(src, dst, k, place):
        return pltpu.make_async_remote_copy(
            src_ref=src, dst_ref=dst, send_sem=halo_send.at[k], recv_sem=halo_recv.at[k],
            device_id=place, device_id_type=MESH,
        )

    first_row = pl.multiple_of(8 * ((3 * j) // 2), 8)
    send_f = far(state.at[0, 0], f12, 0, {"elem": west})
    send_p = far(psend.at[pl.ds(first_row, 24)], precv, 1, {"elem": west})
    send_g = far(gsend, grecv, 2, {"elem": east})

    pl.semaphore_wait(barrier, 5)
    send_f.start()

    loads[0].wait()
    loads[1].wait()
    ext[:, :, PAD : PAD + Y, :] = st[...]
    d = vdiff[...]
    body = slice(PAD, PAD + ROWS)
    f0, f1, f2, f3 = ext[0, 0, body], ext[0, 1, body], ext[0, 2, body], ext[1, 0, body]
    lap = 3.0 * (F32(2 * KM[0, 0]) * f0 + F32(KM[0, 1]) * f1 + F32(KM[0, 2]) * f2 + F32(KM[0, 3]) * f3)
    for offset in range(-3, 4):
        lap = lap + cy[offset + 3] * ext[0, 0, PAD + offset : PAD + offset + ROWS]
    psend[...] = f0 - d * lap
    f0, f1, f2 = ext[3, 0, body], ext[3, 1, body], ext[3, 2, body]
    gsend[...] = d * (3.0 * (F32(KM[3, 0]) * f0 + F32(KM[3, 1]) * f1 + F32(KM[3, 2]) * f2))
    send_g.start()
    send_p.start()

    for copy in loads[2:9]:
        copy.wait()
    basis = jnp.concatenate(
        [vin[...].astype(F32), vlev[...].astype(F32), jnp.zeros((8, 512), F32)], axis=0
    ).astype(BF16)
    read_high, read_low = split2(vread[...])
    read2 = jnp.concatenate([read_high, read_low], axis=0)
    up = nn(basis, vup[...])
    query, key, value = nn(basis, vqkv[0]), nn(basis, vqkv[1]), nn(basis, vqkv[2])
    both = nt(read2, vwout[...])
    out_read = both[:NV] + both[NV:]
    both = nt(read2, vdown[...])
    down_read = (both[:NV] + both[NV:]) * 0.5
    lane = iota((1, 128), 1)
    heads = (lane < HEAD, lane >= HEAD)
    key = key[:24] * (1.0 / math.sqrt(HEAD))
    zero_key = jnp.zeros((48, 128), F32)
    zero_out = jnp.zeros((32, 128), F32)
    keys = jnp.concatenate([jnp.where(h, key, 0.0) for h in heads], axis=0)
    outs = jnp.concatenate([jnp.where(h, out_read, 0.0) for h in heads], axis=0)
    right = jnp.concatenate(
        [
            jnp.concatenate([keys, zero_key], axis=1),
            jnp.concatenate([zero_out, outs], axis=1),
            jnp.zeros((48, 256), F32),
        ],
        axis=0,
    )
    attend = nt(jnp.concatenate([query, value], axis=1), right, HIGHEST)
    msg[0, 0:32, 0:512] = up.astype(BF16)
    msg[0, 0:32, 512:640] = attend.astype(BF16)
    msg[0, 32:48, 0:512] = down_read.astype(BF16)
    msg[0, 32:48, 512:640] = jnp.zeros((16, 128), BF16)
    msgs = []
    for r in (2, 3, 1):
        copy = pltpu.make_async_remote_copy(
            src_ref=msg.at[0], dst_ref=msg.at[r], send_sem=msg_send.at[r], recv_sem=msg_recv.at[r],
            device_id={"mp": peers[r]}, device_id_type=MESH,
        )
        copy.start()
        msgs.append(copy)
    msg_of = {2: msgs[0], 3: msgs[1], 1: msgs[2]}

    gram = nt(basis, basis)
    gram_high = gram.astype(BF16)
    gram_mid, gram_low = split2(gram - gram_high.astype(F32))
    both = nt(read2, basis)
    own_high, own_low = split2(both[:NV] + both[NV:])
    left = jnp.concatenate([gram_high, gram_mid, gram_low, own_high, own_low], axis=0)

    for tile in range(7):
        at = PAD + 8 * tile
        lap = cy[0, 8 * tile : 8 * tile + 8] * ext[:, :, at - 3 : at + 5]
        for offset in range(-2, 4):
            lap = lap + cy[offset + 3, 8 * tile : 8 * tile + 8] * ext[:, :, at + offset : at + offset + 8]
        f0, f1, f2 = ext[:, 0, at : at + 8], ext[:, 1, at : at + 8], ext[:, 2, at : at + 8]
        nothing = jnp.zeros((1, 8, F), F32)
        f3 = jnp.concatenate([f0[1:], nothing], axis=0)
        into = F32(3 * KM[3, 0]) * f0 + F32(3 * KM[3, 1]) * f1 + F32(3 * KM[3, 2]) * f2
        lap0 = (
            F32(6 * KM[0, 0]) * f0 + F32(3 * KM[0, 1]) * f1 + F32(3 * KM[0, 2]) * f2 + F32(3 * KM[0, 3]) * f3
            + jnp.concatenate([nothing, into[:3]], axis=0)
        )
        lap1 = (
            F32(1.2 * KM[1, 0]) * f0 + F32(1.2 * KM[1, 1]) * f1
            + F32(1.2 * KM[1, 2]) * f2 + F32(1.2 * KM[1, 3]) * f3
        )
        lap2 = (
            F32(1.2 * KM[2, 0]) * f0 + F32(1.2 * KM[2, 1]) * f1
            + F32(1.2 * KM[2, 2]) * f2 + F32(1.2 * KM[2, 3]) * f3
        )
        rows = 8 if tile < 6 else 1
        for a, (f, along) in enumerate(((f0, lap0), (f1, lap1), (f2, lap2))):
            fresh[:, a, 8 * tile : 8 * tile + rows] = (f - d * (lap[:, a] + along))[:, :rows]

    send_f.wait_recv()
    for a, weight in enumerate((3 * KM[0, 3], 1.2 * KM[1, 3], 1.2 * KM[2, 3])):
        fresh[3, a] = fresh[3, a] - (d * F32(weight)) * f12[...]
    send_g.wait_recv()
    fresh[0, 0] = fresh[0, 0] - grecv[0:Y]
    send_p.wait_recv()
    n12[...] = precv[...] - gsend[pl.ds(first_row, 24)]
    state_copy = pltpu.make_async_copy(fresh, new_out, out_sem.at[0])
    state_copy.start()

    taps = [fresh[:, :, pl.ds(12 * j + b, 4, stride=3), :].reshape(12, 4, F) for b in range(4)]
    begin = 4 * lax.rem(j, 2)
    taps = [
        jnp.concatenate([tap, n12[pl.ds(begin + b, 4, stride=3), :][None]], axis=0)
        for b, tap in enumerate(taps)
    ]
    across = (
        0.375 * jnp.concatenate([taps[0], taps[3]], axis=1)
        + 0.5 * jnp.concatenate([taps[1], taps[2]], axis=1)
        + 0.125 * jnp.concatenate([taps[2], taps[1]], axis=1)
    )
    cells = []
    for e in range(4):
        x0, x1, x2, x3 = (across[3 * e + a] for a in range(4))
        cells.append(0.375 * x0 + 0.5 * x1 + 0.125 * x2)
        cells.append(0.125 * x1 + 0.5 * x2 + 0.375 * x3)
    cells = jnp.concatenate(cells, axis=0).astype(BF16).astype(F32)

    turned = jnp.concatenate([cells, pltpu.roll(cells, F - NV, 1)], axis=0).T
    variables = jnp.concatenate([turned[32 * p : 32 * p + NV] for p in range(4)], axis=1)
    level = (iota((16, TOK), 1) >> 6) == iota((16, TOK), 0)
    u = jnp.concatenate([variables, jnp.where(level, 1.0, 0.0).astype(F32)], axis=0)
    first = nn(left, u.astype(BF16))
    gram_u = first[0:KU] + first[KU : 2 * KU] + first[2 * KU : 3 * KU]
    total = first[3 * KU : 3 * KU + NV] + first[3 * KU + NV :]
    squares = jnp.sum(gram_u * u, axis=0, keepdims=True)
    scaled = u * lax.rsqrt(squares * F32(1.0 / 512) + F32(1e-5))
    high, low = split2(scaled)
    scaled2 = jnp.concatenate([high, low], axis=0)
    scaled_odd = lane_turn(scaled[:24], CELLS)

    row, col = iota((16, 128), 0), iota((16, 128), 1)
    summing = jnp.where((col >> 3) == row, 1.0, 0.0).astype(BF16)
    row, col = iota((256, 16), 0), iota((256, 16), 1)
    repeat = jnp.where(((row >> 5) == (col & 7)) & (((row >> 4) & 1) == (col >> 3)), 1.0, 0.0).astype(BF16)

    for r in (0, 1, 2, 3):
        if r:
            msg_of[r].wait_recv()
        folded = msg[r, 0:32, :]
        folded2 = jnp.concatenate([folded, folded], axis=0)
        reads = msg[r, 32:48, :]
        att = tn(folded2[:, 512:640], scaled2)
        prods = []
        for h in range(2):
            for k in range(LEV):
                other = lane_turn(scaled[:24] if k % 2 == 0 else scaled_odd, CELLS * (k - k % 2))
                prod = att[24 * h : 24 * h + 24] * other
                prods.append(prod[0:8] + prod[8:16] + prod[16:24])
        prods = jnp.concatenate(prods, axis=0).astype(BF16)
        expo = jnp.exp(nn(summing, prods))
        prob = jnp.concatenate(
            [e / jnp.sum(e, axis=0, keepdims=True) for e in (expo[0:8], expo[8:16])], axis=0
        ).astype(BF16)
        spread = nn(repeat, prob)
        values = att[48:80]
        values_odd = lane_turn(values, CELLS)
        mixed = None
        for k in range(LEV):
            other = lane_turn(values if k % 2 == 0 else values_odd, CELLS * (k - k % 2))
            term = spread[32 * k : 32 * k + 32] * other
            mixed = term if mixed is None else mixed + term
        total = total + mixed[0:16] + mixed[16:32]
        for part in range(2):
            cut = slice(256 * part, 256 * part + 256)
            x = tn(folded2[:, cut], scaled2)
            inner = x * (F32(math.sqrt(2 / math.pi)) + F32(math.sqrt(2 / math.pi) * 0.044715) * (x * x))
            hidden = (x + x * jnp.tanh(inner)).astype(BF16)
            total = total + nn(reads[:, cut], hidden)

    gap = jnp.zeros((16, 128), F32)
    pieces = []
    for p in range(4):
        pieces += [total[:, 128 * p : 128 * p + 128], gap]
    turned = jnp.concatenate(pieces, axis=0).T
    result = turned[:CELLS] + pltpu.roll(turned[CELLS:], NV, 1)
    for x in range(8):
        for c in range(2):
            natural[pl.ds(8 * c + x, 4, stride=16), :] = result[8 * x + 4 * c : 8 * x + 4 * c + 4]
    loads[9].wait()
    live = jnp.where(vstretch[...] >= 0, 1.0, 0.0).astype(BF16)
    pick = jnp.where((iota((CELLS, 8), 0) & 7) == iota((CELLS, 8), 1), 1.0, 0.0).astype(BF16)
    mine = iota((CELLS, 32), 1) == (iota((CELLS, 32), 0) >> 3) + 8 * j
    live = nn(jnp.where(mine, nn(pick, live), 0.0).astype(BF16), jnp.ones((32, F), BF16))
    tbuf[0] = jnp.where(live > 0.5, natural[...], 0.0).astype(BF16)

    sends = []
    for r in (2, 3, 1):
        copy = pltpu.make_async_remote_copy(
            src_ref=tbuf.at[0], dst_ref=tbuf.at[r], send_sem=t_send.at[r], recv_sem=t_recv.at[r],
            device_id={"mp": peers[r]}, device_id_type=MESH,
        )
        copy.start()
        sends.append(copy)
    sends = {2: sends[0], 3: sends[1], 1: sends[2]}
    owner = (j, peers[1], peers[2], peers[3])
    for r in (0, 1, 2, 3):
        if r:
            sends[r].wait_recv()
        tend[pl.ds(8 * owner[r], 8)] = tbuf[r].astype(F32).reshape(8, 8, F)
    tend_copy = pltpu.make_async_copy(tend, tend_out, out_sem.at[1])
    tend_copy.start()

    for copy in (send_f, send_p, send_g, *msgs, *sends.values()):
        copy.wait_send()
    state_copy.wait()
    tend_copy.wait()


def local(elems, state_field, diffusion, stretch, w_in, lemb, w_qkv, w_out, w_up, w_down, w_read):
    state = jnp.transpose(state_field, (1, 0, 2)).reshape(4, 3, Y, F)
    vm = pltpu.VMEM
    dma = pltpu.SemaphoreType.DMA
    new, tend = pl.pallas_call(
        lambda *refs: kernel(elems, *refs),
        out_shape=(
            jax.ShapeDtypeStruct((4, 3, Y, F), F32),
            jax.ShapeDtypeStruct((32, 8, F), F32),
        ),
        in_specs=[pl.BlockSpec(memory_space=pl.ANY)] * 10,
        out_specs=[pl.BlockSpec(memory_space=pl.ANY)] * 2,
        scratch_shapes=[
            vm((4, 3, Y, F), F32),
            vm((4, 3, PAD + 64, F), F32),
            vm((7, ROWS, F), F32),
            vm((4, 3, Y, F), F32),
            vm((24, F), F32),
            vm((Y, F), F32),
            vm((ROWS, F), F32),
            vm((ROWS, F), F32),
            vm((ROWS, F), F32),
            vm((24, F), F32),
            vm((1, F), F32),
            vm((8, 32), jnp.int32),
            vm((16, 512), BF16),
            vm((8, 512), BF16),
            vm((3, 512, 128), BF16),
            vm((128, 512), BF16),
            vm((512, 512), BF16),
            vm((512, 512), BF16),
            vm((16, 512), F32),
            vm((4, 48, 640), BF16),
            vm((CELLS, F), F32),
            vm((4, CELLS, F), BF16),
            vm((32, 8, F), F32),
            dma((10,)),
            dma((2,)),
            dma((3,)),
            dma((3,)),
            dma((4,)),
            dma((4,)),
            dma((4,)),
            dma((4,)),
        ],
        compiler_params=pltpu.CompilerParams(
            collective_id=0, has_side_effects=True, vmem_limit_bytes=40 * 1024 * 1024
        ),
        name="step",
    )(
        state,
        diffusion.reshape(1, F),
        jnp.transpose(stretch),
        w_in,
        lemb,
        w_qkv,
        w_out,
        w_up,
        w_down,
        jnp.transpose(w_read),
    )
    return jnp.transpose(new.reshape(12, Y, F), (1, 0, 2)), tend


def solution(mesh):
    elems = mesh.shape["elem"]
    in_specs = (
        P(None, "elem", None),
        P(),
        P(None, "elem"),
        P(),
        P(),
        P(None, None, "mp"),
        P("mp", None),
        P(None, "mp"),
        P("mp", None),
        P(),
    )
    out_specs = (P(None, "elem", None), P(None, "elem", None))
    return jax.shard_map(
        lambda *args: local(elems, *args), mesh=mesh, in_specs=in_specs, out_specs=out_specs, check_vma=False
    )
```

```python
import math

import jax
import jax.numpy as jnp
import numpy as np
from jax import lax
from jax.experimental import pallas as pl
from jax.experimental.pallas import tpu as pltpu
from jax.sharding import PartitionSpec as P

MESH = pl.DeviceIdType.MESH
F32 = jnp.float32
BF16 = jnp.bfloat16
HIGHEST = lax.Precision.HIGHEST

LEV = 8
NV = 16
F = 128
HEAD = 64
Y = 49
ROWS = 56
PAD = 8
CELLS = 64
TOK = LEV * CELLS
KU = 32


def stiffness_1d():
    points = np.array([-1.0, -1.0 / math.sqrt(5.0), 1.0 / math.sqrt(5.0), 1.0])
    weight = np.array([1.0, 5.0, 5.0, 1.0]) / 6.0
    basis = [np.prod([points[i] - points[o] for o in range(4) if o != i]) for i in range(4)]
    dmat = np.zeros((4, 4))
    for i in range(4):
        for k in range(4):
            if i == k:
                dmat[i, k] = sum(1.0 / (points[i] - points[o]) for o in range(4) if o != i)
            else:
                dmat[i, k] = basis[i] / basis[k] / (points[i] - points[k])
    return dmat.T @ (weight[:, None] * dmat)


KM = stiffness_1d()


def nt(a, b, precision=None):
    return lax.dot_general(a, b, (((1,), (1,)), ((), ())), precision=precision, preferred_element_type=F32)


def tn(a, b):
    return lax.dot_general(a, b, (((0,), (0,)), ((), ())), preferred_element_type=F32)


def nn(a, b):
    return jnp.dot(a, b, preferred_element_type=F32)


def iota(shape, dim):
    return lax.broadcasted_iota(jnp.int32, shape, dim)


def split2(x):
    high = x.astype(BF16)
    return high, (x - high.astype(F32)).astype(BF16)


def lane_turn(x, by):
    return x if by == 0 else jnp.concatenate([x[:, by:], x[:, :by]], axis=1)


def band_along_y(offset):
    y = iota((ROWS, F), 0)
    kind = y - 3 * ((y * 171) >> 9)
    out = jnp.zeros((ROWS, F), F32)
    if 0 <= offset + 1 < 4:
        out = jnp.where(kind == 1, F32(1.2 * KM[1, offset + 1]), out)
    if 0 <= offset + 2 < 4:
        out = jnp.where(kind == 2, F32(1.2 * KM[2, offset + 2]), out)
    corner = jnp.zeros((ROWS, F), F32)
    if offset >= 0:
        corner = corner + jnp.where(y < Y - 1, F32(KM[0, offset]), F32(0))
    if offset <= 0:
        corner = corner + jnp.where(y > 0, F32(KM[3, offset + 3]), F32(0))
    corner = corner * jnp.where((y == 0) | (y == Y - 1), F32(6), F32(3))
    out = jnp.where(kind == 0, corner, out)
    return jnp.where(y < Y, out, F32(0))


def kernel(
    elems, state, diff, stretch, w_in, lemb, w_qkv, w_out, w_up, w_down, w_read,
    fresh, tend,
    st, ext, cy, n12, f12, gsend, grecv, psend, precv,
    vdiff, vstretch, vin, vlev, vqkv, vwout, vup, vdown, vread,
    msg, natural, tbuf,
    load_sem, halo_send, halo_recv, msg_send, msg_recv, t_send, t_recv,
):
    me = lax.axis_index("elem")
    j = lax.axis_index("mp")
    east = lax.rem(me + 1, elems)
    west = lax.rem(me + elems - 1, elems)
    peers = (None, j + 1 - 2 * lax.rem(j, 2), lax.rem(j + 2, 4), 3 - j)

    loads = [
        pltpu.make_async_copy(src, dst, load_sem.at[i])
        for i, (src, dst) in enumerate(
            [
                (state, st), (diff, vdiff), (w_in, vin), (lemb, vlev), (w_read, vread),
                (w_qkv, vqkv), (w_up, vup), (w_out, vwout), (w_down, vdown), (stretch, vstretch),
            ]
        )
    ]
    for copy in loads:
        copy.start()

    barrier = pltpu.get_barrier_semaphore()
    for place in ({"elem": east}, {"elem": west}, {"mp": peers[1]}, {"mp": peers[2]}, {"mp": peers[3]}):
        pl.semaphore_signal(barrier, inc=1, device_id=place, device_id_type=MESH)

    for offset in range(-3, 4):
        cy[offset + 3] = band_along_y(offset)
    ext[:, :, 0:PAD, :] = jnp.zeros((4, 3, PAD, F), F32)
    ext[:, :, PAD + 48 : PAD + 64, :] = jnp.zeros((4, 3, 16, F), F32)

    def far(src, dst, k, place):
        return pltpu.make_async_remote_copy(
            src_ref=src, dst_ref=dst, send_sem=halo_send.at[k], recv_sem=halo_recv.at[k],
            device_id=place, device_id_type=MESH,
        )

    first_row = pl.multiple_of(8 * ((3 * j) // 2), 8)
    send_f = far(state.at[0, 0], f12, 0, {"elem": west})
    send_p = far(psend.at[pl.ds(first_row, 24)], precv, 1, {"elem": west})
    send_g = far(gsend, grecv, 2, {"elem": east})

    pl.semaphore_wait(barrier, 5)
    send_f.start()

    loads[0].wait()
    loads[1].wait()
    ext[:, :, PAD : PAD + Y, :] = st[...]
    d = vdiff[...]
    body = slice(PAD, PAD + ROWS)
    f0, f1, f2, f3 = ext[0, 0, body], ext[0, 1, body], ext[0, 2, body], ext[1, 0, body]
    lap = 3.0 * (F32(2 * KM[0, 0]) * f0 + F32(KM[0, 1]) * f1 + F32(KM[0, 2]) * f2 + F32(KM[0, 3]) * f3)
    for offset in range(-3, 4):
        lap = lap + cy[offset + 3] * ext[0, 0, PAD + offset : PAD + offset + ROWS]
    psend[...] = f0 - d * lap
    f0, f1, f2 = ext[3, 0, body], ext[3, 1, body], ext[3, 2, body]
    gsend[...] = d * (3.0 * (F32(KM[3, 0]) * f0 + F32(KM[3, 1]) * f1 + F32(KM[3, 2]) * f2))
    send_g.start()
    send_p.start()

    for copy in loads[2:9]:
        copy.wait()
    basis = jnp.concatenate(
        [vin[...].astype(F32), vlev[...].astype(F32), jnp.zeros((8, 512), F32)], axis=0
    ).astype(BF16)
    read_high, read_low = split2(vread[...])
    read2 = jnp.concatenate([read_high, read_low], axis=0)
    up = nn(basis, vup[...])
    query, key, value = nn(basis, vqkv[0]), nn(basis, vqkv[1]), nn(basis, vqkv[2])
    both = nt(read2, vwout[...])
    out_read = both[:NV] + both[NV:]
    both = nt(read2, vdown[...])
    down_read = (both[:NV] + both[NV:]) * 0.5
    lane = iota((1, 128), 1)
    heads = (lane < HEAD, lane >= HEAD)
    key = key[:24] * (1.0 / math.sqrt(HEAD))
    zero_key = jnp.zeros((48, 128), F32)
    zero_out = jnp.zeros((32, 128), F32)
    keys = jnp.concatenate([jnp.where(h, key, 0.0) for h in heads], axis=0)
    outs = jnp.concatenate([jnp.where(h, out_read, 0.0) for h in heads], axis=0)
    right = jnp.concatenate(
        [
            jnp.concatenate([keys, zero_key], axis=1),
            jnp.concatenate([zero_out, outs], axis=1),
            jnp.zeros((48, 256), F32),
        ],
        axis=0,
    )
    attend = nt(jnp.concatenate([query, value], axis=1), right, HIGHEST)
    msg[0, 0:32, 0:512] = up.astype(BF16)
    msg[0, 0:32, 512:640] = attend.astype(BF16)
    msg[0, 32:48, 0:512] = down_read.astype(BF16)
    msg[0, 32:48, 512:640] = jnp.zeros((16, 128), BF16)
    msgs = []
    for r in (2, 3, 1):
        copy = pltpu.make_async_remote_copy(
            src_ref=msg.at[0], dst_ref=msg.at[r], send_sem=msg_send.at[r], recv_sem=msg_recv.at[r],
            device_id={"mp": peers[r]}, device_id_type=MESH,
        )
        copy.start()
        msgs.append(copy)
    msg_of = {2: msgs[0], 3: msgs[1], 1: msgs[2]}

    gram = nt(basis, basis)
    gram_high = gram.astype(BF16)
    gram_mid, gram_low = split2(gram - gram_high.astype(F32))
    both = nt(read2, basis)
    own_high, own_low = split2(both[:NV] + both[NV:])
    left = jnp.concatenate([gram_high, gram_mid, gram_low, own_high, own_low], axis=0)

    for tile in range(7):
        at = PAD + 8 * tile
        lap = cy[0, 8 * tile : 8 * tile + 8] * ext[:, :, at - 3 : at + 5]
        for offset in range(-2, 4):
            lap = lap + cy[offset + 3, 8 * tile : 8 * tile + 8] * ext[:, :, at + offset : at + offset + 8]
        f0, f1, f2 = ext[:, 0, at : at + 8], ext[:, 1, at : at + 8], ext[:, 2, at : at + 8]
        nothing = jnp.zeros((1, 8, F), F32)
        f3 = jnp.concatenate([f0[1:], nothing], axis=0)
        into = F32(3 * KM[3, 0]) * f0 + F32(3 * KM[3, 1]) * f1 + F32(3 * KM[3, 2]) * f2
        lap0 = (
            F32(6 * KM[0, 0]) * f0 + F32(3 * KM[0, 1]) * f1 + F32(3 * KM[0, 2]) * f2 + F32(3 * KM[0, 3]) * f3
            + jnp.concatenate([nothing, into[:3]], axis=0)
        )
        lap1 = (
            F32(1.2 * KM[1, 0]) * f0 + F32(1.2 * KM[1, 1]) * f1
            + F32(1.2 * KM[1, 2]) * f2 + F32(1.2 * KM[1, 3]) * f3
        )
        lap2 = (
            F32(1.2 * KM[2, 0]) * f0 + F32(1.2 * KM[2, 1]) * f1
            + F32(1.2 * KM[2, 2]) * f2 + F32(1.2 * KM[2, 3]) * f3
        )
        rows = 8 if tile < 6 else 1
        for a, (f, along) in enumerate(((f0, lap0), (f1, lap1), (f2, lap2))):
            fresh[:, a, 8 * tile : 8 * tile + rows] = (f - d * (lap[:, a] + along))[:, :rows]

    send_f.wait_recv()
    for a, weight in enumerate((3 * KM[0, 3], 1.2 * KM[1, 3], 1.2 * KM[2, 3])):
        fresh[3, a] = fresh[3, a] - (d * F32(weight)) * f12[...]
    send_g.wait_recv()
    fresh[0, 0] = fresh[0, 0] - grecv[0:Y]
    send_p.wait_recv()
    n12[...] = precv[...] - gsend[pl.ds(first_row, 24)]

    taps = [fresh[:, :, pl.ds(12 * j + b, 4, stride=3), :].reshape(12, 4, F) for b in range(4)]
    begin = 4 * lax.rem(j, 2)
    taps = [
        jnp.concatenate([tap, n12[pl.ds(begin + b, 4, stride=3), :][None]], axis=0)
        for b, tap in enumerate(taps)
    ]
    across = (
        0.375 * jnp.concatenate([taps[0], taps[3]], axis=1)
        + 0.5 * jnp.concatenate([taps[1], taps[2]], axis=1)
        + 0.125 * jnp.concatenate([taps[2], taps[1]], axis=1)
    )
    cells = []
    for e in range(4):
        x0, x1, x2, x3 = (across[3 * e + a] for a in range(4))
        cells.append(0.375 * x0 + 0.5 * x1 + 0.125 * x2)
        cells.append(0.125 * x1 + 0.5 * x2 + 0.375 * x3)
    cells = jnp.concatenate(cells, axis=0).astype(BF16).astype(F32)

    turned = jnp.concatenate([cells, pltpu.roll(cells, F - NV, 1)], axis=0).T
    variables = jnp.concatenate([turned[32 * p : 32 * p + NV] for p in range(4)], axis=1)
    level = (iota((16, TOK), 1) >> 6) == iota((16, TOK), 0)
    u = jnp.concatenate([variables, jnp.where(level, 1.0, 0.0).astype(F32)], axis=0)
    first = nn(left, u.astype(BF16))
    gram_u = first[0:KU] + first[KU : 2 * KU] + first[2 * KU : 3 * KU]
    total = first[3 * KU : 3 * KU + NV] + first[3 * KU + NV :]
    squares = jnp.sum(gram_u * u, axis=0, keepdims=True)
    scaled = u * lax.rsqrt(squares * F32(1.0 / 512) + F32(1e-5))
    high, low = split2(scaled)
    scaled2 = jnp.concatenate([high, low], axis=0)
    scaled_odd = lane_turn(scaled[:24], CELLS)

    row, col = iota((16, 128), 0), iota((16, 128), 1)
    summing = jnp.where((col >> 3) == row, 1.0, 0.0).astype(BF16)
    row, col = iota((256, 16), 0), iota((256, 16), 1)
    repeat = jnp.where(((row >> 5) == (col & 7)) & (((row >> 4) & 1) == (col >> 3)), 1.0, 0.0).astype(BF16)

    for r in (0, 1, 2, 3):
        if r:
            msg_of[r].wait_recv()
        folded = msg[r, 0:32, :]
        folded2 = jnp.concatenate([folded, folded], axis=0)
        reads = msg[r, 32:48, :]
        att = tn(folded2[:, 512:640], scaled2)
        prods = []
        for h in range(2):
            for k in range(LEV):
                other = lane_turn(scaled[:24] if k % 2 == 0 else scaled_odd, CELLS * (k - k % 2))
                prod = att[24 * h : 24 * h + 24] * other
                prods.append(prod[0:8] + prod[8:16] + prod[16:24])
        prods = jnp.concatenate(prods, axis=0).astype(BF16)
        expo = jnp.exp(nn(summing, prods))
        prob = jnp.concatenate(
            [e / jnp.sum(e, axis=0, keepdims=True) for e in (expo[0:8], expo[8:16])], axis=0
        ).astype(BF16)
        spread = nn(repeat, prob)
        values = att[48:80]
        values_odd = lane_turn(values, CELLS)
        mixed = None
        for k in range(LEV):
            other = lane_turn(values if k % 2 == 0 else values_odd, CELLS * (k - k % 2))
            term = spread[32 * k : 32 * k + 32] * other
            mixed = term if mixed is None else mixed + term
        total = total + mixed[0:16] + mixed[16:32]
        for part in range(2):
            cut = slice(256 * part, 256 * part + 256)
            x = tn(folded2[:, cut], scaled2)
            inner = x * (F32(math.sqrt(2 / math.pi)) + F32(math.sqrt(2 / math.pi) * 0.044715) * (x * x))
            hidden = (x + x * jnp.tanh(inner)).astype(BF16)
            total = total + nn(reads[:, cut], hidden)

    gap = jnp.zeros((16, 128), F32)
    pieces = []
    for p in range(4):
        pieces += [total[:, 128 * p : 128 * p + 128], gap]
    turned = jnp.concatenate(pieces, axis=0).T
    result = turned[:CELLS] + pltpu.roll(turned[CELLS:], NV, 1)
    for x in range(8):
        for c in range(2):
            natural[pl.ds(8 * c + x, 4, stride=16), :] = result[8 * x + 4 * c : 8 * x + 4 * c + 4]
    loads[9].wait()
    live = jnp.where(vstretch[...] >= 0, 1.0, 0.0).astype(BF16)
    pick = jnp.where((iota((CELLS, 8), 0) & 7) == iota((CELLS, 8), 1), 1.0, 0.0).astype(BF16)
    mine = iota((CELLS, 32), 1) == (iota((CELLS, 32), 0) >> 3) + 8 * j
    live = nn(jnp.where(mine, nn(pick, live), 0.0).astype(BF16), jnp.ones((32, F), BF16))
    tbuf[0] = jnp.where(live > 0.5, natural[...], 0.0).astype(BF16)

    sends = []
    for r in (2, 3, 1):
        copy = pltpu.make_async_remote_copy(
            src_ref=tbuf.at[0], dst_ref=tbuf.at[r], send_sem=t_send.at[r], recv_sem=t_recv.at[r],
            device_id={"mp": peers[r]}, device_id_type=MESH,
        )
        copy.start()
        sends.append(copy)
    sends = {2: sends[0], 3: sends[1], 1: sends[2]}
    owner = (j, peers[1], peers[2], peers[3])
    for r in (0, 1, 2, 3):
        if r:
            sends[r].wait_recv()
        tend[pl.ds(8 * owner[r], 8)] = tbuf[r].astype(F32).reshape(8, 8, F)

    for copy in (send_f, send_p, send_g, *msgs, *sends.values()):
        copy.wait_send()


def store(new, tend, new_out, tend_out, sem):
    first = pltpu.make_async_copy(new, new_out, sem.at[0])
    second = pltpu.make_async_copy(tend, tend_out, sem.at[1])
    first.start()
    second.start()
    first.wait()
    second.wait()


def local(elems, state_field, diffusion, stretch, w_in, lemb, w_qkv, w_out, w_up, w_down, w_read):
    state = jnp.transpose(state_field, (1, 0, 2)).reshape(4, 3, Y, F)
    operands = (
        state, diffusion.reshape(1, F), jnp.transpose(stretch), w_in, lemb,
        w_qkv, w_out, w_up, w_down, jnp.transpose(w_read),
    )
    vm = pltpu.VMEM
    dma = pltpu.SemaphoreType.DMA
    new, tend = pl.pallas_call(
        lambda *refs: kernel(elems, *refs),
        out_shape=(
            jax.ShapeDtypeStruct((4, 3, Y, F), F32),
            jax.ShapeDtypeStruct((32, 8, F), F32),
        ),
        in_specs=[pl.BlockSpec(memory_space=pltpu.HBM)] * 10,
        out_specs=[pl.BlockSpec(memory_space=pltpu.VMEM)] * 2,
        scratch_shapes=[
            vm((4, 3, Y, F), F32),
            vm((4, 3, PAD + 64, F), F32),
            vm((7, ROWS, F), F32),
            vm((24, F), F32),
            vm((Y, F), F32),
            vm((ROWS, F), F32),
            vm((ROWS, F), F32),
            vm((ROWS, F), F32),
            vm((24, F), F32),
            vm((1, F), F32),
            vm((8, 32), jnp.int32),
            vm((16, 512), BF16),
            vm((8, 512), BF16),
            vm((3, 512, 128), BF16),
            vm((128, 512), BF16),
            vm((512, 512), BF16),
            vm((512, 512), BF16),
            vm((16, 512), F32),
            vm((4, 48, 640), BF16),
            vm((CELLS, F), F32),
            vm((4, CELLS, F), BF16),
            dma((10,)),
            dma((3,)),
            dma((3,)),
            dma((4,)),
            dma((4,)),
            dma((4,)),
            dma((4,)),
        ],
        compiler_params=pltpu.CompilerParams(
            collective_id=0, has_side_effects=True, vmem_limit_bytes=40 * 1024 * 1024
        ),
        name="step",
    )(*(pltpu.with_memory_space_constraint(x, pltpu.HBM) for x in operands))
    return jnp.transpose(new.reshape(12, Y, F), (1, 0, 2)), tend


def solution(mesh):
    elems = mesh.shape["elem"]
    in_specs = (
        P(None, "elem", None),
        P(),
        P(None, "elem"),
        P(),
        P(),
        P(None, None, "mp"),
        P("mp", None),
        P(None, "mp"),
        P("mp", None),
        P(),
    )
    out_specs = (P(None, "elem", None), P(None, "elem", None))
    return jax.shard_map(
        lambda *args: local(elems, *args), mesh=mesh, in_specs=in_specs, out_specs=out_specs, check_vma=False
    )
```

```python
import math

import jax
import jax.numpy as jnp
import numpy as np
from jax import lax
from jax.experimental import pallas as pl
from jax.experimental.pallas import tpu as pltpu
from jax.sharding import PartitionSpec as P

MESH = pl.DeviceIdType.MESH
F32 = jnp.float32
BF16 = jnp.bfloat16
HIGHEST = lax.Precision.HIGHEST

LEV = 8
NV = 16
F = 128
HEAD = 64
Y = 49
ROWS = 56
PAD = 8
CELLS = 64
HALF = 32
TOK = LEV * HALF
KU = 32


def stiffness_1d():
    points = np.array([-1.0, -1.0 / math.sqrt(5.0), 1.0 / math.sqrt(5.0), 1.0])
    weight = np.array([1.0, 5.0, 5.0, 1.0]) / 6.0
    basis = [np.prod([points[i] - points[o] for o in range(4) if o != i]) for i in range(4)]
    dmat = np.zeros((4, 4))
    for i in range(4):
        for k in range(4):
            if i == k:
                dmat[i, k] = sum(1.0 / (points[i] - points[o]) for o in range(4) if o != i)
            else:
                dmat[i, k] = basis[i] / basis[k] / (points[i] - points[k])
    return dmat.T @ (weight[:, None] * dmat)


KM = stiffness_1d()


def nt(a, b, precision=None):
    return lax.dot_general(a, b, (((1,), (1,)), ((), ())), precision=precision, preferred_element_type=F32)


def tn(a, b):
    return lax.dot_general(a, b, (((0,), (0,)), ((), ())), preferred_element_type=F32)


def nn(a, b):
    return jnp.dot(a, b, preferred_element_type=F32)


def iota(shape, dim):
    return lax.broadcasted_iota(jnp.int32, shape, dim)


def split2(x):
    high = x.astype(BF16)
    return high, (x - high.astype(F32)).astype(BF16)


def lane_turn(x, by):
    return x if by == 0 else jnp.concatenate([x[:, by:], x[:, :by]], axis=1)


def band_along_y(offset):
    y = iota((ROWS, F), 0)
    kind = y - 3 * ((y * 171) >> 9)
    out = jnp.zeros((ROWS, F), F32)
    if 0 <= offset + 1 < 4:
        out = jnp.where(kind == 1, F32(1.2 * KM[1, offset + 1]), out)
    if 0 <= offset + 2 < 4:
        out = jnp.where(kind == 2, F32(1.2 * KM[2, offset + 2]), out)
    corner = jnp.zeros((ROWS, F), F32)
    if offset >= 0:
        corner = corner + jnp.where(y < Y - 1, F32(KM[0, offset]), F32(0))
    if offset <= 0:
        corner = corner + jnp.where(y > 0, F32(KM[3, offset + 3]), F32(0))
    corner = corner * jnp.where((y == 0) | (y == Y - 1), F32(6), F32(3))
    out = jnp.where(kind == 0, corner, out)
    return jnp.where(y < Y, out, F32(0))


def kernel(
    elems, state, diff, stretch, w_in, lemb, w_qkv, w_out, w_up, w_down, w_read,
    fresh, tend,
    st, ext, cy, n12, f12, gsend, grecv, psend, precv,
    vdiff, vstretch, vin, vlev, vqkv, vwout, vup, vdown, vread,
    msg, mask, tbuf,
    load_sem, halo_send, halo_recv, msg_send, msg_recv, t_send, t_recv,
):
    me = lax.axis_index("elem")
    j = lax.axis_index("mp")
    peers = (None, j + 1 - 2 * lax.rem(j, 2), lax.rem(j + 2, 4), 3 - j)

    east = {"elem": lax.rem(me + 1, elems), "mp": peers[2]}
    west = {"elem": lax.rem(me + elems - 1, elems), "mp": peers[2]}
    barrier = pltpu.get_barrier_semaphore()
    for place in (east, west, {"mp": peers[2]}, {"mp": peers[3]}, {"mp": peers[1]}):
        pl.semaphore_signal(barrier, inc=1, device_id=place, device_id_type=MESH)

    loads = [
        pltpu.make_async_copy(src, dst, load_sem.at[i])
        for i, (src, dst) in enumerate(
            [
                (state, st), (diff, vdiff), (w_in, vin), (lemb, vlev), (w_read, vread),
                (w_qkv, vqkv), (w_up, vup), (w_out, vwout), (w_down, vdown), (stretch, vstretch),
            ]
        )
    ]
    for copy in loads:
        copy.start()

    for offset in range(-3, 4):
        cy[offset + 3] = band_along_y(offset)
    ext[:, :, 0:PAD, :] = jnp.zeros((4, 3, PAD, F), F32)
    ext[:, :, PAD + 48 : PAD + 64, :] = jnp.zeros((4, 3, 16, F), F32)

    def far(src, dst, k, place):
        return pltpu.make_async_remote_copy(
            src_ref=src, dst_ref=dst, send_sem=halo_send.at[k], recv_sem=halo_recv.at[k],
            device_id=place, device_id_type=MESH,
        )

    first_row = pl.multiple_of(8 * ((3 * j) // 2), 8)
    their_row = pl.multiple_of(8 * ((3 * peers[2]) // 2), 8)
    send_f = far(state.at[0, 0], f12, 0, west)
    send_p = far(psend.at[pl.ds(their_row, 24)], precv, 1, west)
    send_g = far(gsend, grecv, 2, east)

    pl.semaphore_wait(barrier, 5)
    send_f.start()

    loads[0].wait()
    loads[1].wait()
    ext[:, :, PAD : PAD + Y, :] = st[...]
    d = vdiff[...]
    body = slice(PAD, PAD + ROWS)
    f0, f1, f2, f3 = ext[0, 0, body], ext[0, 1, body], ext[0, 2, body], ext[1, 0, body]
    lap = 3.0 * (F32(2 * KM[0, 0]) * f0 + F32(KM[0, 1]) * f1 + F32(KM[0, 2]) * f2 + F32(KM[0, 3]) * f3)
    for offset in range(-3, 4):
        lap = lap + cy[offset + 3] * ext[0, 0, PAD + offset : PAD + offset + ROWS]
    psend[...] = f0 - d * lap
    f0, f1, f2 = ext[3, 0, body], ext[3, 1, body], ext[3, 2, body]
    gsend[...] = d * (3.0 * (F32(KM[3, 0]) * f0 + F32(KM[3, 1]) * f1 + F32(KM[3, 2]) * f2))
    send_g.start()
    send_p.start()

    for copy in loads[2:9]:
        copy.wait()
    basis = jnp.concatenate(
        [vin[...].astype(F32), vlev[...].astype(F32), jnp.zeros((8, 512), F32)], axis=0
    ).astype(BF16)
    read_high, read_low = split2(vread[...])
    read2 = jnp.concatenate([read_high, read_low], axis=0)
    up = nn(basis, vup[...])
    query, key, value = nn(basis, vqkv[0]), nn(basis, vqkv[1]), nn(basis, vqkv[2])
    both = nt(read2, vwout[...])
    out_read = both[:NV] + both[NV:]
    both = nt(read2, vdown[...])
    down_read = (both[:NV] + both[NV:]) * 0.5
    lane = iota((1, 128), 1)
    heads = (lane < HEAD, lane >= HEAD)
    key = key[:24] * (1.0 / math.sqrt(HEAD))
    zero_key = jnp.zeros((48, 128), F32)
    zero_out = jnp.zeros((32, 128), F32)
    keys = jnp.concatenate([jnp.where(h, key, 0.0) for h in heads], axis=0)
    outs = jnp.concatenate([jnp.where(h, out_read, 0.0) for h in heads], axis=0)
    right = jnp.concatenate(
        [
            jnp.concatenate([keys, zero_key], axis=1),
            jnp.concatenate([zero_out, outs], axis=1),
            jnp.zeros((48, 256), F32),
        ],
        axis=0,
    )
    attend = nt(jnp.concatenate([query, value], axis=1), right, HIGHEST)
    msg[0, 0:32, 0:512] = up.astype(BF16)
    msg[0, 0:32, 512:640] = attend.astype(BF16)
    msg[0, 32:48, 0:512] = down_read.astype(BF16)
    msg[0, 32:48, 512:640] = jnp.zeros((16, 128), BF16)
    msg_of = {}
    for r, held in ((2, 0), (1, 0), (3, 2)):
        msg_of[r] = pltpu.make_async_remote_copy(
            src_ref=msg.at[held], dst_ref=msg.at[r], send_sem=msg_send.at[r], recv_sem=msg_recv.at[r],
            device_id={"mp": peers[r - held]}, device_id_type=MESH,
        )
    msg_of[2].start()
    msg_of[1].start()
    forward = msg_of[3]

    gram = nt(basis, basis)
    gram_high = gram.astype(BF16)
    gram_mid, gram_low = split2(gram - gram_high.astype(F32))
    both = nt(read2, basis)
    own_high, own_low = split2(both[:NV] + both[NV:])
    left = jnp.concatenate([gram_high, gram_mid, gram_low, own_high, own_low], axis=0)

    loads[9].wait()
    live = jnp.where(vstretch[...] >= 0, 1.0, 0.0).astype(BF16)
    cell, other = iota((CELLS, 8), 0), iota((CELLS, 8), 1)
    place = (cell >> 3) & 3
    place = jnp.where(cell < HALF, place + 1, jnp.where(place == 0, 0, place + 4))
    pick = jnp.where(place == other, 1.0, 0.0).astype(BF16)
    cell, other = iota((CELLS, 32), 0), iota((CELLS, 32), 1)
    mine = other == 8 * j + 2 * (cell & 3) + ((cell >> 2) & 1)
    mask[...] = nn(jnp.where(mine, nn(pick, live), 0.0).astype(BF16), jnp.ones((32, F), BF16))

    for tile in range(7):
        at = PAD + 8 * tile
        lap = cy[0, 8 * tile : 8 * tile + 8] * ext[:, :, at - 3 : at + 5]
        for offset in range(-2, 4):
            lap = lap + cy[offset + 3, 8 * tile : 8 * tile + 8] * ext[:, :, at + offset : at + offset + 8]
        f0, f1, f2 = ext[:, 0, at : at + 8], ext[:, 1, at : at + 8], ext[:, 2, at : at + 8]
        nothing = jnp.zeros((1, 8, F), F32)
        f3 = jnp.concatenate([f0[1:], nothing], axis=0)
        into = F32(3 * KM[3, 0]) * f0 + F32(3 * KM[3, 1]) * f1 + F32(3 * KM[3, 2]) * f2
        lap0 = (
            F32(6 * KM[0, 0]) * f0 + F32(3 * KM[0, 1]) * f1 + F32(3 * KM[0, 2]) * f2 + F32(3 * KM[0, 3]) * f3
            + jnp.concatenate([nothing, into[:3]], axis=0)
        )
        lap1 = (
            F32(1.2 * KM[1, 0]) * f0 + F32(1.2 * KM[1, 1]) * f1
            + F32(1.2 * KM[1, 2]) * f2 + F32(1.2 * KM[1, 3]) * f3
        )
        lap2 = (
            F32(1.2 * KM[2, 0]) * f0 + F32(1.2 * KM[2, 1]) * f1
            + F32(1.2 * KM[2, 2]) * f2 + F32(1.2 * KM[2, 3]) * f3
        )
        rows = 8 if tile < 6 else 1
        for a, (f, along) in enumerate(((f0, lap0), (f1, lap1), (f2, lap2))):
            fresh[:, a, 8 * tile : 8 * tile + rows] = (f - d * (lap[:, a] + along))[:, :rows]

    row, col = iota((16, 128), 0), iota((16, 128), 1)
    summing = jnp.where((col >> 3) == row, 1.0, 0.0).astype(BF16)
    row, col = iota((256, 16), 0), iota((256, 16), 1)
    repeat = jnp.where(((row >> 5) == (col & 7)) & (((row >> 4) & 1) == (col >> 3)), 1.0, 0.0).astype(BF16)

    begin = 4 * lax.rem(j, 2)

    def across(x):
        taps = [
            n12[pl.ds(begin + b, 4, stride=3), :]
            if x == 12
            else fresh[x // 3, x % 3, pl.ds(12 * j + b, 4, stride=3), :]
            for b in range(4)
        ]
        return (
            0.375 * jnp.concatenate([taps[0], taps[3]], axis=0)
            + 0.5 * jnp.concatenate([taps[1], taps[2]], axis=0)
            + 0.125 * jnp.concatenate([taps[2], taps[1]], axis=0)
        )

    def prepare(places):
        nodes = {x: across(x) for x in sorted({3 * (p // 2) + p % 2 + i for p in places for i in range(3)})}
        cells = []
        for p in places:
            x0, x1, x2 = (nodes[3 * (p // 2) + p % 2 + i] for i in range(3))
            cells.append(0.375 * x0 + 0.5 * x1 + 0.125 * x2 if p % 2 == 0 else 0.125 * x0 + 0.5 * x1 + 0.375 * x2)
        cells = jnp.concatenate(cells, axis=0).astype(BF16).astype(F32)

        turned = jnp.concatenate([cells] + [pltpu.roll(cells, F - NV * q, 1) for q in (1, 2, 3)], axis=0).T
        variables = jnp.concatenate([turned[0:NV], turned[64 : 64 + NV]], axis=1)
        level = (iota((16, TOK), 1) >> 5) == iota((16, TOK), 0)
        u = jnp.concatenate([variables, jnp.where(level, 1.0, 0.0).astype(F32)], axis=0)
        first = nn(left, u.astype(BF16))
        gram_u = first[0:KU] + first[KU : 2 * KU] + first[2 * KU : 3 * KU]
        squares = jnp.sum(gram_u * u, axis=0, keepdims=True)
        scaled = u * lax.rsqrt(squares * F32(1.0 / 512) + F32(1e-5))
        high, low = split2(scaled)
        scaled2 = jnp.concatenate([high, low], axis=0)
        return dict(
            places=places,
            scaled2=scaled2,
            tokens=scaled2.astype(F32).T.astype(BF16),
            quarter=[lane_turn(scaled[:24], HALF * k) for k in range(4)],
            total=first[3 * KU : 3 * KU + NV] + first[3 * KU + NV :],
            acc=None,
            atts={},
            sums={},
            spreads={},
        )

    def open_share(half, r):
        folded = msg[r, 0:32, 512:640]
        half["atts"][r] = tn(jnp.concatenate([folded, folded], axis=0), half["scaled2"])

    def hidden_units(half, r):
        folded = msg[r, 0:32, 0:512]
        folded2 = jnp.concatenate([folded, folded], axis=0)
        reads = msg[r, 32:48, 0:512]
        for part in range(2):
            cut = slice(256 * part, 256 * part + 256)
            x = nn(half["tokens"], folded2[:, cut])
            inner = x * (F32(math.sqrt(2 / math.pi)) + F32(math.sqrt(2 / math.pi) * 0.044715) * (x * x))
            hidden = (x + x * jnp.tanh(inner)).astype(BF16)
            term = nt(hidden, reads[:, cut])
            half["acc"] = term if half["acc"] is None else half["acc"] + term

    def scores(half, r):
        att, quarter = half["atts"][r], half["quarter"]
        prods = []
        for h in range(2):
            for k in range(LEV):
                prod = att[24 * h : 24 * h + 24] * lane_turn(quarter[k % 4], 128 * (k // 4))
                prods.append(prod[0:8] + prod[8:16] + prod[16:24])
        half["sums"][r] = nn(summing, jnp.concatenate(prods, axis=0).astype(BF16))

    def probabilities(half, r):
        expo = jnp.exp(half["sums"][r])
        prob = jnp.concatenate(
            [e / jnp.sum(e, axis=0, keepdims=True) for e in (expo[0:8], expo[8:16])], axis=0
        ).astype(BF16)
        half["spreads"][r] = nn(repeat, prob)

    def mix(half, r):
        att, spread = half["atts"][r], half["spreads"][r]
        values = [lane_turn(att[48:80], HALF * k) for k in range(4)]
        mixed = None
        for k in range(LEV):
            term = spread[32 * k : 32 * k + 32] * lane_turn(values[k % 4], 128 * (k // 4))
            mixed = term if mixed is None else mixed + term
        half["total"] = half["total"] + mixed[0:16] + mixed[16:32]

    def shares(half, several):
        for r in several:
            open_share(half, r)
        stages = (hidden_units, scores, probabilities, mix)
        for step in range(len(several) + 3):
            for i, stage in enumerate(stages):
                if 0 <= step - i < len(several):
                    stage(half, several[step - i])

    def finish(half, h):
        total, acc = half["total"], half["acc"]
        gap = jnp.zeros((48, 128), F32)
        turned = jnp.concatenate([total[:, 0:128], gap, total[:, 128:256], gap], axis=0).T
        wide = jnp.concatenate([acc, jnp.zeros((TOK, F - NV), F32)], axis=1)
        turned = turned + wide[0:128] + pltpu.roll(wide[128:256], 64, 1)
        result = turned[0:HALF]
        for q in (1, 2, 3):
            result = result + pltpu.roll(turned[HALF * q : HALF * q + HALF], NV * q, 1)
        result = jnp.where(mask[HALF * h : HALF * h + HALF] > 0.5, result, 0.0)
        tbuf[0, h] = result.astype(BF16)
        copies = {}
        for r in (2, 3, 1):
            copies[r] = pltpu.make_async_remote_copy(
                src_ref=tbuf.at[0, h], dst_ref=tbuf.at[r, h], send_sem=t_send.at[r, h], recv_sem=t_recv.at[r, h],
                device_id={"mp": peers[r]}, device_id_type=MESH,
            )
            copies[r].start()
        return copies

    owner = (j, peers[1], peers[2], peers[3])

    def place_rows(half, h, r):
        block = tbuf[r, h].astype(F32)
        for i, p in enumerate(half["places"]):
            for c in range(2):
                tend[pl.ds(64 * owner[r] + 8 * c + p, 4, stride=16), :] = block[8 * i + 4 * c : 8 * i + 4 * c + 4]

    inner_half = prepare((1, 2, 3, 4))
    shares(inner_half, (0,))
    msg_of[1].wait_recv()
    shares(inner_half, (1,))
    msg_of[2].wait_recv()
    forward.start()
    shares(inner_half, (2,))
    msg_of[3].wait_recv()
    shares(inner_half, (3,))
    inner_sends = finish(inner_half, 0)

    send_f.wait_recv()
    for a, weight in enumerate((3 * KM[0, 3], 1.2 * KM[1, 3], 1.2 * KM[2, 3])):
        fresh[3, a] = fresh[3, a] - (d * F32(weight)) * f12[...]
    send_g.wait_recv()
    fresh[0, 0] = fresh[0, 0] - grecv[0:Y]
    send_p.wait_recv()
    n12[...] = precv[...] - gsend[pl.ds(first_row, 24)]
    outer_half = prepare((0, 5, 6, 7))
    shares(outer_half, (0, 1, 2, 3))
    outer_sends = finish(outer_half, 1)

    place_rows(inner_half, 0, 0)
    place_rows(outer_half, 1, 0)
    for r in (1, 2, 3):
        inner_sends[r].wait_recv()
        place_rows(inner_half, 0, r)
    for r in (1, 2, 3):
        outer_sends[r].wait_recv()
        place_rows(outer_half, 1, r)

    sent = (send_f, send_p, send_g, *msg_of.values(), *inner_sends.values(), *outer_sends.values())
    for copy in sent:
        copy.wait_send()


def local(elems, state_field, diffusion, stretch, w_in, lemb, w_qkv, w_out, w_up, w_down, w_read):
    state = jnp.transpose(state_field, (1, 0, 2)).reshape(4, 3, Y, F)
    operands = (
        state, diffusion.reshape(1, F), jnp.transpose(stretch), w_in, lemb,
        w_qkv, w_out, w_up, w_down, jnp.transpose(w_read),
    )
    vm = pltpu.VMEM
    dma = pltpu.SemaphoreType.DMA
    new, tend = pl.pallas_call(
        lambda *refs: kernel(elems, *refs),
        out_shape=(
            jax.ShapeDtypeStruct((4, 3, Y, F), F32),
            jax.ShapeDtypeStruct((256, F), F32),
        ),
        in_specs=[pl.BlockSpec(memory_space=pltpu.HBM)] * 10,
        out_specs=[pl.BlockSpec(memory_space=pltpu.VMEM)] * 2,
        scratch_shapes=[
            vm((4, 3, Y, F), F32),
            vm((4, 3, PAD + 64, F), F32),
            vm((7, ROWS, F), F32),
            vm((24, F), F32),
            vm((Y, F), F32),
            vm((ROWS, F), F32),
            vm((ROWS, F), F32),
            vm((ROWS, F), F32),
            vm((24, F), F32),
            vm((1, F), F32),
            vm((8, 32), jnp.int32),
            vm((16, 512), BF16),
            vm((8, 512), BF16),
            vm((3, 512, 128), BF16),
            vm((128, 512), BF16),
            vm((512, 512), BF16),
            vm((512, 512), BF16),
            vm((16, 512), F32),
            vm((4, 48, 640), BF16),
            vm((CELLS, F), F32),
            vm((4, 2, HALF, F), BF16),
            dma((10,)),
            dma((3,)),
            dma((3,)),
            dma((4,)),
            dma((4,)),
            dma((4, 2)),
            dma((4, 2)),
        ],
        compiler_params=pltpu.CompilerParams(
            collective_id=0, has_side_effects=True, vmem_limit_bytes=40 * 1024 * 1024
        ),
        name="step",
    )(*(pltpu.with_memory_space_constraint(x, pltpu.HBM) for x in operands))
    return jnp.transpose(new.reshape(12, Y, F), (1, 0, 2)), tend.reshape(32, 8, F)


def solution(mesh):
    elems = mesh.shape["elem"]
    in_specs = (
        P(None, "elem", None),
        P(),
        P(None, "elem"),
        P(),
        P(),
        P(None, None, "mp"),
        P("mp", None),
        P(None, "mp"),
        P("mp", None),
        P(),
    )
    out_specs = (P(None, "elem", None), P(None, "elem", None))
    return jax.shard_map(
        lambda *args: local(elems, *args), mesh=mesh, in_specs=in_specs, out_specs=out_specs, check_vma=False
    )
```

```python
import math

import jax
import jax.numpy as jnp
import numpy as np
from jax import lax
from jax.experimental import pallas as pl
from jax.experimental.pallas import tpu as pltpu
from jax.sharding import PartitionSpec as P

MESH = pl.DeviceIdType.MESH
F32 = jnp.float32
BF16 = jnp.bfloat16
HIGHEST = lax.Precision.HIGHEST

LEV = 8
NV = 16
F = 128
HEAD = 64
Y = 49
ROWS = 56
PAD = 8
ACROSS = 16
CELLS = 8 * ACROSS
KU = 32


def stiffness_1d():
    points = np.array([-1.0, -1.0 / math.sqrt(5.0), 1.0 / math.sqrt(5.0), 1.0])
    weight = np.array([1.0, 5.0, 5.0, 1.0]) / 6.0
    basis = [np.prod([points[i] - points[o] for o in range(4) if o != i]) for i in range(4)]
    dmat = np.zeros((4, 4))
    for i in range(4):
        for k in range(4):
            if i == k:
                dmat[i, k] = sum(1.0 / (points[i] - points[o]) for o in range(4) if o != i)
            else:
                dmat[i, k] = basis[i] / basis[k] / (points[i] - points[k])
    return dmat.T @ (weight[:, None] * dmat)


KM = stiffness_1d()


def nt(a, b, precision=None):
    return lax.dot_general(a, b, (((1,), (1,)), ((), ())), precision=precision, preferred_element_type=F32)


def tn(a, b):
    return lax.dot_general(a, b, (((0,), (0,)), ((), ())), preferred_element_type=F32)


def nn(a, b):
    return jnp.dot(a, b, preferred_element_type=F32)


def iota(shape, dim):
    return lax.broadcasted_iota(jnp.int32, shape, dim)


def split2(x):
    high = x.astype(BF16)
    return high, (x - high.astype(F32)).astype(BF16)


def lane_turn(x, by):
    return x if by == 0 else jnp.concatenate([x[:, by:], x[:, :by]], axis=1)


def band_along_y(offset):
    y = iota((ROWS, F), 0)
    kind = y - 3 * ((y * 171) >> 9)
    out = jnp.zeros((ROWS, F), F32)
    if 0 <= offset + 1 < 4:
        out = jnp.where(kind == 1, F32(1.2 * KM[1, offset + 1]), out)
    if 0 <= offset + 2 < 4:
        out = jnp.where(kind == 2, F32(1.2 * KM[2, offset + 2]), out)
    corner = jnp.zeros((ROWS, F), F32)
    if offset >= 0:
        corner = corner + jnp.where(y < Y - 1, F32(KM[0, offset]), F32(0))
    if offset <= 0:
        corner = corner + jnp.where(y > 0, F32(KM[3, offset + 3]), F32(0))
    corner = corner * jnp.where((y == 0) | (y == Y - 1), F32(6), F32(3))
    out = jnp.where(kind == 0, corner, out)
    return jnp.where(y < Y, out, F32(0))


def kernel(
    elems, state, diff, stretch, w_in, lemb, w_qkv, w_out, w_up, w_down, w_read,
    fresh, tend,
    st, ext, cy, n12, gown, f12, gsend, grecv, psend, precv,
    vdiff, vstretch, vin, vlev, vqkv, vwout, vup, vdown, vread,
    msg, mask, tbuf0, tbuf1,
    load_sem, halo_send, halo_recv, msg_send, msg_recv, t_send, t_recv, west_in,
):
    me = lax.axis_index("elem")
    j = lax.axis_index("mp")
    tbufs = (tbuf0, tbuf1)
    peers = (None, j + 1 - 2 * lax.rem(j, 2), lax.rem(j + 2, 4), 3 - j)

    core = lax.rem(j, 2)
    east = {"elem": lax.rem(me + 1, elems), "mp": peers[2]}
    west = {"elem": lax.rem(me + elems - 1, elems), "mp": peers[2]}

    barrier = pltpu.get_barrier_semaphore()
    for place in (west, {"mp": peers[2]}, {"mp": peers[3]}, {"mp": peers[1]}):
        pl.semaphore_signal(barrier, inc=1, device_id=place, device_id_type=MESH)

    @pl.when(me != elems - 1)
    def _():
        pl.semaphore_signal(barrier, inc=1, device_id=east, device_id_type=MESH)

    loads = [
        pltpu.make_async_copy(src, dst, load_sem.at[i])
        for i, (src, dst) in enumerate(
            [
                (state, st), (diff, vdiff), (w_in, vin), (lemb, vlev), (w_read, vread),
                (w_qkv, vqkv), (w_up, vup), (w_out, vwout), (w_down, vdown), (stretch, vstretch),
            ]
        )
    ]
    for copy in loads:
        copy.start()

    for offset in range(-3, 4):
        cy[offset + 3] = band_along_y(offset)
    ext[:, :, 0:PAD, :] = jnp.zeros((4, 3, PAD, F), F32)
    ext[:, :, PAD + 48 : PAD + 64, :] = jnp.zeros((4, 3, 16, F), F32)

    def far(src, dst, k, place):
        return pltpu.make_async_remote_copy(
            src_ref=src, dst_ref=dst, send_sem=halo_send.at[k], recv_sem=halo_recv.at[k],
            device_id=place, device_id_type=MESH,
        )

    first_row = pl.multiple_of(24 * core, 8)
    send_f = far(state.at[0, 0], f12, 0, west)
    send_p = far(psend.at[pl.ds(first_row, 32)], precv, 1, west)
    send_g = far(gsend, grecv, 2, east)

    loads[0].wait()
    loads[1].wait()
    d = vdiff[...]
    share = d * (3.0 * (F32(KM[3, 0]) * st[3, 0] + F32(KM[3, 1]) * st[3, 1] + F32(KM[3, 2]) * st[3, 2]))
    gown[0:Y] = share
    gsend[...] = jnp.concatenate([share, jnp.zeros((64 - Y, F), F32)], axis=0).astype(BF16)

    ext[:, :, PAD : PAD + Y, :] = st[...]
    body = slice(PAD, PAD + ROWS)
    f0, f1, f2, f3 = ext[0, 0, body], ext[0, 1, body], ext[0, 2, body], ext[1, 0, body]
    lap = 3.0 * (F32(2 * KM[0, 0]) * f0 + F32(KM[0, 1]) * f1 + F32(KM[0, 2]) * f2 + F32(KM[0, 3]) * f3)
    for offset in range(-3, 4):
        lap = lap + cy[offset + 3] * ext[0, 0, PAD + offset : PAD + offset + ROWS]
    psend[...] = f0 - d * lap

    for copy in loads[2:9]:
        copy.wait()
    basis = jnp.concatenate(
        [vin[...].astype(F32), vlev[...].astype(F32), jnp.zeros((8, 512), F32)], axis=0
    ).astype(BF16)
    read_high, read_low = split2(vread[...])
    read2 = jnp.concatenate([read_high, read_low], axis=0)
    up = nn(basis, vup[...])
    query, key, value = nn(basis, vqkv[0]), nn(basis, vqkv[1]), nn(basis, vqkv[2])
    both = nt(read2, vwout[...])
    out_read = both[:NV] + both[NV:]
    both = nt(read2, vdown[...])
    down_read = (both[:NV] + both[NV:]) * 0.5
    lane = iota((1, 128), 1)
    heads = (lane < HEAD, lane >= HEAD)
    key = key[:24] * (1.0 / math.sqrt(HEAD))
    zero_key = jnp.zeros((48, 128), F32)
    zero_out = jnp.zeros((32, 128), F32)
    keys = jnp.concatenate([jnp.where(h, key, 0.0) for h in heads], axis=0)
    outs = jnp.concatenate([jnp.where(h, out_read, 0.0) for h in heads], axis=0)
    right = jnp.concatenate(
        [
            jnp.concatenate([keys, zero_key], axis=1),
            jnp.concatenate([zero_out, outs], axis=1),
            jnp.zeros((48, 256), F32),
        ],
        axis=0,
    )
    attend = nt(jnp.concatenate([query, value], axis=1), right, HIGHEST)
    msg[j, 0:32, 0:512] = up.astype(BF16)
    msg[j, 0:32, 512:640] = attend.astype(BF16)
    msg[j, 32:48, 0:512] = down_read.astype(BF16)
    msg[j, 32:48, 512:640] = jnp.zeros((16, 128), BF16)
    def share_copy(owner, k, place):
        return pltpu.make_async_remote_copy(
            src_ref=msg.at[owner], dst_ref=msg.at[owner], send_sem=msg_send.at[k], recv_sem=msg_recv.at[k],
            device_id={"mp": place}, device_id_type=MESH,
        )

    to_core = share_copy(j, 0, peers[1])
    to_chip = share_copy(j, 1, peers[2])
    onward = share_copy(peers[2], 2, peers[1])

    pl.semaphore_wait(barrier, jnp.where(me == 0, 4, 5))
    send_g.start()

    @pl.when(me == elems - 1)
    def _():
        pl.semaphore_signal(west_in, inc=1, device_id=east, device_id_type=MESH)

    @pl.when(me != 0)
    def _():
        send_f.start()
        send_p.start()

    to_core.start()
    to_chip.start()

    gram = nt(basis, basis)
    gram_high = gram.astype(BF16)
    gram_mid, gram_low = split2(gram - gram_high.astype(F32))
    both = nt(read2, basis)
    own_high, own_low = split2((both[:NV] + both[NV:]) * 0.5)
    left = jnp.concatenate([gram_high, gram_mid, gram_low, own_high, own_low], axis=0)

    loads[9].wait()
    live = jnp.where(vstretch[...] >= 0, 1.0, 0.0).astype(BF16)
    cell, other = iota((CELLS + 32, 8), 0), iota((CELLS + 32, 8), 1)
    pick = jnp.where(jnp.where(cell < CELLS, cell >> 4, 0) == other, 1.0, 0.0).astype(BF16)
    cell, other = iota((CELLS + 32, 32), 0), iota((CELLS + 32, 32), 1)
    part_row = ACROSS * core + 2 * (cell & 7) + ((cell >> 3) & 1)
    whole_row = 2 * (cell & 15) + ((cell >> 4) & 1)
    mine = other == jnp.where(cell < CELLS, part_row, whole_row)
    mask[...] = nn(jnp.where(mine, nn(pick, live), 0.0).astype(BF16), jnp.ones((32, F), BF16))

    for tile in range(7):
        at = PAD + 8 * tile
        lap = cy[0, 8 * tile : 8 * tile + 8] * ext[:, :, at - 3 : at + 5]
        for offset in range(-2, 4):
            lap = lap + cy[offset + 3, 8 * tile : 8 * tile + 8] * ext[:, :, at + offset : at + offset + 8]
        f0, f1, f2 = ext[:, 0, at : at + 8], ext[:, 1, at : at + 8], ext[:, 2, at : at + 8]
        nothing = jnp.zeros((1, 8, F), F32)
        f3 = jnp.concatenate([f0[1:], nothing], axis=0)
        into = F32(3 * KM[3, 0]) * f0 + F32(3 * KM[3, 1]) * f1 + F32(3 * KM[3, 2]) * f2
        lap0 = (
            F32(6 * KM[0, 0]) * f0 + F32(3 * KM[0, 1]) * f1 + F32(3 * KM[0, 2]) * f2 + F32(3 * KM[0, 3]) * f3
            + jnp.concatenate([nothing, into[:3]], axis=0)
        )
        lap1 = (
            F32(1.2 * KM[1, 0]) * f0 + F32(1.2 * KM[1, 1]) * f1
            + F32(1.2 * KM[1, 2]) * f2 + F32(1.2 * KM[1, 3]) * f3
        )
        lap2 = (
            F32(1.2 * KM[2, 0]) * f0 + F32(1.2 * KM[2, 1]) * f1
            + F32(1.2 * KM[2, 2]) * f2 + F32(1.2 * KM[2, 3]) * f3
        )
        rows = 8 if tile < 6 else 1
        for a, (f, along) in enumerate(((f0, lap0), (f1, lap1), (f2, lap2))):
            fresh[:, a, 8 * tile : 8 * tile + rows] = (f - d * (lap[:, a] + along))[:, :rows]

    row, col = iota((16, 128), 0), iota((16, 128), 1)
    summing = jnp.where((col >> 3) == row, 1.0, 0.0).astype(BF16)
    row, col = iota((256, 16), 0), iota((256, 16), 1)
    repeat = jnp.where(((row >> 5) == (col & 7)) & (((row >> 4) & 1) == (col >> 3)), 1.0, 0.0).astype(BF16)

    def across(x, whole):
        begin, rows = (0, 16) if whole else (24 * core, 8)
        t0, t1, t2, t3 = (
            n12[pl.ds(b, 8, stride=3), :]
            if x == 12
            else fresh[x // 3, x % 3, pl.ds(begin + b, rows, stride=3), :]
            for b in range(4)
        )
        return jnp.concatenate([0.375 * t0 + 0.5 * t1 + 0.125 * t2, 0.125 * t1 + 0.5 * t2 + 0.375 * t3], axis=0)

    def prepare(number, places, slots, whole=False):
        nodes = {x: across(x, whole) for x in sorted({3 * (p // 2) + p % 2 + i for p in places for i in range(3)})}
        cells = []
        for p in places:
            x0, x1, x2 = (nodes[3 * (p // 2) + p % 2 + i] for i in range(3))
            cells.append(0.375 * x0 + 0.5 * x1 + 0.125 * x2 if p % 2 == 0 else 0.125 * x0 + 0.5 * x1 + 0.375 * x2)
        cells = jnp.concatenate(cells, axis=0).astype(BF16).astype(F32)

        count = (32 if whole else ACROSS) * len(places)
        tok, per = LEV * count, F // count
        turned = jnp.concatenate([cells] + [pltpu.roll(cells, F - NV * q, 1) for q in range(1, per)], axis=0).T
        variables = jnp.concatenate(
            [turned[NV * per * t : NV * per * t + NV] for t in range(LEV // per)], axis=1
        )
        level = iota((16, tok), 1) // count == iota((16, tok), 0)
        u = jnp.concatenate([variables, jnp.where(level, 1.0, 0.0).astype(F32)], axis=0)
        first = nn(left, u.astype(BF16))
        gram_u = first[0:KU] + first[KU : 2 * KU] + first[2 * KU : 3 * KU]
        squares = jnp.sum(gram_u * u, axis=0, keepdims=True)
        scaled = u * lax.rsqrt(squares * F32(1.0 / 512) + F32(1e-5))
        high, low = split2(scaled)
        scaled2 = jnp.concatenate([high, low], axis=0)
        return dict(
            number=number,
            places=places,
            slots=slots,
            count=count,
            per=per,
            scaled2=scaled2,
            tokens=scaled2.astype(F32).T.astype(BF16),
            turns=[lane_turn(scaled[:24], count * k) for k in range(per)],
            total=first[3 * KU : 3 * KU + NV] + first[3 * KU + NV :],
            acc=None,
            atts={},
            sums={},
            spreads={},
        )

    def open_share(half, r):
        folded = msg[half["slots"][r], 0:32, 512:640]
        half["atts"][r] = tn(jnp.concatenate([folded, folded], axis=0), half["scaled2"])

    def hidden_units(half, r):
        slot = half["slots"][r]
        folded = msg[slot, 0:32, 0:512]
        folded2 = jnp.concatenate([folded, folded], axis=0)
        reads = msg[slot, 32:48, 0:512]
        for part in range(2):
            cut = slice(256 * part, 256 * part + 256)
            x = nn(half["tokens"], folded2[:, cut])
            inner = x * (F32(math.sqrt(2 / math.pi)) + F32(math.sqrt(2 / math.pi) * 0.044715) * (x * x))
            hidden = (x + x * jnp.tanh(inner)).astype(BF16)
            term = nt(hidden, reads[:, cut])
            half["acc"] = term if half["acc"] is None else half["acc"] + term

    def scores(half, r):
        att, turns, per = half["atts"][r], half["turns"], half["per"]
        prods = []
        for h in range(2):
            for k in range(LEV):
                prod = att[24 * h : 24 * h + 24] * lane_turn(turns[k % per], F * (k // per))
                prods.append(prod[0:8] + prod[8:16] + prod[16:24])
        half["sums"][r] = nn(summing, jnp.concatenate(prods, axis=0).astype(BF16))

    def probabilities(half, r):
        expo = jnp.exp(half["sums"][r])
        prob = jnp.concatenate(
            [e / jnp.sum(e, axis=0, keepdims=True) for e in (expo[0:8], expo[8:16])], axis=0
        ).astype(BF16)
        half["spreads"][r] = nn(repeat, prob)

    def mix(half, r):
        att, spread, per = half["atts"][r], half["spreads"][r], half["per"]
        values = [lane_turn(att[48:80], half["count"] * k) for k in range(per)]
        mixed = None
        for k in range(LEV):
            term = spread[32 * k : 32 * k + 32] * lane_turn(values[k % per], F * (k // per))
            mixed = term if mixed is None else mixed + term
        half["total"] = half["total"] + mixed[0:16] + mixed[16:32]

    def shares(*pairs):
        for half, r in pairs:
            open_share(half, r)
        stages = (hidden_units, scores, probabilities, mix)
        for step in range(len(pairs) + 3):
            for i, stage in enumerate(stages):
                if 0 <= step - i < len(pairs):
                    stage(*pairs[step - i])

    def turned_back(half):
        total, acc, count, per = half["total"], half["acc"], half["count"], half["per"]
        tiles = LEV // per
        pieces = []
        for t in range(tiles):
            pieces += [total[:, F * t : F * t + F], jnp.zeros((NV * (per - 1), F), F32)]
        turned = jnp.concatenate(pieces, axis=0).T
        wide = jnp.concatenate([acc, jnp.zeros((LEV * count, F - NV), F32)], axis=1)
        for t in range(tiles):
            block = wide[F * t : F * t + F]
            turned = turned + (block if t == 0 else pltpu.roll(block, NV * per * t, 1))
        result = turned[0:count]
        for q in range(1, per):
            result = result + pltpu.roll(turned[count * q : count * q + count], NV * q, 1)
        return result

    def finish(half, skip=0):
        live = jnp.concatenate([mask[ACROSS * p : ACROSS * p + ACROSS] for p in half["places"]], axis=0)
        buffer, n = tbufs[half["number"]], half["number"]
        buffer[0] = jnp.where(live > 0.5, turned_back(half), 0.0).astype(BF16)
        rows = pl.ds(ACROSS * skip, ACROSS * (len(half["places"]) - skip))
        half["sends"] = {}
        for r in (2, 3, 1):
            copy = pltpu.make_async_remote_copy(
                src_ref=buffer.at[0, rows], dst_ref=buffer.at[r, rows], send_sem=t_send.at[n, r], recv_sem=t_recv.at[n, r],
                device_id={"mp": peers[r]}, device_id_type=MESH,
            )
            copy.start()
            half["sends"][r] = copy

    def place_rows(half, skip=()):
        buffer = tbufs[half["number"]]
        for r, owner in ((0, core), (1, 1 - core)):
            if r:
                half["sends"][1].wait_recv()
            half["sends"][r + 2].wait_recv()
            block = buffer[r].astype(F32) + buffer[r + 2].astype(F32)
            for i, p in enumerate(half["places"]):
                for c in range(2):
                    if p not in skip:
                        at = ACROSS * i + 8 * c
                        tend[pl.ds(128 * owner + 8 * c + p, 8, stride=16), :] = block[at : at + 8]

    chip = (j, peers[1])
    inner = prepare(0, (1, 2, 3, 4), chip)
    shares((inner, 0))
    to_core.wait_recv()
    shares((inner, 1))
    finish(inner)

    to_chip.wait_recv()
    onward.start()
    send_f.wait_recv()
    for a, weight in enumerate((3 * KM[0, 3], 1.2 * KM[1, 3], 1.2 * KM[2, 3])):
        fresh[3, a] = fresh[3, a] - (d * F32(weight)) * f12[...]
    send_p.wait_recv()
    n12[...] = precv[...] - gown[pl.ds(first_row, 32)]
    eastern = prepare(1, (4, 5, 6, 7), chip)
    shares((eastern, 0), (eastern, 1))
    finish(eastern, skip=1)
    place_rows(inner)

    onward.wait_recv()

    @pl.when(me == 0)
    def _():
        pl.semaphore_wait(west_in, 1)
        send_f.start()
        send_p.start()

    send_g.wait_recv()
    fresh[0, 0] = fresh[0, 0] - grecv[...].astype(F32)[0:Y]
    western = prepare(2, (0,), (0, 1, 2, 3), whole=True)
    western["total"] = western["total"] * 2.0
    shares((western, 0), (western, 1), (western, 2), (western, 3))
    result = jnp.where(mask[CELLS : CELLS + 32] > 0.5, turned_back(western), 0.0)
    for c in range(2):
        tend[pl.ds(8 * c, 16, stride=16), :] = result[16 * c : 16 * c + 16]
    place_rows(eastern, skip=(4,))

    sent = [send_f, send_p, send_g, to_core, to_chip, onward, *inner["sends"].values(), *eastern["sends"].values()]
    for copy in sent:
        copy.wait_send()


def local(elems, state_field, diffusion, stretch, w_in, lemb, w_qkv, w_out, w_up, w_down, w_read):
    state = jnp.transpose(state_field, (1, 0, 2)).reshape(4, 3, Y, F)
    operands = (
        state, diffusion.reshape(1, F), jnp.transpose(stretch), w_in, lemb,
        w_qkv, w_out, w_up, w_down, jnp.transpose(w_read),
    )
    vm = pltpu.VMEM
    dma = pltpu.SemaphoreType.DMA
    new, tend = pl.pallas_call(
        lambda *refs: kernel(elems, *refs),
        out_shape=(
            jax.ShapeDtypeStruct((4, 3, Y, F), F32),
            jax.ShapeDtypeStruct((256, F), F32),
        ),
        in_specs=[pl.BlockSpec(memory_space=pltpu.HBM)] * 10,
        out_specs=[pl.BlockSpec(memory_space=pltpu.VMEM)] * 2,
        scratch_shapes=[
            vm((4, 3, Y, F), F32),
            vm((4, 3, PAD + 64, F), F32),
            vm((7, ROWS, F), F32),
            vm((32, F), F32),
            vm((ROWS, F), F32),
            vm((Y, F), F32),
            vm((64, F), BF16),
            vm((64, F), BF16),
            vm((ROWS, F), F32),
            vm((32, F), F32),
            vm((1, F), F32),
            vm((8, 32), jnp.int32),
            vm((16, 512), BF16),
            vm((8, 512), BF16),
            vm((3, 512, 128), BF16),
            vm((128, 512), BF16),
            vm((512, 512), BF16),
            vm((512, 512), BF16),
            vm((16, 512), F32),
            vm((4, 48, 640), BF16),
            vm((CELLS + 32, F), F32),
            vm((4, 4 * ACROSS, F), BF16),
            vm((4, 4 * ACROSS, F), BF16),
            dma((10,)),
            dma((4,)),
            dma((3,)),
            dma((3,)),
            dma((3,)),
            dma((2, 4)),
            dma((2, 4)),
            pltpu.SemaphoreType.REGULAR,
        ],
        compiler_params=pltpu.CompilerParams(
            collective_id=0, has_side_effects=True, vmem_limit_bytes=40 * 1024 * 1024
        ),
        name="step",
    )(*(pltpu.with_memory_space_constraint(x, pltpu.HBM) for x in operands))
    return jnp.transpose(new.reshape(12, Y, F), (1, 0, 2)), tend.reshape(32, 8, F)


def solution(mesh):
    elems = mesh.shape["elem"]
    in_specs = (
        P(None, "elem", None),
        P(),
        P(None, "elem"),
        P(),
        P(),
        P(None, None, "mp"),
        P("mp", None),
        P(None, "mp"),
        P("mp", None),
        P(),
    )
    out_specs = (P(None, "elem", None), P(None, "elem", None))
    return jax.shard_map(
        lambda *args: local(elems, *args), mesh=mesh, in_specs=in_specs, out_specs=out_specs, check_vma=False
    )
```

```python
import math

import jax
import jax.numpy as jnp
import numpy as np
from jax import lax
from jax.experimental import pallas as pl
from jax.experimental.pallas import tpu as pltpu
from jax.sharding import PartitionSpec as P

MESH = pl.DeviceIdType.MESH
F32 = jnp.float32
BF16 = jnp.bfloat16
HIGHEST = lax.Precision.HIGHEST

LEV = 8
NV = 16
F = 128
HEAD = 64
Y = 49
ROWS = 56
PAD = 8
ACROSS = 16
CELLS = 8 * ACROSS
KU = 32


def stiffness_1d():
    points = np.array([-1.0, -1.0 / math.sqrt(5.0), 1.0 / math.sqrt(5.0), 1.0])
    weight = np.array([1.0, 5.0, 5.0, 1.0]) / 6.0
    basis = [np.prod([points[i] - points[o] for o in range(4) if o != i]) for i in range(4)]
    dmat = np.zeros((4, 4))
    for i in range(4):
        for k in range(4):
            if i == k:
                dmat[i, k] = sum(1.0 / (points[i] - points[o]) for o in range(4) if o != i)
            else:
                dmat[i, k] = basis[i] / basis[k] / (points[i] - points[k])
    return dmat.T @ (weight[:, None] * dmat)


KM = stiffness_1d()


def nt(a, b, precision=None):
    return lax.dot_general(a, b, (((1,), (1,)), ((), ())), precision=precision, preferred_element_type=F32)


def tn(a, b):
    return lax.dot_general(a, b, (((0,), (0,)), ((), ())), preferred_element_type=F32)


def nn(a, b):
    return jnp.dot(a, b, preferred_element_type=F32)


def iota(shape, dim):
    return lax.broadcasted_iota(jnp.int32, shape, dim)


def split2(x):
    high = x.astype(BF16)
    return high, (x - high.astype(F32)).astype(BF16)


def lane_turn(x, by):
    return x if by == 0 else jnp.concatenate([x[:, by:], x[:, :by]], axis=1)


def band_along_y(offset):
    y = iota((ROWS, F), 0)
    kind = y - 3 * ((y * 171) >> 9)
    out = jnp.zeros((ROWS, F), F32)
    if 0 <= offset + 1 < 4:
        out = jnp.where(kind == 1, F32(1.2 * KM[1, offset + 1]), out)
    if 0 <= offset + 2 < 4:
        out = jnp.where(kind == 2, F32(1.2 * KM[2, offset + 2]), out)
    corner = jnp.zeros((ROWS, F), F32)
    if offset >= 0:
        corner = corner + jnp.where(y < Y - 1, F32(KM[0, offset]), F32(0))
    if offset <= 0:
        corner = corner + jnp.where(y > 0, F32(KM[3, offset + 3]), F32(0))
    corner = corner * jnp.where((y == 0) | (y == Y - 1), F32(6), F32(3))
    out = jnp.where(kind == 0, corner, out)
    return jnp.where(y < Y, out, F32(0))


def kernel(
    elems, state, diff, stretch, w_in, lemb, w_qkv, w_out, w_up, w_down, w_read,
    fresh, tend,
    st, ext, cy, n12, gown, f12, gsend, grecv, psend, precv,
    vdiff, vstretch, vin, vlev, vqkv, vwout, vup, vdown, vread,
    msg, mask, tbuf0, tbuf1,
    load_sem, halo_send, halo_recv, msg_send, msg_recv, t_send, t_recv, west_in, all_in,
):
    me = lax.axis_index("elem")
    j = lax.axis_index("mp")
    tbufs = (tbuf0, tbuf1)
    peers = (None, j + 1 - 2 * lax.rem(j, 2), lax.rem(j + 2, 4), 3 - j)

    core = lax.rem(j, 2)
    east = {"elem": lax.rem(me + 1, elems), "mp": peers[2]}
    east_other = {"elem": lax.rem(me + 1, elems), "mp": peers[3]}
    west = {"elem": lax.rem(me + elems - 1, elems), "mp": peers[2]}
    west_first = {"elem": lax.rem(me + elems - 1, elems), "mp": peers[2] - core}
    east_second = {"elem": lax.rem(me + 1, elems), "mp": peers[2] - core + 1}

    loads = [
        pltpu.make_async_copy(src, dst, load_sem.at[i])
        for i, (src, dst) in enumerate(
            [
                (state.at[3], st.at[3]), (diff, vdiff), (state.at[0:3], st.at[0:3]), (w_in, vin), (lemb, vlev), (w_read, vread),
                (w_qkv, vqkv), (w_up, vup), (w_out, vwout), (w_down, vdown), (stretch, vstretch),
            ]
        )
    ]
    loads[0].start()
    loads[1].start()

    barrier = pltpu.get_barrier_semaphore()
    pl.semaphore_signal(barrier, inc=1, device_id=west_first, device_id_type=MESH)
    pl.semaphore_signal(barrier, inc=1, device_id={"mp": peers[2] - core + 1}, device_id_type=MESH)

    pl.semaphore_signal(barrier, inc=1, device_id={"mp": peers[1]}, device_id_type=MESH)

    @pl.when(me != elems - 1)
    def _():
        pl.semaphore_signal(barrier, inc=1, device_id=east_second, device_id_type=MESH)

    def far(src, dst, k, place, s=None):
        return pltpu.make_async_remote_copy(
            src_ref=src, dst_ref=dst, send_sem=halo_send.at[k if s is None else s], recv_sem=halo_recv.at[k],
            device_id=place, device_id_type=MESH,
        )

    first_row = pl.multiple_of(24 * core, 8)
    send_f = far(state.at[0, 0], f12, 0, west)
    send_p = far(psend.at[pl.ds(first_row, 32)], precv, 1, west)
    send_g = far(gsend, grecv, 2, east)
    send_g_other = far(gsend, grecv, 2, east_other, 3)

    for copy in loads[2:]:
        copy.start()
    loads[0].wait()
    loads[1].wait()
    d = vdiff[...]
    share = d * (3.0 * (F32(KM[3, 0]) * st[3, 0] + F32(KM[3, 1]) * st[3, 1] + F32(KM[3, 2]) * st[3, 2]))
    gown[0:Y] = share
    gsend[...] = jnp.concatenate([share, jnp.zeros((64 - Y, F), F32)], axis=0).astype(BF16)

    @pl.when(core == 0)
    def _():
        pl.semaphore_wait(barrier, 3)

        @pl.when(me == elems - 1)
        def _():
            pl.semaphore_signal(west_in, inc=1, device_id=east, device_id_type=MESH)
            pl.semaphore_signal(west_in, inc=1, device_id=east_other, device_id_type=MESH)

        send_g.start()
        send_g_other.start()

    for offset in range(-3, 4):
        cy[offset + 3] = band_along_y(offset)
    ext[:, :, 0:PAD, :] = jnp.zeros((4, 3, PAD, F), F32)
    ext[:, :, PAD + 48 : PAD + 64, :] = jnp.zeros((4, 3, 16, F), F32)

    loads[2].wait()
    ext[:, :, PAD : PAD + Y, :] = st[...]
    body = slice(PAD, PAD + ROWS)
    f0, f1, f2, f3 = ext[0, 0, body], ext[0, 1, body], ext[0, 2, body], ext[1, 0, body]
    lap = 3.0 * (F32(2 * KM[0, 0]) * f0 + F32(KM[0, 1]) * f1 + F32(KM[0, 2]) * f2 + F32(KM[0, 3]) * f3)
    for offset in range(-3, 4):
        lap = lap + cy[offset + 3] * ext[0, 0, PAD + offset : PAD + offset + ROWS]
    psend[...] = f0 - d * lap

    for copy in loads[3:10]:
        copy.wait()
    basis = jnp.concatenate(
        [vin[...].astype(F32), vlev[...].astype(F32), jnp.zeros((8, 512), F32)], axis=0
    ).astype(BF16)
    read_high, read_low = split2(vread[...])
    read2 = jnp.concatenate([read_high, read_low], axis=0)
    up = nn(basis, vup[...])
    query, key, value = nn(basis, vqkv[0]), nn(basis, vqkv[1]), nn(basis, vqkv[2])
    both = nt(read2, vwout[...])
    out_read = both[:NV] + both[NV:]
    both = nt(read2, vdown[...])
    down_read = (both[:NV] + both[NV:]) * 0.5
    lane = iota((1, 128), 1)
    heads = (lane < HEAD, lane >= HEAD)
    key = key[:24] * (1.0 / math.sqrt(HEAD))
    zero_key = jnp.zeros((48, 128), F32)
    zero_out = jnp.zeros((32, 128), F32)
    keys = jnp.concatenate([jnp.where(h, key, 0.0) for h in heads], axis=0)
    outs = jnp.concatenate([jnp.where(h, out_read, 0.0) for h in heads], axis=0)
    right = jnp.concatenate(
        [
            jnp.concatenate([keys, zero_key], axis=1),
            jnp.concatenate([zero_out, outs], axis=1),
            jnp.zeros((48, 256), F32),
        ],
        axis=0,
    )
    attend = nt(jnp.concatenate([query, value], axis=1), right, HIGHEST)
    msg[j, 0:32, 0:512] = up.astype(BF16)
    msg[j, 0:32, 512:640] = attend.astype(BF16)
    msg[j, 32:48, 0:512] = down_read.astype(BF16)
    msg[j, 32:48, 512:640] = jnp.zeros((16, 128), BF16)
    def share_copy(owner, k, place):
        return pltpu.make_async_remote_copy(
            src_ref=msg.at[owner], dst_ref=msg.at[owner], send_sem=msg_send.at[k], recv_sem=msg_recv.at[k],
            device_id={"mp": place}, device_id_type=MESH,
        )

    to_core = share_copy(j, 0, peers[1])
    to_chip = share_copy(j, 1, peers[2])
    onward = share_copy(peers[2], 2, peers[1])

    @pl.when(core == 1)
    def _():
        pl.semaphore_wait(barrier, jnp.where(me == 0, 3, 5))
        pl.semaphore_signal(all_in, inc=1, device_id={"mp": peers[1]}, device_id_type=MESH)

    @pl.when(core == 0)
    def _():
        pl.semaphore_wait(all_in, 1)


    @pl.when(me != 0)
    def _():
        send_f.start()
        send_p.start()

    to_core.start()
    to_chip.start()

    gram = nt(basis, basis)
    gram_high = gram.astype(BF16)
    gram_mid, gram_low = split2(gram - gram_high.astype(F32))
    both = nt(read2, basis)
    own_high, own_low = split2((both[:NV] + both[NV:]) * 0.5)
    left = jnp.concatenate([gram_high, gram_mid, gram_low, own_high, own_low], axis=0)

    loads[10].wait()
    live = jnp.where(vstretch[...] >= 0, 1.0, 0.0).astype(BF16)
    cell, other = iota((CELLS + 32, 8), 0), iota((CELLS + 32, 8), 1)
    pick = jnp.where(jnp.where(cell < CELLS, cell >> 4, 0) == other, 1.0, 0.0).astype(BF16)
    cell, other = iota((CELLS + 32, 32), 0), iota((CELLS + 32, 32), 1)
    part_row = ACROSS * core + 2 * (cell & 7) + ((cell >> 3) & 1)
    whole_row = 2 * (cell & 15) + ((cell >> 4) & 1)
    mine = other == jnp.where(cell < CELLS, part_row, whole_row)
    mask[...] = nn(jnp.where(mine, nn(pick, live), 0.0).astype(BF16), jnp.ones((32, F), BF16))

    for tile in range(7):
        at = PAD + 8 * tile
        lap = cy[0, 8 * tile : 8 * tile + 8] * ext[:, :, at - 3 : at + 5]
        for offset in range(-2, 4):
            lap = lap + cy[offset + 3, 8 * tile : 8 * tile + 8] * ext[:, :, at + offset : at + offset + 8]
        f0, f1, f2 = ext[:, 0, at : at + 8], ext[:, 1, at : at + 8], ext[:, 2, at : at + 8]
        nothing = jnp.zeros((1, 8, F), F32)
        f3 = jnp.concatenate([f0[1:], nothing], axis=0)
        into = F32(3 * KM[3, 0]) * f0 + F32(3 * KM[3, 1]) * f1 + F32(3 * KM[3, 2]) * f2
        lap0 = (
            F32(6 * KM[0, 0]) * f0 + F32(3 * KM[0, 1]) * f1 + F32(3 * KM[0, 2]) * f2 + F32(3 * KM[0, 3]) * f3
            + jnp.concatenate([nothing, into[:3]], axis=0)
        )
        lap1 = (
            F32(1.2 * KM[1, 0]) * f0 + F32(1.2 * KM[1, 1]) * f1
            + F32(1.2 * KM[1, 2]) * f2 + F32(1.2 * KM[1, 3]) * f3
        )
        lap2 = (
            F32(1.2 * KM[2, 0]) * f0 + F32(1.2 * KM[2, 1]) * f1
            + F32(1.2 * KM[2, 2]) * f2 + F32(1.2 * KM[2, 3]) * f3
        )
        rows = 8 if tile < 6 else 1
        for a, (f, along) in enumerate(((f0, lap0), (f1, lap1), (f2, lap2))):
            fresh[:, a, 8 * tile : 8 * tile + rows] = (f - d * (lap[:, a] + along))[:, :rows]

    row, col = iota((16, 128), 0), iota((16, 128), 1)
    summing = jnp.where((col >> 3) == row, 1.0, 0.0).astype(BF16)
    row, col = iota((256, 16), 0), iota((256, 16), 1)
    repeat = jnp.where(((row >> 5) == (col & 7)) & (((row >> 4) & 1) == (col >> 3)), 1.0, 0.0).astype(BF16)

    def across(x, whole):
        begin, rows = (0, 16) if whole else (24 * core, 8)
        t0, t1, t2, t3 = (
            n12[pl.ds(b, 8, stride=3), :]
            if x == 12
            else fresh[x // 3, x % 3, pl.ds(begin + b, rows, stride=3), :]
            for b in range(4)
        )
        return jnp.concatenate([0.375 * t0 + 0.5 * t1 + 0.125 * t2, 0.125 * t1 + 0.5 * t2 + 0.375 * t3], axis=0)

    def prepare(number, places, slots, whole=False, known={}):
        nodes = {x: known[x] if x in known else across(x, whole) for x in sorted({3 * (p // 2) + p % 2 + i for p in places for i in range(3)})}
        cells = []
        for p in places:
            x0, x1, x2 = (nodes[3 * (p // 2) + p % 2 + i] for i in range(3))
            cells.append(0.375 * x0 + 0.5 * x1 + 0.125 * x2 if p % 2 == 0 else 0.125 * x0 + 0.5 * x1 + 0.375 * x2)
        cells = jnp.concatenate(cells, axis=0).astype(BF16).astype(F32)

        count = (32 if whole else ACROSS) * len(places)
        tok, per = LEV * count, F // count
        turned = jnp.concatenate([cells] + [pltpu.roll(cells, F - NV * q, 1) for q in range(1, per)], axis=0).T
        variables = jnp.concatenate(
            [turned[NV * per * t : NV * per * t + NV] for t in range(LEV // per)], axis=1
        )
        level = iota((16, tok), 1) // count == iota((16, tok), 0)
        u = jnp.concatenate([variables, jnp.where(level, 1.0, 0.0).astype(F32)], axis=0)
        first = nn(left, u.astype(BF16))
        gram_u = first[0:KU] + first[KU : 2 * KU] + first[2 * KU : 3 * KU]
        squares = jnp.sum(gram_u * u, axis=0, keepdims=True)
        scaled = u * lax.rsqrt(squares * F32(1.0 / 512) + F32(1e-5))
        high, low = split2(scaled)
        scaled2 = jnp.concatenate([high, low], axis=0)
        return dict(
            number=number,
            places=places,
            slots=slots,
            count=count,
            per=per,
            scaled2=scaled2,
            tokens=scaled2.astype(F32).T.astype(BF16),
            turns=[lane_turn(scaled[:24], count * k) for k in range(per)],
            total=first[3 * KU : 3 * KU + NV] + first[3 * KU + NV :],
            acc=None,
            atts={},
            sums={},
            spreads={},
        )

    def open_share(half, r):
        folded = msg[half["slots"][r], 0:32, 512:640]
        half["atts"][r] = tn(jnp.concatenate([folded, folded], axis=0), half["scaled2"])

    def hidden_units(half, r):
        slot = half["slots"][r]
        folded = msg[slot, 0:32, 0:512]
        folded2 = jnp.concatenate([folded, folded], axis=0)
        reads = msg[slot, 32:48, 0:512]
        for part in range(2):
            cut = slice(256 * part, 256 * part + 256)
            x = nn(half["tokens"], folded2[:, cut])
            inner = x * (F32(math.sqrt(2 / math.pi)) + F32(math.sqrt(2 / math.pi) * 0.044715) * (x * x))
            hidden = (x + x * jnp.tanh(inner)).astype(BF16)
            term = nt(hidden, reads[:, cut])
            half["acc"] = term if half["acc"] is None else half["acc"] + term

    def scores(half, r):
        att, turns, per = half["atts"][r], half["turns"], half["per"]
        prods = []
        for h in range(2):
            for k in range(LEV):
                prod = att[24 * h : 24 * h + 24] * lane_turn(turns[k % per], F * (k // per))
                prods.append(prod[0:8] + prod[8:16] + prod[16:24])
        half["sums"][r] = nn(summing, jnp.concatenate(prods, axis=0).astype(BF16))

    def probabilities(half, r):
        expo = jnp.exp(half["sums"][r])
        prob = jnp.concatenate(
            [e / jnp.sum(e, axis=0, keepdims=True) for e in (expo[0:8], expo[8:16])], axis=0
        ).astype(BF16)
        half["spreads"][r] = nn(repeat, prob)

    def mix(half, r):
        att, spread, per = half["atts"][r], half["spreads"][r], half["per"]
        values = [lane_turn(att[48:80], half["count"] * k) for k in range(per)]
        mixed = None
        for k in range(LEV):
            term = spread[32 * k : 32 * k + 32] * lane_turn(values[k % per], F * (k // per))
            mixed = term if mixed is None else mixed + term
        half["total"] = half["total"] + mixed[0:16] + mixed[16:32]

    def shares(*pairs):
        for pair in pairs:
            open_share(*pair)
        stages = (scores, probabilities, mix)
        for i, pair in enumerate(pairs):
            hidden_units(*pair)
            for stage in stages[i : i + 1] if i < len(pairs) - 1 else stages[i:]:
                for other in pairs:
                    stage(*other)

    def turned_back(half):
        total, acc, count, per = half["total"], half["acc"], half["count"], half["per"]
        tiles = LEV // per
        pieces = []
        for t in range(tiles):
            pieces += [total[:, F * t : F * t + F], jnp.zeros((NV * (per - 1), F), F32)]
        turned = jnp.concatenate(pieces, axis=0).T
        wide = jnp.concatenate([acc, jnp.zeros((LEV * count, F - NV), F32)], axis=1)
        for t in range(tiles):
            block = wide[F * t : F * t + F]
            turned = turned + (block if t == 0 else pltpu.roll(block, NV * per * t, 1))
        result = turned[0:count]
        for q in range(1, per):
            result = result + pltpu.roll(turned[count * q : count * q + count], NV * q, 1)
        return result

    def finish(half, skip=0):
        live = jnp.concatenate([mask[ACROSS * p : ACROSS * p + ACROSS] for p in half["places"]], axis=0)
        buffer, n = tbufs[half["number"]], half["number"]
        buffer[0] = jnp.where(live > 0.5, turned_back(half), 0.0).astype(BF16)
        rows = pl.ds(ACROSS * skip, ACROSS * (len(half["places"]) - skip))
        half["sends"] = {}
        for r in (2, 3, 1):
            copy = pltpu.make_async_remote_copy(
                src_ref=buffer.at[0, rows], dst_ref=buffer.at[r, rows], send_sem=t_send.at[n, r], recv_sem=t_recv.at[n, r],
                device_id={"mp": peers[r]}, device_id_type=MESH,
            )
            copy.start()
            half["sends"][r] = copy

    def place_rows(half, skip=()):
        buffer = tbufs[half["number"]]
        for r, owner in ((0, core), (1, 1 - core)):
            if r:
                half["sends"][1].wait_recv()
            half["sends"][r + 2].wait_recv()
            block = buffer[r].astype(F32) + buffer[r + 2].astype(F32)
            for i, p in enumerate(half["places"]):
                for c in range(2):
                    if p not in skip:
                        at = ACROSS * i + 8 * c
                        tend[pl.ds(128 * owner + 8 * c + p, 8, stride=16), :] = block[at : at + 8]

    chip = (j, peers[1])
    inner = prepare(0, (1, 2, 3, 4), chip)
    shares((inner, 0))
    to_core.wait_recv()
    shares((inner, 1))
    finish(inner)

    to_chip.wait_recv()
    onward.start()
    send_f.wait_recv()
    for a, weight in enumerate((3 * KM[0, 3], 1.2 * KM[1, 3], 1.2 * KM[2, 3])):
        fresh[3, a] = fresh[3, a] - (d * F32(weight)) * f12[...]
    send_p.wait_recv()
    n12[...] = precv[...] - gown[pl.ds(first_row, 32)]
    eastern = prepare(1, (4, 5, 6, 7), chip)
    shares((eastern, 0), (eastern, 1))
    finish(eastern, skip=1)
    place_rows(inner)

    @pl.when(me == 0)
    def _():
        place_rows(eastern, skip=(4,))

    onward.wait_recv()

    @pl.when(me == 0)
    def _():
        pl.semaphore_wait(west_in, 1)
        send_f.start()
        send_p.start()

    known = {x: across(x, True) for x in (1, 2)}
    send_g.wait_recv()
    fresh[0, 0] = fresh[0, 0] - grecv[...].astype(F32)[0:Y]
    western = prepare(2, (0,), (0, 1, 2, 3), whole=True, known=known)
    western["total"] = western["total"] * 2.0
    shares((western, 0), (western, 1), (western, 2), (western, 3))
    result = jnp.where(mask[CELLS : CELLS + 32] > 0.5, turned_back(western), 0.0)
    for c in range(2):
        tend[pl.ds(8 * c, 16, stride=16), :] = result[16 * c : 16 * c + 16]

    @pl.when(me != 0)
    def _():
        place_rows(eastern, skip=(4,))

    sent = [send_f, send_p, to_core, to_chip, onward, *inner["sends"].values(), *eastern["sends"].values()]
    for copy in sent:
        copy.wait_send()

    @pl.when(core == 0)
    def _():
        send_g.wait_send()
        send_g_other.wait_send()


def store(new, tend, new_out, tend_out, sem):
    first = pltpu.make_async_copy(new, new_out, sem.at[0])
    second = pltpu.make_async_copy(tend, tend_out, sem.at[1])
    first.start()
    second.start()
    first.wait()
    second.wait()


def local(elems, state_field, diffusion, stretch, w_in, lemb, w_qkv, w_out, w_up, w_down, w_read):
    state = jnp.transpose(state_field, (1, 0, 2)).reshape(4, 3, Y, F)
    operands = (
        state, diffusion.reshape(1, F), jnp.transpose(stretch), w_in, lemb,
        w_qkv, w_out, w_up, w_down, jnp.transpose(w_read),
    )
    vm = pltpu.VMEM
    dma = pltpu.SemaphoreType.DMA
    new, tend = pl.pallas_call(
        lambda *refs: kernel(elems, *refs),
        out_shape=(
            jax.ShapeDtypeStruct((4, 3, Y, F), F32),
            jax.ShapeDtypeStruct((256, F), F32),
        ),
        in_specs=[pl.BlockSpec(memory_space=pltpu.HBM)] * 10,
        out_specs=[pl.BlockSpec(memory_space=pltpu.VMEM)] * 2,
        scratch_shapes=[
            vm((4, 3, Y, F), F32),
            vm((4, 3, PAD + 64, F), F32),
            vm((7, ROWS, F), F32),
            vm((32, F), F32),
            vm((ROWS, F), F32),
            vm((Y, F), F32),
            vm((64, F), BF16),
            vm((64, F), BF16),
            vm((ROWS, F), F32),
            vm((32, F), F32),
            vm((1, F), F32),
            vm((8, 32), jnp.int32),
            vm((16, 512), BF16),
            vm((8, 512), BF16),
            vm((3, 512, 128), BF16),
            vm((128, 512), BF16),
            vm((512, 512), BF16),
            vm((512, 512), BF16),
            vm((16, 512), F32),
            vm((4, 48, 640), BF16),
            vm((CELLS + 32, F), F32),
            vm((4, 4 * ACROSS, F), BF16),
            vm((4, 4 * ACROSS, F), BF16),
            dma((11,)),
            dma((4,)),
            dma((3,)),
            dma((3,)),
            dma((3,)),
            dma((2, 4)),
            dma((2, 4)),
            pltpu.SemaphoreType.REGULAR,
            pltpu.SemaphoreType.REGULAR,
        ],
        compiler_params=pltpu.CompilerParams(
            collective_id=0, has_side_effects=True, vmem_limit_bytes=40 * 1024 * 1024
        ),
        name="step",
    )(*(pltpu.with_memory_space_constraint(x, pltpu.HBM) for x in operands))
    new, tend = (pltpu.with_memory_space_constraint(x, pltpu.VMEM) for x in (new, tend))
    new, tend = pl.pallas_call(
        store,
        out_shape=(jax.ShapeDtypeStruct(new.shape, F32), jax.ShapeDtypeStruct(tend.shape, F32)),
        in_specs=[pl.BlockSpec(memory_space=pltpu.VMEM)] * 2,
        out_specs=[pl.BlockSpec(memory_space=pltpu.HBM)] * 2,
        scratch_shapes=[dma((2,))],
        name="store",
    )(new, tend)
    return jnp.transpose(new.reshape(12, Y, F), (1, 0, 2)), tend.reshape(32, 8, F)


def solution(mesh):
    elems = mesh.shape["elem"]
    in_specs = (
        P(None, "elem", None),
        P(),
        P(None, "elem"),
        P(),
        P(),
        P(None, None, "mp"),
        P("mp", None),
        P(None, "mp"),
        P("mp", None),
        P(),
    )
    out_specs = (P(None, "elem", None), P(None, "elem", None))
    return jax.shard_map(
        lambda *args: local(elems, *args), mesh=mesh, in_specs=in_specs, out_specs=out_specs, check_vma=False
    )
```

```python
import math

import jax
import jax.numpy as jnp
import numpy as np
from jax import lax
from jax.experimental import pallas as pl
from jax.experimental.pallas import tpu as pltpu
from jax.sharding import PartitionSpec as P

MESH = pl.DeviceIdType.MESH
F32 = jnp.float32
BF16 = jnp.bfloat16
HIGHEST = lax.Precision.HIGHEST

LEV = 8
NV = 16
F = 128
HEAD = 64
Y = 49
ROWS = 56
PAD = 8
ACROSS = 16
CELLS = 8 * ACROSS
KU = 32


def stiffness_1d():
    points = np.array([-1.0, -1.0 / math.sqrt(5.0), 1.0 / math.sqrt(5.0), 1.0])
    weight = np.array([1.0, 5.0, 5.0, 1.0]) / 6.0
    basis = [np.prod([points[i] - points[o] for o in range(4) if o != i]) for i in range(4)]
    dmat = np.zeros((4, 4))
    for i in range(4):
        for k in range(4):
            if i == k:
                dmat[i, k] = sum(1.0 / (points[i] - points[o]) for o in range(4) if o != i)
            else:
                dmat[i, k] = basis[i] / basis[k] / (points[i] - points[k])
    return dmat.T @ (weight[:, None] * dmat)


KM = stiffness_1d()


def nt(a, b, precision=None):
    return lax.dot_general(a, b, (((1,), (1,)), ((), ())), precision=precision, preferred_element_type=F32)


def tn(a, b):
    return lax.dot_general(a, b, (((0,), (0,)), ((), ())), preferred_element_type=F32)


def nn(a, b):
    return jnp.dot(a, b, preferred_element_type=F32)


def iota(shape, dim):
    return lax.broadcasted_iota(jnp.int32, shape, dim)


def split2(x):
    high = x.astype(BF16)
    return high, (x - high.astype(F32)).astype(BF16)


def lane_turn(x, by):
    return x if by == 0 else jnp.concatenate([x[:, by:], x[:, :by]], axis=1)


def band_along_y(offset):
    y = iota((ROWS, F), 0)
    kind = y - 3 * ((y * 171) >> 9)
    out = jnp.zeros((ROWS, F), F32)
    if 0 <= offset + 1 < 4:
        out = jnp.where(kind == 1, F32(1.2 * KM[1, offset + 1]), out)
    if 0 <= offset + 2 < 4:
        out = jnp.where(kind == 2, F32(1.2 * KM[2, offset + 2]), out)
    corner = jnp.zeros((ROWS, F), F32)
    if offset >= 0:
        corner = corner + jnp.where(y < Y - 1, F32(KM[0, offset]), F32(0))
    if offset <= 0:
        corner = corner + jnp.where(y > 0, F32(KM[3, offset + 3]), F32(0))
    corner = corner * jnp.where((y == 0) | (y == Y - 1), F32(6), F32(3))
    out = jnp.where(kind == 0, corner, out)
    return jnp.where(y < Y, out, F32(0))


def kernel(
    elems, state, diff, stretch, w_in, lemb, w_qkv, w_out, w_up, w_down, w_read,
    fresh, tend,
    st, ext, cy, n12, gown, f12, gsend, grecv, psend, precv,
    vdiff, vstretch, vin, vlev, vqkv, vwout, vup, vdown, vread,
    msg, mask, tbuf0, tbuf1,
    load_sem, halo_send, halo_recv, msg_send, msg_recv, t_send, t_recv, west_in, all_in,
):
    me = lax.axis_index("elem")
    j = lax.axis_index("mp")
    tbufs = (tbuf0, tbuf1)
    peers = (None, j + 1 - 2 * lax.rem(j, 2), lax.rem(j + 2, 4), 3 - j)

    core = lax.rem(j, 2)
    east = {"elem": lax.rem(me + 1, elems), "mp": peers[2]}
    east_other = {"elem": lax.rem(me + 1, elems), "mp": peers[3]}
    west = {"elem": lax.rem(me + elems - 1, elems), "mp": peers[2]}
    west_first = {"elem": lax.rem(me + elems - 1, elems), "mp": peers[2] - core}
    east_second = {"elem": lax.rem(me + 1, elems), "mp": peers[2] - core + 1}

    loads = [
        pltpu.make_async_copy(src, dst, load_sem.at[i])
        for i, (src, dst) in enumerate(
            [
                (state.at[3], st.at[3]), (diff, vdiff), (state.at[0:3], st.at[0:3]), (w_in, vin), (lemb, vlev), (w_read, vread),
                (w_qkv, vqkv), (w_up, vup), (w_out, vwout), (w_down, vdown), (stretch, vstretch),
            ]
        )
    ]
    loads[0].start()
    loads[1].start()

    barrier = pltpu.get_barrier_semaphore()
    pl.semaphore_signal(barrier, inc=1, device_id=west_first, device_id_type=MESH)
    pl.semaphore_signal(barrier, inc=1, device_id={"mp": peers[2] - core + 1}, device_id_type=MESH)

    pl.semaphore_signal(barrier, inc=1, device_id={"mp": peers[1]}, device_id_type=MESH)

    @pl.when(me != elems - 1)
    def _():
        pl.semaphore_signal(barrier, inc=1, device_id=east_second, device_id_type=MESH)

    def far(src, dst, k, place, s=None):
        return pltpu.make_async_remote_copy(
            src_ref=src, dst_ref=dst, send_sem=halo_send.at[k if s is None else s], recv_sem=halo_recv.at[k],
            device_id=place, device_id_type=MESH,
        )

    first_row = pl.multiple_of(24 * core, 8)
    send_f = far(state.at[0, 0], f12, 0, west)
    send_p = far(psend.at[pl.ds(first_row, 32)], precv, 1, west)
    send_g = far(gsend, grecv, 2, east)
    send_g_other = far(gsend, grecv, 2, east_other, 3)

    for copy in loads[2:]:
        copy.start()

    @pl.when(core == 0)
    def _():
        pl.semaphore_wait(barrier, 3)

        @pl.when(me == elems - 1)
        def _():
            pl.semaphore_signal(west_in, inc=1, device_id=east_other, device_id_type=MESH)
            pl.semaphore_signal(west_in, inc=1, device_id=east, device_id_type=MESH)

    loads[0].wait()
    loads[1].wait()
    d = vdiff[...]
    share = d * (3.0 * (F32(KM[3, 0]) * st[3, 0] + F32(KM[3, 1]) * st[3, 1] + F32(KM[3, 2]) * st[3, 2]))
    gown[0:Y] = share
    gsend[...] = jnp.concatenate([share, jnp.zeros((64 - Y, F), F32)], axis=0).astype(BF16)

    @pl.when(core == 0)
    def _():
        send_g_other.start()
        send_g.start()

    for offset in range(-3, 4):
        cy[offset + 3] = band_along_y(offset)
    ext[:, :, 0:PAD, :] = jnp.zeros((4, 3, PAD, F), F32)
    ext[:, :, PAD + 48 : PAD + 64, :] = jnp.zeros((4, 3, 16, F), F32)

    loads[2].wait()
    ext[:, :, PAD : PAD + Y, :] = st[...]
    body = slice(PAD, PAD + ROWS)
    f0, f1, f2, f3 = ext[0, 0, body], ext[0, 1, body], ext[0, 2, body], ext[1, 0, body]
    lap = 3.0 * (F32(2 * KM[0, 0]) * f0 + F32(KM[0, 1]) * f1 + F32(KM[0, 2]) * f2 + F32(KM[0, 3]) * f3)
    for offset in range(-3, 4):
        lap = lap + cy[offset + 3] * ext[0, 0, PAD + offset : PAD + offset + ROWS]
    psend[...] = f0 - d * lap

    for copy in loads[3:10]:
        copy.wait()
    basis = jnp.concatenate(
        [vin[...].astype(F32), vlev[...].astype(F32), jnp.zeros((8, 512), F32)], axis=0
    ).astype(BF16)
    read_high, read_low = split2(vread[...])
    read2 = jnp.concatenate([read_high, read_low], axis=0)
    up = nn(basis, vup[...])
    query, key, value = nn(basis, vqkv[0]), nn(basis, vqkv[1]), nn(basis, vqkv[2])
    both = nt(read2, vwout[...])
    out_read = both[:NV] + both[NV:]
    both = nt(read2, vdown[...])
    down_read = (both[:NV] + both[NV:]) * 0.5
    lane = iota((1, 128), 1)
    heads = (lane < HEAD, lane >= HEAD)
    key = key[:24] * (1.0 / math.sqrt(HEAD))
    zero_key = jnp.zeros((48, 128), F32)
    zero_out = jnp.zeros((32, 128), F32)
    keys = jnp.concatenate([jnp.where(h, key, 0.0) for h in heads], axis=0)
    outs = jnp.concatenate([jnp.where(h, out_read, 0.0) for h in heads], axis=0)
    right = jnp.concatenate(
        [
            jnp.concatenate([keys, zero_key], axis=1),
            jnp.concatenate([zero_out, outs], axis=1),
            jnp.zeros((48, 256), F32),
        ],
        axis=0,
    )
    attend = nt(jnp.concatenate([query, value], axis=1), right, HIGHEST)
    msg[j, 0:32, 0:512] = up.astype(BF16)
    msg[j, 0:32, 512:640] = attend.astype(BF16)
    msg[j, 32:48, 0:512] = down_read.astype(BF16)
    msg[j, 32:48, 512:640] = jnp.zeros((16, 128), BF16)
    def share_copy(owner, k, place):
        return pltpu.make_async_remote_copy(
            src_ref=msg.at[owner], dst_ref=msg.at[owner], send_sem=msg_send.at[k], recv_sem=msg_recv.at[k],
            device_id={"mp": place}, device_id_type=MESH,
        )

    to_core = share_copy(j, 0, peers[1])
    to_chip = share_copy(j, 1, peers[2])
    onward = share_copy(peers[2], 2, peers[1])

    @pl.when(core == 1)
    def _():
        pl.semaphore_wait(barrier, jnp.where(me == 0, 3, 5))
        pl.semaphore_signal(all_in, inc=1, device_id={"mp": peers[1]}, device_id_type=MESH)

    @pl.when(core == 0)
    def _():
        pl.semaphore_wait(all_in, 1)


    @pl.when(me != 0)
    def _():
        send_f.start()
        send_p.start()

    to_core.start()
    to_chip.start()

    gram = nt(basis, basis)
    gram_high = gram.astype(BF16)
    gram_mid, gram_low = split2(gram - gram_high.astype(F32))
    both = nt(read2, basis)
    own_high, own_low = split2((both[:NV] + both[NV:]) * 0.5)
    left = jnp.concatenate([gram_high, gram_mid, gram_low, own_high, own_low], axis=0)

    loads[10].wait()
    live = jnp.where(vstretch[...] >= 0, 1.0, 0.0).astype(BF16)
    cell, other = iota((CELLS + 32, 8), 0), iota((CELLS + 32, 8), 1)
    pick = jnp.where(jnp.where(cell < CELLS, cell >> 4, 0) == other, 1.0, 0.0).astype(BF16)
    cell, other = iota((CELLS + 32, 32), 0), iota((CELLS + 32, 32), 1)
    part_row = ACROSS * core + 2 * (cell & 7) + ((cell >> 3) & 1)
    whole_row = 2 * (cell & 15) + ((cell >> 4) & 1)
    mine = other == jnp.where(cell < CELLS, part_row, whole_row)
    mask[...] = nn(jnp.where(mine, nn(pick, live), 0.0).astype(BF16), jnp.ones((32, F), BF16))

    for tile in range(7):
        at = PAD + 8 * tile
        lap = cy[0, 8 * tile : 8 * tile + 8] * ext[:, :, at - 3 : at + 5]
        for offset in range(-2, 4):
            lap = lap + cy[offset + 3, 8 * tile : 8 * tile + 8] * ext[:, :, at + offset : at + offset + 8]
        f0, f1, f2 = ext[:, 0, at : at + 8], ext[:, 1, at : at + 8], ext[:, 2, at : at + 8]
        nothing = jnp.zeros((1, 8, F), F32)
        f3 = jnp.concatenate([f0[1:], nothing], axis=0)
        into = F32(3 * KM[3, 0]) * f0 + F32(3 * KM[3, 1]) * f1 + F32(3 * KM[3, 2]) * f2
        lap0 = (
            F32(6 * KM[0, 0]) * f0 + F32(3 * KM[0, 1]) * f1 + F32(3 * KM[0, 2]) * f2 + F32(3 * KM[0, 3]) * f3
            + jnp.concatenate([nothing, into[:3]], axis=0)
        )
        lap1 = (
            F32(1.2 * KM[1, 0]) * f0 + F32(1.2 * KM[1, 1]) * f1
            + F32(1.2 * KM[1, 2]) * f2 + F32(1.2 * KM[1, 3]) * f3
        )
        lap2 = (
            F32(1.2 * KM[2, 0]) * f0 + F32(1.2 * KM[2, 1]) * f1
            + F32(1.2 * KM[2, 2]) * f2 + F32(1.2 * KM[2, 3]) * f3
        )
        rows = 8 if tile < 6 else 1
        for a, (f, along) in enumerate(((f0, lap0), (f1, lap1), (f2, lap2))):
            fresh[:, a, 8 * tile : 8 * tile + rows] = (f - d * (lap[:, a] + along))[:, :rows]

    row, col = iota((16, 128), 0), iota((16, 128), 1)
    summing = jnp.where((col >> 3) == row, 1.0, 0.0).astype(BF16)
    row, col = iota((256, 16), 0), iota((256, 16), 1)
    repeat = jnp.where(((row >> 5) == (col & 7)) & (((row >> 4) & 1) == (col >> 3)), 1.0, 0.0).astype(BF16)

    def across(x, whole):
        begin, rows = (0, 16) if whole else (24 * core, 8)
        t0, t1, t2, t3 = (
            n12[pl.ds(b, 8, stride=3), :]
            if x == 12
            else fresh[x // 3, x % 3, pl.ds(begin + b, rows, stride=3), :]
            for b in range(4)
        )
        return jnp.concatenate([0.375 * t0 + 0.5 * t1 + 0.125 * t2, 0.125 * t1 + 0.5 * t2 + 0.375 * t3], axis=0)

    def prepare(number, places, slots, whole=False, known={}):
        nodes = {x: known[x] if x in known else across(x, whole) for x in sorted({3 * (p // 2) + p % 2 + i for p in places for i in range(3)})}
        cells = []
        for p in places:
            x0, x1, x2 = (nodes[3 * (p // 2) + p % 2 + i] for i in range(3))
            cells.append(0.375 * x0 + 0.5 * x1 + 0.125 * x2 if p % 2 == 0 else 0.125 * x0 + 0.5 * x1 + 0.375 * x2)
        cells = jnp.concatenate(cells, axis=0).astype(BF16).astype(F32)

        count = (32 if whole else ACROSS) * len(places)
        tok, per = LEV * count, F // count
        turned = jnp.concatenate([cells] + [pltpu.roll(cells, F - NV * q, 1) for q in range(1, per)], axis=0).T
        variables = jnp.concatenate(
            [turned[NV * per * t : NV * per * t + NV] for t in range(LEV // per)], axis=1
        )
        level = iota((16, tok), 1) // count == iota((16, tok), 0)
        u = jnp.concatenate([variables, jnp.where(level, 1.0, 0.0).astype(F32)], axis=0)
        first = nn(left, u.astype(BF16))
        gram_u = first[0:KU] + first[KU : 2 * KU] + first[2 * KU : 3 * KU]
        squares = jnp.sum(gram_u * u, axis=0, keepdims=True)
        scaled = u * lax.rsqrt(squares * F32(1.0 / 512) + F32(1e-5))
        high, low = split2(scaled)
        scaled2 = jnp.concatenate([high, low], axis=0)
        return dict(
            number=number,
            places=places,
            slots=slots,
            count=count,
            per=per,
            scaled2=scaled2,
            tokens=scaled2.astype(F32).T.astype(BF16),
            turns=[lane_turn(scaled[:24], count * k) for k in range(per)],
            total=first[3 * KU : 3 * KU + NV] + first[3 * KU + NV :],
            acc=None,
            atts={},
            sums={},
            spreads={},
        )

    def open_share(half, r):
        folded = msg[half["slots"][r], 0:32, 512:640]
        half["atts"][r] = tn(jnp.concatenate([folded, folded], axis=0), half["scaled2"])

    def hidden_units(half, r):
        slot = half["slots"][r]
        folded = msg[slot, 0:32, 0:512]
        folded2 = jnp.concatenate([folded, folded], axis=0)
        reads = msg[slot, 32:48, 0:512]
        for part in range(2):
            cut = slice(256 * part, 256 * part + 256)
            x = nn(half["tokens"], folded2[:, cut])
            inner = x * (F32(math.sqrt(2 / math.pi)) + F32(math.sqrt(2 / math.pi) * 0.044715) * (x * x))
            hidden = (x + x * jnp.tanh(inner)).astype(BF16)
            term = nt(hidden, reads[:, cut])
            half["acc"] = term if half["acc"] is None else half["acc"] + term

    def scores(half, r):
        att, turns, per = half["atts"][r], half["turns"], half["per"]
        prods = []
        for h in range(2):
            for k in range(LEV):
                prod = att[24 * h : 24 * h + 24] * lane_turn(turns[k % per], F * (k // per))
                prods.append(prod[0:8] + prod[8:16] + prod[16:24])
        half["sums"][r] = nn(summing, jnp.concatenate(prods, axis=0).astype(BF16))

    def probabilities(half, r):
        expo = jnp.exp(half["sums"][r])
        prob = jnp.concatenate(
            [e / jnp.sum(e, axis=0, keepdims=True) for e in (expo[0:8], expo[8:16])], axis=0
        ).astype(BF16)
        half["spreads"][r] = nn(repeat, prob)

    def mix(half, r):
        att, spread, per = half["atts"][r], half["spreads"][r], half["per"]
        values = [lane_turn(att[48:80], half["count"] * k) for k in range(per)]
        mixed = None
        for k in range(LEV):
            term = spread[32 * k : 32 * k + 32] * lane_turn(values[k % per], F * (k // per))
            mixed = term if mixed is None else mixed + term
        half["total"] = half["total"] + mixed[0:16] + mixed[16:32]

    def shares(*pairs):
        for pair in pairs:
            open_share(*pair)
        stages = (scores, probabilities, mix)
        for i, pair in enumerate(pairs):
            hidden_units(*pair)
            for stage in stages[i : i + 1] if i < len(pairs) - 1 else stages[i:]:
                for other in pairs:
                    stage(*other)

    def turned_back(half):
        total, acc, count, per = half["total"], half["acc"], half["count"], half["per"]
        tiles = LEV // per
        pieces = []
        for t in range(tiles):
            pieces += [total[:, F * t : F * t + F], jnp.zeros((NV * (per - 1), F), F32)]
        turned = jnp.concatenate(pieces, axis=0).T
        wide = jnp.concatenate([acc, jnp.zeros((LEV * count, F - NV), F32)], axis=1)
        for t in range(tiles):
            block = wide[F * t : F * t + F]
            turned = turned + (block if t == 0 else pltpu.roll(block, NV * per * t, 1))
        result = turned[0:count]
        for q in range(1, per):
            result = result + pltpu.roll(turned[count * q : count * q + count], NV * q, 1)
        return result

    def finish(half, skip=0):
        live = jnp.concatenate([mask[ACROSS * p : ACROSS * p + ACROSS] for p in half["places"]], axis=0)
        buffer, n = tbufs[half["number"]], half["number"]
        buffer[0] = jnp.where(live > 0.5, turned_back(half), 0.0).astype(BF16)
        rows = pl.ds(ACROSS * skip, ACROSS * (len(half["places"]) - skip))
        half["sends"] = {}
        for r in (2, 3, 1):
            copy = pltpu.make_async_remote_copy(
                src_ref=buffer.at[0, rows], dst_ref=buffer.at[r, rows], send_sem=t_send.at[n, r], recv_sem=t_recv.at[n, r],
                device_id={"mp": peers[r]}, device_id_type=MESH,
            )
            copy.start()
            half["sends"][r] = copy

    def place_rows(half, skip=()):
        buffer = tbufs[half["number"]]
        for r, owner in ((0, core), (1, 1 - core)):
            if r:
                half["sends"][1].wait_recv()
            half["sends"][r + 2].wait_recv()
            block = buffer[r].astype(F32) + buffer[r + 2].astype(F32)
            for i, p in enumerate(half["places"]):
                for c in range(2):
                    if p not in skip:
                        at = ACROSS * i + 8 * c
                        tend[pl.ds(128 * owner + 8 * c + p, 8, stride=16), :] = block[at : at + 8]

    chip = (j, peers[1])
    inner = prepare(0, (1, 2, 3, 4), chip)
    shares((inner, 0))
    to_core.wait_recv()
    shares((inner, 1))
    finish(inner)

    to_chip.wait_recv()
    onward.start()
    send_f.wait_recv()
    for a, weight in enumerate((3 * KM[0, 3], 1.2 * KM[1, 3], 1.2 * KM[2, 3])):
        fresh[3, a] = fresh[3, a] - (d * F32(weight)) * f12[...]
    send_p.wait_recv()
    n12[...] = precv[...] - gown[pl.ds(first_row, 32)]
    eastern = prepare(1, (4, 5, 6, 7), chip)
    shares((eastern, 0), (eastern, 1))
    finish(eastern, skip=1)
    place_rows(inner)

    @pl.when(me == 0)
    def _():
        place_rows(eastern, skip=(4,))

    onward.wait_recv()

    @pl.when(me == 0)
    def _():
        pl.semaphore_wait(west_in, 1)
        send_f.start()
        send_p.start()

    known = {x: across(x, True) for x in (1, 2)}
    send_g.wait_recv()
    fresh[0, 0] = fresh[0, 0] - grecv[...].astype(F32)[0:Y]
    western = prepare(2, (0,), (0, 1, 2, 3), whole=True, known=known)
    western["total"] = western["total"] * 2.0
    shares((western, 0), (western, 1), (western, 2), (western, 3))
    result = jnp.where(mask[CELLS : CELLS + 32] > 0.5, turned_back(western), 0.0)
    for c in range(2):
        tend[pl.ds(8 * c, 16, stride=16), :] = result[16 * c : 16 * c + 16]

    @pl.when(me != 0)
    def _():
        place_rows(eastern, skip=(4,))

    sent = [send_f, send_p, to_core, to_chip, onward, *inner["sends"].values(), *eastern["sends"].values()]
    for copy in sent:
        copy.wait_send()

    @pl.when(core == 0)
    def _():
        send_g.wait_send()
        send_g_other.wait_send()


def store(new, tend, new_out, tend_out, sem):
    first = pltpu.make_async_copy(new, new_out, sem.at[0])
    second = pltpu.make_async_copy(tend, tend_out, sem.at[1])
    first.start()
    second.start()
    first.wait()
    second.wait()


def local(elems, state_field, diffusion, stretch, w_in, lemb, w_qkv, w_out, w_up, w_down, w_read):
    state = jnp.transpose(state_field, (1, 0, 2)).reshape(4, 3, Y, F)
    operands = (
        state, diffusion.reshape(1, F), jnp.transpose(stretch), w_in, lemb,
        w_qkv, w_out, w_up, w_down, jnp.transpose(w_read),
    )
    vm = pltpu.VMEM
    dma = pltpu.SemaphoreType.DMA
    new, tend = pl.pallas_call(
        lambda *refs: kernel(elems, *refs),
        out_shape=(
            jax.ShapeDtypeStruct((4, 3, Y, F), F32),
            jax.ShapeDtypeStruct((256, F), F32),
        ),
        in_specs=[pl.BlockSpec(memory_space=pltpu.HBM)] * 10,
        out_specs=[pl.BlockSpec(memory_space=pltpu.VMEM)] * 2,
        scratch_shapes=[
            vm((4, 3, Y, F), F32),
            vm((4, 3, PAD + 64, F), F32),
            vm((7, ROWS, F), F32),
            vm((32, F), F32),
            vm((ROWS, F), F32),
            vm((Y, F), F32),
            vm((64, F), BF16),
            vm((64, F), BF16),
            vm((ROWS, F), F32),
            vm((32, F), F32),
            vm((1, F), F32),
            vm((8, 32), jnp.int32),
            vm((16, 512), BF16),
            vm((8, 512), BF16),
            vm((3, 512, 128), BF16),
            vm((128, 512), BF16),
            vm((512, 512), BF16),
            vm((512, 512), BF16),
            vm((16, 512), F32),
            vm((4, 48, 640), BF16),
            vm((CELLS + 32, F), F32),
            vm((4, 4 * ACROSS, F), BF16),
            vm((4, 4 * ACROSS, F), BF16),
            dma((11,)),
            dma((4,)),
            dma((3,)),
            dma((3,)),
            dma((3,)),
            dma((2, 4)),
            dma((2, 4)),
            pltpu.SemaphoreType.REGULAR,
            pltpu.SemaphoreType.REGULAR,
        ],
        compiler_params=pltpu.CompilerParams(
            collective_id=0, has_side_effects=True, vmem_limit_bytes=40 * 1024 * 1024
        ),
        name="step",
    )(*(pltpu.with_memory_space_constraint(x, pltpu.HBM) for x in operands))
    new, tend = (pltpu.with_memory_space_constraint(x, pltpu.VMEM) for x in (new, tend))
    new, tend = pl.pallas_call(
        store,
        out_shape=(jax.ShapeDtypeStruct(new.shape, F32), jax.ShapeDtypeStruct(tend.shape, F32)),
        in_specs=[pl.BlockSpec(memory_space=pltpu.VMEM)] * 2,
        out_specs=[pl.BlockSpec(memory_space=pltpu.HBM)] * 2,
        scratch_shapes=[dma((2,))],
        name="store",
    )(new, tend)
    return jnp.transpose(new.reshape(12, Y, F), (1, 0, 2)), tend.reshape(32, 8, F)


def solution(mesh):
    elems = mesh.shape["elem"]
    in_specs = (
        P(None, "elem", None),
        P(),
        P(None, "elem"),
        P(),
        P(),
        P(None, None, "mp"),
        P("mp", None),
        P(None, "mp"),
        P("mp", None),
        P(),
    )
    out_specs = (P(None, "elem", None), P(None, "elem", None))
    return jax.shard_map(
        lambda *args: local(elems, *args), mesh=mesh, in_specs=in_specs, out_specs=out_specs, check_vma=False
    )
```

```python
import math

import jax
import jax.numpy as jnp
import numpy as np
from jax import lax
from jax.experimental import pallas as pl
from jax.experimental.pallas import tpu as pltpu
from jax.sharding import PartitionSpec as P

MESH = pl.DeviceIdType.MESH
F32 = jnp.float32
BF16 = jnp.bfloat16
HIGHEST = lax.Precision.HIGHEST

LEV = 8
NV = 16
F = 128
HEAD = 64
Y = 49
ROWS = 56
PAD = 8
ACROSS = 16
CELLS = 8 * ACROSS
KU = 32


def stiffness_1d():
    points = np.array([-1.0, -1.0 / math.sqrt(5.0), 1.0 / math.sqrt(5.0), 1.0])
    weight = np.array([1.0, 5.0, 5.0, 1.0]) / 6.0
    basis = [np.prod([points[i] - points[o] for o in range(4) if o != i]) for i in range(4)]
    dmat = np.zeros((4, 4))
    for i in range(4):
        for k in range(4):
            if i == k:
                dmat[i, k] = sum(1.0 / (points[i] - points[o]) for o in range(4) if o != i)
            else:
                dmat[i, k] = basis[i] / basis[k] / (points[i] - points[k])
    return dmat.T @ (weight[:, None] * dmat)


KM = stiffness_1d()


def nt(a, b, precision=None):
    return lax.dot_general(a, b, (((1,), (1,)), ((), ())), precision=precision, preferred_element_type=F32)


def tn(a, b):
    return lax.dot_general(a, b, (((0,), (0,)), ((), ())), preferred_element_type=F32)


def nn(a, b):
    return jnp.dot(a, b, preferred_element_type=F32)


def iota(shape, dim):
    return lax.broadcasted_iota(jnp.int32, shape, dim)


def split2(x):
    high = x.astype(BF16)
    return high, (x - high.astype(F32)).astype(BF16)


def lane_turn(x, by):
    return x if by == 0 else jnp.concatenate([x[:, by:], x[:, :by]], axis=1)


def band_along_y(offset):
    y = iota((ROWS, F), 0)
    kind = y - 3 * ((y * 171) >> 9)
    out = jnp.zeros((ROWS, F), F32)
    if 0 <= offset + 1 < 4:
        out = jnp.where(kind == 1, F32(1.2 * KM[1, offset + 1]), out)
    if 0 <= offset + 2 < 4:
        out = jnp.where(kind == 2, F32(1.2 * KM[2, offset + 2]), out)
    corner = jnp.zeros((ROWS, F), F32)
    if offset >= 0:
        corner = corner + jnp.where(y < Y - 1, F32(KM[0, offset]), F32(0))
    if offset <= 0:
        corner = corner + jnp.where(y > 0, F32(KM[3, offset + 3]), F32(0))
    corner = corner * jnp.where((y == 0) | (y == Y - 1), F32(6), F32(3))
    out = jnp.where(kind == 0, corner, out)
    return jnp.where(y < Y, out, F32(0))


def kernel(
    elems, state, diff, stretch, w_in, lemb, w_qkv, w_out, w_up, w_down, w_read,
    fresh, tend,
    st, ext, cy, n12, gown, f12, gsend, grecv, psend, precv,
    vdiff, vstretch, vin, vlev, vqkv, vwout, vup, vdown, vread,
    msg, mask, tbuf0, tbuf1,
    load_sem, halo_send, halo_recv, msg_send, msg_recv, t_send, t_recv, west_in, all_in,
):
    me = lax.axis_index("elem")
    j = lax.axis_index("mp")
    tbufs = (tbuf0, tbuf1)
    peers = (None, j + 1 - 2 * lax.rem(j, 2), lax.rem(j + 2, 4), 3 - j)

    core = lax.rem(j, 2)
    east = {"elem": lax.rem(me + 1, elems), "mp": peers[2]}
    east_other = {"elem": lax.rem(me + 1, elems), "mp": peers[3]}
    west = {"elem": lax.rem(me + elems - 1, elems), "mp": peers[2]}
    west_first = {"elem": lax.rem(me + elems - 1, elems), "mp": peers[2] - core}
    east_second = {"elem": lax.rem(me + 1, elems), "mp": peers[2] - core + 1}

    loads = [
        pltpu.make_async_copy(src, dst, load_sem.at[i])
        for i, (src, dst) in enumerate(
            [
                (state.at[3], st.at[3]), (diff, vdiff), (state.at[0:3], st.at[0:3]), (w_in, vin), (lemb, vlev), (w_read, vread),
                (w_qkv, vqkv), (w_up, vup), (w_out, vwout), (w_down, vdown), (stretch, vstretch),
            ]
        )
    ]
    loads[0].start()
    loads[1].start()

    barrier = pltpu.get_barrier_semaphore()
    pl.semaphore_signal(barrier, inc=1, device_id=west_first, device_id_type=MESH)
    pl.semaphore_signal(barrier, inc=1, device_id={"mp": peers[2] - core + 1}, device_id_type=MESH)

    pl.semaphore_signal(barrier, inc=1, device_id={"mp": peers[1]}, device_id_type=MESH)

    @pl.when(me != elems - 1)
    def _():
        pl.semaphore_signal(barrier, inc=1, device_id=east_second, device_id_type=MESH)

    def far(src, dst, k, place, s=None):
        return pltpu.make_async_remote_copy(
            src_ref=src, dst_ref=dst, send_sem=halo_send.at[k if s is None else s], recv_sem=halo_recv.at[k],
            device_id=place, device_id_type=MESH,
        )

    first_row = pl.multiple_of(24 * core, 8)
    send_f = far(state.at[0, 0], f12, 0, west)
    send_p = far(psend.at[pl.ds(first_row, 32)], precv, 1, west)
    send_g = far(gsend, grecv, 2, east)
    send_g_other = far(gsend, grecv, 2, east_other, 3)

    for copy in loads[2:]:
        copy.start()

    @pl.when(core == 0)
    def _():
        pl.semaphore_wait(barrier, 3)

        @pl.when(me == elems - 1)
        def _():
            pl.semaphore_signal(west_in, inc=1, device_id=east_other, device_id_type=MESH)
            pl.semaphore_signal(west_in, inc=1, device_id=east, device_id_type=MESH)

    loads[0].wait()
    loads[1].wait()
    d = vdiff[...]
    share = d * (3.0 * (F32(KM[3, 0]) * st[3, 0] + F32(KM[3, 1]) * st[3, 1] + F32(KM[3, 2]) * st[3, 2]))
    gown[0:Y] = share
    gsend[...] = jnp.concatenate([share, jnp.zeros((64 - Y, F), F32)], axis=0).astype(BF16)

    @pl.when(core == 0)
    def _():
        send_g_other.start()
        send_g.start()

    for offset in range(-3, 4):
        cy[offset + 3] = band_along_y(offset)
    ext[:, :, 0:PAD, :] = jnp.zeros((4, 3, PAD, F), F32)
    ext[:, :, PAD + 48 : PAD + 64, :] = jnp.zeros((4, 3, 16, F), F32)

    loads[2].wait()
    ext[:, :, PAD : PAD + Y, :] = st[...]
    body = slice(PAD, PAD + ROWS)
    f0, f1, f2, f3 = ext[0, 0, body], ext[0, 1, body], ext[0, 2, body], ext[1, 0, body]
    lap = 3.0 * (F32(2 * KM[0, 0]) * f0 + F32(KM[0, 1]) * f1 + F32(KM[0, 2]) * f2 + F32(KM[0, 3]) * f3)
    for offset in range(-3, 4):
        lap = lap + cy[offset + 3] * ext[0, 0, PAD + offset : PAD + offset + ROWS]
    psend[...] = f0 - d * lap

    for copy in loads[3:10]:
        copy.wait()
    basis = jnp.concatenate(
        [vin[...].astype(F32), vlev[...].astype(F32), jnp.zeros((8, 512), F32)], axis=0
    ).astype(BF16)
    read_high, read_low = split2(vread[...])
    read2 = jnp.concatenate([read_high, read_low], axis=0)
    up = nn(basis, vup[...])
    query, key, value = nn(basis, vqkv[0]), nn(basis, vqkv[1]), nn(basis, vqkv[2])
    both = nt(read2, vwout[...])
    out_read = both[:NV] + both[NV:]
    both = nt(read2, vdown[...])
    down_read = (both[:NV] + both[NV:]) * 0.5
    lane = iota((1, 128), 1)
    heads = (lane < HEAD, lane >= HEAD)
    key = key[:24] * (1.0 / math.sqrt(HEAD))
    zero_key = jnp.zeros((48, 128), F32)
    zero_out = jnp.zeros((32, 128), F32)
    keys = jnp.concatenate([jnp.where(h, key, 0.0) for h in heads], axis=0)
    outs = jnp.concatenate([jnp.where(h, out_read, 0.0) for h in heads], axis=0)
    right = jnp.concatenate(
        [
            jnp.concatenate([keys, zero_key], axis=1),
            jnp.concatenate([zero_out, outs], axis=1),
            jnp.zeros((48, 256), F32),
        ],
        axis=0,
    )
    attend = nt(jnp.concatenate([query, value], axis=1), right, HIGHEST)
    msg[j, 0:32, 0:512] = up.astype(BF16)
    msg[j, 0:32, 512:640] = attend.astype(BF16)
    msg[j, 32:48, 0:512] = down_read.astype(BF16)
    msg[j, 32:48, 512:640] = jnp.zeros((16, 128), BF16)
    def share_copy(owner, k, place):
        return pltpu.make_async_remote_copy(
            src_ref=msg.at[owner], dst_ref=msg.at[owner], send_sem=msg_send.at[k], recv_sem=msg_recv.at[k],
            device_id={"mp": place}, device_id_type=MESH,
        )

    to_core = share_copy(j, 0, peers[1])
    to_chip = share_copy(j, 1, peers[2])
    onward = share_copy(peers[2], 2, peers[1])

    @pl.when(core == 1)
    def _():
        pl.semaphore_wait(barrier, jnp.where(me == 0, 3, 5))
        pl.semaphore_signal(all_in, inc=1, device_id={"mp": peers[1]}, device_id_type=MESH)

    @pl.when(core == 0)
    def _():
        pl.semaphore_wait(all_in, 1)


    @pl.when(me != 0)
    def _():
        send_f.start()
        send_p.start()

    to_core.start()
    to_chip.start()

    gram = nt(basis, basis)
    gram_high = gram.astype(BF16)
    gram_mid, gram_low = split2(gram - gram_high.astype(F32))
    both = nt(read2, basis)
    own_high, own_low = split2((both[:NV] + both[NV:]) * 0.5)
    left = jnp.concatenate([gram_high, gram_mid, gram_low, own_high, own_low], axis=0)

    loads[10].wait()
    live = jnp.where(vstretch[...] >= 0, 1.0, 0.0).astype(BF16)
    cell, other = iota((CELLS + 32, 8), 0), iota((CELLS + 32, 8), 1)
    pick = jnp.where(jnp.where(cell < CELLS, cell >> 4, 0) == other, 1.0, 0.0).astype(BF16)
    cell, other = iota((CELLS + 32, 32), 0), iota((CELLS + 32, 32), 1)
    part_row = ACROSS * core + 2 * (cell & 7) + ((cell >> 3) & 1)
    whole_row = 2 * (cell & 15) + ((cell >> 4) & 1)
    mine = other == jnp.where(cell < CELLS, part_row, whole_row)
    mask[...] = nn(jnp.where(mine, nn(pick, live), 0.0).astype(BF16), jnp.ones((32, F), BF16))

    for tile in range(7):
        at = PAD + 8 * tile
        lap = cy[0, 8 * tile : 8 * tile + 8] * ext[:, :, at - 3 : at + 5]
        for offset in range(-2, 4):
            lap = lap + cy[offset + 3, 8 * tile : 8 * tile + 8] * ext[:, :, at + offset : at + offset + 8]
        f0, f1, f2 = ext[:, 0, at : at + 8], ext[:, 1, at : at + 8], ext[:, 2, at : at + 8]
        nothing = jnp.zeros((1, 8, F), F32)
        f3 = jnp.concatenate([f0[1:], nothing], axis=0)
        into = F32(3 * KM[3, 0]) * f0 + F32(3 * KM[3, 1]) * f1 + F32(3 * KM[3, 2]) * f2
        lap0 = (
            F32(6 * KM[0, 0]) * f0 + F32(3 * KM[0, 1]) * f1 + F32(3 * KM[0, 2]) * f2 + F32(3 * KM[0, 3]) * f3
            + jnp.concatenate([nothing, into[:3]], axis=0)
        )
        lap1 = (
            F32(1.2 * KM[1, 0]) * f0 + F32(1.2 * KM[1, 1]) * f1
            + F32(1.2 * KM[1, 2]) * f2 + F32(1.2 * KM[1, 3]) * f3
        )
        lap2 = (
            F32(1.2 * KM[2, 0]) * f0 + F32(1.2 * KM[2, 1]) * f1
            + F32(1.2 * KM[2, 2]) * f2 + F32(1.2 * KM[2, 3]) * f3
        )
        rows = 8 if tile < 6 else 1
        for a, (f, along) in enumerate(((f0, lap0), (f1, lap1), (f2, lap2))):
            fresh[:, a, 8 * tile : 8 * tile + rows] = (f - d * (lap[:, a] + along))[:, :rows]

    row, col = iota((16, 128), 0), iota((16, 128), 1)
    summing = jnp.where((col >> 3) == row, 1.0, 0.0).astype(BF16)
    row, col = iota((256, 16), 0), iota((256, 16), 1)
    repeat = jnp.where(((row >> 5) == (col & 7)) & (((row >> 4) & 1) == (col >> 3)), 1.0, 0.0).astype(BF16)

    def across(x, whole):
        begin, rows = (0, 16) if whole else (24 * core, 8)
        t0, t1, t2, t3 = (
            n12[pl.ds(b, 8, stride=3), :]
            if x == 12
            else fresh[x // 3, x % 3, pl.ds(begin + b, rows, stride=3), :]
            for b in range(4)
        )
        return jnp.concatenate([0.375 * t0 + 0.5 * t1 + 0.125 * t2, 0.125 * t1 + 0.5 * t2 + 0.375 * t3], axis=0)

    def prepare(number, places, slots, whole=False, known={}):
        nodes = {x: known[x] if x in known else across(x, whole) for x in sorted({3 * (p // 2) + p % 2 + i for p in places for i in range(3)})}
        cells = []
        for p in places:
            x0, x1, x2 = (nodes[3 * (p // 2) + p % 2 + i] for i in range(3))
            cells.append(0.375 * x0 + 0.5 * x1 + 0.125 * x2 if p % 2 == 0 else 0.125 * x0 + 0.5 * x1 + 0.375 * x2)
        cells = jnp.concatenate(cells, axis=0).astype(BF16).astype(F32)

        count = (32 if whole else ACROSS) * len(places)
        tok, per = LEV * count, F // count
        turned = jnp.concatenate([cells] + [pltpu.roll(cells, F - NV * q, 1) for q in range(1, per)], axis=0).T
        variables = jnp.concatenate(
            [turned[NV * per * t : NV * per * t + NV] for t in range(LEV // per)], axis=1
        )
        level = iota((16, tok), 1) // count == iota((16, tok), 0)
        u = jnp.concatenate([variables, jnp.where(level, 1.0, 0.0).astype(F32)], axis=0)
        first = nn(left, u.astype(BF16))
        gram_u = first[0:KU] + first[KU : 2 * KU] + first[2 * KU : 3 * KU]
        squares = jnp.maximum(jnp.sum(gram_u * u, axis=0, keepdims=True), 0.0)
        scaled = u * lax.rsqrt(squares * F32(1.0 / 512) + F32(1e-5))
        high, low = split2(scaled)
        scaled2 = jnp.concatenate([high, low], axis=0)
        return dict(
            number=number,
            places=places,
            slots=slots,
            count=count,
            per=per,
            scaled2=scaled2,
            tokens=scaled2.astype(F32).T.astype(BF16),
            turns=[lane_turn(scaled[:24], count * k) for k in range(per)],
            total=first[3 * KU : 3 * KU + NV] + first[3 * KU + NV :],
            acc=None,
            atts={},
            sums={},
            spreads={},
        )

    def open_share(half, r):
        folded = msg[half["slots"][r], 0:32, 512:640]
        half["atts"][r] = tn(jnp.concatenate([folded, folded], axis=0), half["scaled2"])

    def hidden_units(half, r):
        slot = half["slots"][r]
        folded = msg[slot, 0:32, 0:512]
        folded2 = jnp.concatenate([folded, folded], axis=0)
        reads = msg[slot, 32:48, 0:512]
        for part in range(2):
            cut = slice(256 * part, 256 * part + 256)
            x = nn(half["tokens"], folded2[:, cut])
            inner = x * (F32(math.sqrt(2 / math.pi)) + F32(math.sqrt(2 / math.pi) * 0.044715) * (x * x))
            hidden = (x + x * jnp.tanh(inner)).astype(BF16)
            term = nt(hidden, reads[:, cut])
            half["acc"] = term if half["acc"] is None else half["acc"] + term

    def scores(half, r):
        att, turns, per = half["atts"][r], half["turns"], half["per"]
        prods = []
        for h in range(2):
            for k in range(LEV):
                prod = att[24 * h : 24 * h + 24] * lane_turn(turns[k % per], F * (k // per))
                prods.append(prod[0:8] + prod[8:16] + prod[16:24])
        half["sums"][r] = nn(summing, jnp.concatenate(prods, axis=0).astype(BF16))

    def probabilities(half, r):
        expo = jnp.exp(half["sums"][r])
        prob = jnp.concatenate(
            [e / jnp.sum(e, axis=0, keepdims=True) for e in (expo[0:8], expo[8:16])], axis=0
        ).astype(BF16)
        half["spreads"][r] = nn(repeat, prob)

    def mix(half, r):
        att, spread, per = half["atts"][r], half["spreads"][r], half["per"]
        values = [lane_turn(att[48:80], half["count"] * k) for k in range(per)]
        mixed = None
        for k in range(LEV):
            term = spread[32 * k : 32 * k + 32] * lane_turn(values[k % per], F * (k // per))
            mixed = term if mixed is None else mixed + term
        half["total"] = half["total"] + mixed[0:16] + mixed[16:32]

    def shares(*pairs):
        for pair in pairs:
            open_share(*pair)
        stages = (scores, probabilities, mix)
        for i, pair in enumerate(pairs):
            hidden_units(*pair)
            for stage in stages[i : i + 1] if i < len(pairs) - 1 else stages[i:]:
                for other in pairs:
                    stage(*other)

    def turned_back(half):
        total, acc, count, per = half["total"], half["acc"], half["count"], half["per"]
        tiles = LEV // per
        pieces = []
        for t in range(tiles):
            pieces += [total[:, F * t : F * t + F], jnp.zeros((NV * (per - 1), F), F32)]
        turned = jnp.concatenate(pieces, axis=0).T
        wide = jnp.concatenate([acc, jnp.zeros((LEV * count, F - NV), F32)], axis=1)
        for t in range(tiles):
            block = wide[F * t : F * t + F]
            turned = turned + (block if t == 0 else pltpu.roll(block, NV * per * t, 1))
        result = turned[0:count]
        for q in range(1, per):
            result = result + pltpu.roll(turned[count * q : count * q + count], NV * q, 1)
        return result

    def finish(half, skip=0):
        live = jnp.concatenate([mask[ACROSS * p : ACROSS * p + ACROSS] for p in half["places"]], axis=0)
        buffer, n = tbufs[half["number"]], half["number"]
        buffer[0] = jnp.where(live > 0.5, turned_back(half), 0.0).astype(BF16)
        rows = pl.ds(ACROSS * skip, ACROSS * (len(half["places"]) - skip))
        half["sends"] = {}
        for r in (2, 3, 1):
            copy = pltpu.make_async_remote_copy(
                src_ref=buffer.at[0, rows], dst_ref=buffer.at[r, rows], send_sem=t_send.at[n, r], recv_sem=t_recv.at[n, r],
                device_id={"mp": peers[r]}, device_id_type=MESH,
            )
            copy.start()
            half["sends"][r] = copy

    def place_rows(half, skip=()):
        buffer = tbufs[half["number"]]
        for r, owner in ((0, core), (1, 1 - core)):
            if r:
                half["sends"][1].wait_recv()
            half["sends"][r + 2].wait_recv()
            block = buffer[r].astype(F32) + buffer[r + 2].astype(F32)
            for i, p in enumerate(half["places"]):
                for c in range(2):
                    if p not in skip:
                        at = ACROSS * i + 8 * c
                        tend[pl.ds(128 * owner + 8 * c + p, 8, stride=16), :] = block[at : at + 8]

    chip = (j, peers[1])
    inner = prepare(0, (1, 2, 3, 4), chip)
    shares((inner, 0))
    to_core.wait_recv()
    shares((inner, 1))
    finish(inner)

    to_chip.wait_recv()
    onward.start()
    send_f.wait_recv()
    for a, weight in enumerate((3 * KM[0, 3], 1.2 * KM[1, 3], 1.2 * KM[2, 3])):
        fresh[3, a] = fresh[3, a] - (d * F32(weight)) * f12[...]
    send_p.wait_recv()
    n12[...] = precv[...] - gown[pl.ds(first_row, 32)]
    eastern = prepare(1, (4, 5, 6, 7), chip)
    shares((eastern, 0), (eastern, 1))
    finish(eastern, skip=1)
    place_rows(inner)

    @pl.when(me == 0)
    def _():
        place_rows(eastern, skip=(4,))

    onward.wait_recv()

    @pl.when(me == 0)
    def _():
        pl.semaphore_wait(west_in, 1)
        send_f.start()
        send_p.start()

    for copy in (to_core, to_chip, onward, *inner["sends"].values()):
        copy.wait_send()

    @pl.when(core == 0)
    def _():
        send_g.wait_send()
        send_g_other.wait_send()

    known = {x: across(x, True) for x in (1, 2)}
    send_g.wait_recv()
    fresh[0, 0] = fresh[0, 0] - grecv[...].astype(F32)[0:Y]
    western = prepare(2, (0,), (0, 1, 2, 3), whole=True, known=known)
    western["total"] = western["total"] * 2.0
    shares((western, 0), (western, 1), (western, 2), (western, 3))
    result = jnp.where(mask[CELLS : CELLS + 32] > 0.5, turned_back(western), 0.0)
    for c in range(2):
        tend[pl.ds(8 * c, 16, stride=16), :] = result[16 * c : 16 * c + 16]

    @pl.when(me != 0)
    def _():
        place_rows(eastern, skip=(4,))

    for copy in (send_f, send_p, *eastern["sends"].values()):
        copy.wait_send()


def store(new, tend, new_out, tend_out, sem):
    first = pltpu.make_async_copy(new, new_out, sem.at[0])
    second = pltpu.make_async_copy(tend, tend_out, sem.at[1])
    first.start()
    second.start()
    first.wait()
    second.wait()


def local(elems, state_field, diffusion, stretch, w_in, lemb, w_qkv, w_out, w_up, w_down, w_read):
    state = jnp.transpose(state_field, (1, 0, 2)).reshape(4, 3, Y, F)
    operands = (
        state, diffusion.reshape(1, F), jnp.transpose(stretch), w_in, lemb,
        w_qkv, w_out, w_up, w_down, jnp.transpose(w_read),
    )
    vm = pltpu.VMEM
    dma = pltpu.SemaphoreType.DMA
    new, tend = pl.pallas_call(
        lambda *refs: kernel(elems, *refs),
        out_shape=(
            jax.ShapeDtypeStruct((4, 3, Y, F), F32),
            jax.ShapeDtypeStruct((256, F), F32),
        ),
        in_specs=[pl.BlockSpec(memory_space=pltpu.HBM)] * 10,
        out_specs=[pl.BlockSpec(memory_space=pltpu.VMEM)] * 2,
        scratch_shapes=[
            vm((4, 3, Y, F), F32),
            vm((4, 3, PAD + 64, F), F32),
            vm((7, ROWS, F), F32),
            vm((32, F), F32),
            vm((ROWS, F), F32),
            vm((Y, F), F32),
            vm((64, F), BF16),
            vm((64, F), BF16),
            vm((ROWS, F), F32),
            vm((32, F), F32),
            vm((1, F), F32),
            vm((8, 32), jnp.int32),
            vm((16, 512), BF16),
            vm((8, 512), BF16),
            vm((3, 512, 128), BF16),
            vm((128, 512), BF16),
            vm((512, 512), BF16),
            vm((512, 512), BF16),
            vm((16, 512), F32),
            vm((4, 48, 640), BF16),
            vm((CELLS + 32, F), F32),
            vm((4, 4 * ACROSS, F), BF16),
            vm((4, 4 * ACROSS, F), BF16),
            dma((11,)),
            dma((4,)),
            dma((3,)),
            dma((3,)),
            dma((3,)),
            dma((2, 4)),
            dma((2, 4)),
            pltpu.SemaphoreType.REGULAR,
            pltpu.SemaphoreType.REGULAR,
        ],
        compiler_params=pltpu.CompilerParams(
            collective_id=0, has_side_effects=True, vmem_limit_bytes=40 * 1024 * 1024
        ),
        name="step",
    )(*(pltpu.with_memory_space_constraint(x, pltpu.HBM) for x in operands))
    new, tend = (pltpu.with_memory_space_constraint(x, pltpu.VMEM) for x in (new, tend))
    new, tend = pl.pallas_call(
        store,
        out_shape=(jax.ShapeDtypeStruct(new.shape, F32), jax.ShapeDtypeStruct(tend.shape, F32)),
        in_specs=[pl.BlockSpec(memory_space=pltpu.VMEM)] * 2,
        out_specs=[pl.BlockSpec(memory_space=pltpu.HBM)] * 2,
        scratch_shapes=[dma((2,))],
        name="store",
    )(new, tend)
    return jnp.transpose(new.reshape(12, Y, F), (1, 0, 2)), tend.reshape(32, 8, F)


def solution(mesh):
    elems = mesh.shape["elem"]
    in_specs = (
        P(None, "elem", None),
        P(),
        P(None, "elem"),
        P(),
        P(),
        P(None, None, "mp"),
        P("mp", None),
        P(None, "mp"),
        P("mp", None),
        P(),
    )
    out_specs = (P(None, "elem", None), P(None, "elem", None))
    return jax.shard_map(
        lambda *args: local(elems, *args), mesh=mesh, in_specs=in_specs, out_specs=out_specs, check_vma=False
    )
```

```python
import math

import jax
import jax.numpy as jnp
import numpy as np
from jax import lax
from jax.experimental import pallas as pl
from jax.experimental.pallas import tpu as pltpu
from jax.sharding import PartitionSpec as P

MESH = pl.DeviceIdType.MESH
F32 = jnp.float32
BF16 = jnp.bfloat16
HIGHEST = lax.Precision.HIGHEST

LEV = 8
NV = 16
F = 128
HEAD = 64
Y = 49
ROWS = 56
PAD = 8
ACROSS = 16
CELLS = 8 * ACROSS
KU = 32


def stiffness_1d():
    points = np.array([-1.0, -1.0 / math.sqrt(5.0), 1.0 / math.sqrt(5.0), 1.0])
    weight = np.array([1.0, 5.0, 5.0, 1.0]) / 6.0
    basis = [np.prod([points[i] - points[o] for o in range(4) if o != i]) for i in range(4)]
    dmat = np.zeros((4, 4))
    for i in range(4):
        for k in range(4):
            if i == k:
                dmat[i, k] = sum(1.0 / (points[i] - points[o]) for o in range(4) if o != i)
            else:
                dmat[i, k] = basis[i] / basis[k] / (points[i] - points[k])
    return dmat.T @ (weight[:, None] * dmat)


KM = stiffness_1d()


def nt(a, b, precision=None):
    return lax.dot_general(a, b, (((1,), (1,)), ((), ())), precision=precision, preferred_element_type=F32)


def tn(a, b):
    return lax.dot_general(a, b, (((0,), (0,)), ((), ())), preferred_element_type=F32)


def nn(a, b):
    return jnp.dot(a, b, preferred_element_type=F32)


def iota(shape, dim):
    return lax.broadcasted_iota(jnp.int32, shape, dim)


def split2(x):
    high = x.astype(BF16)
    return high, (x - high.astype(F32)).astype(BF16)


def lane_turn(x, by):
    return x if by == 0 else jnp.concatenate([x[:, by:], x[:, :by]], axis=1)


def band_along_y(offset):
    y = iota((ROWS, F), 0)
    kind = y - 3 * ((y * 171) >> 9)
    out = jnp.zeros((ROWS, F), F32)
    if 0 <= offset + 1 < 4:
        out = jnp.where(kind == 1, F32(1.2 * KM[1, offset + 1]), out)
    if 0 <= offset + 2 < 4:
        out = jnp.where(kind == 2, F32(1.2 * KM[2, offset + 2]), out)
    corner = jnp.zeros((ROWS, F), F32)
    if offset >= 0:
        corner = corner + jnp.where(y < Y - 1, F32(KM[0, offset]), F32(0))
    if offset <= 0:
        corner = corner + jnp.where(y > 0, F32(KM[3, offset + 3]), F32(0))
    corner = corner * jnp.where((y == 0) | (y == Y - 1), F32(6), F32(3))
    out = jnp.where(kind == 0, corner, out)
    return jnp.where(y < Y, out, F32(0))


def kernel(
    elems, state, diff, stretch, w_in, lemb, w_qkv, w_out, w_up, w_down, w_read,
    fresh, tend,
    st, ext, cy, n12, gown, f12, gsend, grecv, psend, precv,
    vdiff, vstretch, vin, vlev, vqkv, vwout, vup, vdown, vread,
    msg, mask, tbuf0, tbuf1,
    load_sem, halo_send, halo_recv, msg_send, msg_recv, t_send, t_recv, west_in, all_in,
):
    me = lax.axis_index("elem")
    j = lax.axis_index("mp")
    tbufs = (tbuf0, tbuf1)
    peers = (None, j + 1 - 2 * lax.rem(j, 2), lax.rem(j + 2, 4), 3 - j)

    core = lax.rem(j, 2)
    east = {"elem": lax.rem(me + 1, elems), "mp": peers[2]}
    east_other = {"elem": lax.rem(me + 1, elems), "mp": peers[3]}
    west = {"elem": lax.rem(me + elems - 1, elems), "mp": peers[2]}
    west_first = {"elem": lax.rem(me + elems - 1, elems), "mp": peers[2] - core}
    east_second = {"elem": lax.rem(me + 1, elems), "mp": peers[2] - core + 1}

    loads = [
        pltpu.make_async_copy(src, dst, load_sem.at[i])
        for i, (src, dst) in enumerate(
            [
                (state.at[3], st.at[3]), (diff, vdiff), (state.at[0:3], st.at[0:3]), (w_in, vin), (lemb, vlev), (w_read, vread),
                (w_qkv, vqkv), (w_up, vup), (w_out, vwout), (w_down, vdown), (stretch, vstretch),
            ]
        )
    ]
    loads[0].start()
    loads[1].start()

    barrier = pltpu.get_barrier_semaphore()
    pl.semaphore_signal(barrier, inc=1, device_id=west_first, device_id_type=MESH)
    pl.semaphore_signal(barrier, inc=1, device_id={"mp": peers[2] - core + 1}, device_id_type=MESH)

    pl.semaphore_signal(barrier, inc=1, device_id={"mp": peers[1]}, device_id_type=MESH)

    @pl.when(me != elems - 1)
    def _():
        pl.semaphore_signal(barrier, inc=1, device_id=east_second, device_id_type=MESH)

    def far(src, dst, k, place, s=None):
        return pltpu.make_async_remote_copy(
            src_ref=src, dst_ref=dst, send_sem=halo_send.at[k if s is None else s], recv_sem=halo_recv.at[k],
            device_id=place, device_id_type=MESH,
        )

    first_row = pl.multiple_of(24 * core, 8)
    send_f = far(state.at[0, 0], f12, 0, west)
    send_p = far(psend.at[pl.ds(first_row, 32)], precv, 1, west)
    send_g = far(gsend, grecv, 2, east)
    send_g_other = far(gsend, grecv, 2, east_other, 3)

    for copy in loads[2:]:
        copy.start()

    @pl.when(core == 0)
    def _():
        pl.semaphore_wait(barrier, 3)

        @pl.when(me == elems - 1)
        def _():
            pl.semaphore_signal(west_in, inc=1, device_id=east_other, device_id_type=MESH)
            pl.semaphore_signal(west_in, inc=1, device_id=east, device_id_type=MESH)

    loads[0].wait()
    loads[1].wait()
    d = vdiff[...]
    share = d * (3.0 * (F32(KM[3, 0]) * st[3, 0] + F32(KM[3, 1]) * st[3, 1] + F32(KM[3, 2]) * st[3, 2]))
    gown[0:Y] = share
    gsend[...] = jnp.concatenate([share, jnp.zeros((64 - Y, F), F32)], axis=0).astype(BF16)

    @pl.when(core == 0)
    def _():
        send_g_other.start()
        send_g.start()

    for offset in range(-3, 4):
        cy[offset + 3] = band_along_y(offset)
    ext[:, :, 0:PAD, :] = jnp.zeros((4, 3, PAD, F), F32)
    ext[:, :, PAD + 48 : PAD + 64, :] = jnp.zeros((4, 3, 16, F), F32)

    loads[2].wait()
    ext[:, :, PAD : PAD + Y, :] = st[...]
    body = slice(PAD, PAD + ROWS)
    f0, f1, f2, f3 = ext[0, 0, body], ext[0, 1, body], ext[0, 2, body], ext[1, 0, body]
    lap = 3.0 * (F32(2 * KM[0, 0]) * f0 + F32(KM[0, 1]) * f1 + F32(KM[0, 2]) * f2 + F32(KM[0, 3]) * f3)
    for offset in range(-3, 4):
        lap = lap + cy[offset + 3] * ext[0, 0, PAD + offset : PAD + offset + ROWS]
    psend[...] = f0 - d * lap

    for copy in loads[3:10]:
        copy.wait()
    basis = jnp.concatenate(
        [vin[...].astype(F32), vlev[...].astype(F32), jnp.zeros((8, 512), F32)], axis=0
    ).astype(BF16)
    read_high, read_low = split2(vread[...])
    read2 = jnp.concatenate([read_high, read_low], axis=0)
    up = nn(basis, vup[...])
    query, key, value = nn(basis, vqkv[0]), nn(basis, vqkv[1]), nn(basis, vqkv[2])
    both = nt(read2, vwout[...])
    out_read = both[:NV] + both[NV:]
    both = nt(read2, vdown[...])
    down_read = (both[:NV] + both[NV:]) * 0.5
    lane = iota((1, 128), 1)
    heads = (lane < HEAD, lane >= HEAD)
    key = key[:24] * (1.0 / math.sqrt(HEAD))
    zero_key = jnp.zeros((48, 128), F32)
    zero_out = jnp.zeros((32, 128), F32)
    keys = jnp.concatenate([jnp.where(h, key, 0.0) for h in heads], axis=0)
    outs = jnp.concatenate([jnp.where(h, out_read, 0.0) for h in heads], axis=0)
    right = jnp.concatenate(
        [
            jnp.concatenate([keys, zero_key], axis=1),
            jnp.concatenate([zero_out, outs], axis=1),
            jnp.zeros((48, 256), F32),
        ],
        axis=0,
    )
    attend = nt(jnp.concatenate([query, value], axis=1), right, HIGHEST)
    msg[j, 0:32, 0:512] = up.astype(BF16)
    msg[j, 0:32, 512:640] = attend.astype(BF16)
    msg[j, 32:48, 0:512] = down_read.astype(BF16)
    msg[j, 32:48, 512:640] = jnp.zeros((16, 128), BF16)
    def share_copy(owner, k, place):
        return pltpu.make_async_remote_copy(
            src_ref=msg.at[owner], dst_ref=msg.at[owner], send_sem=msg_send.at[k], recv_sem=msg_recv.at[k],
            device_id={"mp": place}, device_id_type=MESH,
        )

    to_core = share_copy(j, 0, peers[1])
    to_chip = share_copy(j, 1, peers[2])
    onward = share_copy(peers[2], 2, peers[1])

    @pl.when(core == 1)
    def _():
        pl.semaphore_wait(barrier, jnp.where(me == 0, 3, 5))
        pl.semaphore_signal(all_in, inc=1, device_id={"mp": peers[1]}, device_id_type=MESH)

    @pl.when(core == 0)
    def _():
        pl.semaphore_wait(all_in, 1)


    @pl.when(me != 0)
    def _():
        send_f.start()
        send_p.start()

    to_core.start()
    to_chip.start()

    gram = nt(basis, basis)
    gram_high = gram.astype(BF16)
    gram_mid, gram_low = split2(gram - gram_high.astype(F32))
    both = nt(read2, basis)
    own_high, own_low = split2((both[:NV] + both[NV:]) * 0.5)
    left = jnp.concatenate([gram_high, gram_mid, gram_low, own_high, own_low], axis=0)

    loads[10].wait()
    live = jnp.where(vstretch[...] >= 0, 1.0, 0.0).astype(BF16)
    cell, other = iota((CELLS + 32, 8), 0), iota((CELLS + 32, 8), 1)
    pick = jnp.where(jnp.where(cell < CELLS, cell >> 4, 0) == other, 1.0, 0.0).astype(BF16)
    cell, other = iota((CELLS + 32, 32), 0), iota((CELLS + 32, 32), 1)
    part_row = ACROSS * core + 2 * (cell & 7) + ((cell >> 3) & 1)
    whole_row = 2 * (cell & 15) + ((cell >> 4) & 1)
    mine = other == jnp.where(cell < CELLS, part_row, whole_row)
    mask[...] = nn(jnp.where(mine, nn(pick, live), 0.0).astype(BF16), jnp.ones((32, F), BF16))

    for tile in range(7):
        at = PAD + 8 * tile
        lap = cy[0, 8 * tile : 8 * tile + 8] * ext[:, :, at - 3 : at + 5]
        for offset in range(-2, 4):
            lap = lap + cy[offset + 3, 8 * tile : 8 * tile + 8] * ext[:, :, at + offset : at + offset + 8]
        f0, f1, f2 = ext[:, 0, at : at + 8], ext[:, 1, at : at + 8], ext[:, 2, at : at + 8]
        nothing = jnp.zeros((1, 8, F), F32)
        f3 = jnp.concatenate([f0[1:], nothing], axis=0)
        into = F32(3 * KM[3, 0]) * f0 + F32(3 * KM[3, 1]) * f1 + F32(3 * KM[3, 2]) * f2
        lap0 = (
            F32(6 * KM[0, 0]) * f0 + F32(3 * KM[0, 1]) * f1 + F32(3 * KM[0, 2]) * f2 + F32(3 * KM[0, 3]) * f3
            + jnp.concatenate([nothing, into[:3]], axis=0)
        )
        lap1 = (
            F32(1.2 * KM[1, 0]) * f0 + F32(1.2 * KM[1, 1]) * f1
            + F32(1.2 * KM[1, 2]) * f2 + F32(1.2 * KM[1, 3]) * f3
        )
        lap2 = (
            F32(1.2 * KM[2, 0]) * f0 + F32(1.2 * KM[2, 1]) * f1
            + F32(1.2 * KM[2, 2]) * f2 + F32(1.2 * KM[2, 3]) * f3
        )
        rows = 8 if tile < 6 else 1
        for a, (f, along) in enumerate(((f0, lap0), (f1, lap1), (f2, lap2))):
            fresh[:, a, 8 * tile : 8 * tile + rows] = (f - d * (lap[:, a] + along))[:, :rows]

    row, col = iota((16, 128), 0), iota((16, 128), 1)
    summing = jnp.where((col >> 3) == row, 1.0, 0.0).astype(BF16)
    row, col = iota((256, 16), 0), iota((256, 16), 1)
    repeat = jnp.where(((row >> 5) == (col & 7)) & (((row >> 4) & 1) == (col >> 3)), 1.0, 0.0).astype(BF16)

    def across(x, whole):
        begin, rows = (0, 16) if whole else (24 * core, 8)
        t0, t1, t2, t3 = (
            n12[pl.ds(b, 8, stride=3), :]
            if x == 12
            else fresh[x // 3, x % 3, pl.ds(begin + b, rows, stride=3), :]
            for b in range(4)
        )
        return jnp.concatenate([0.375 * t0 + 0.5 * t1 + 0.125 * t2, 0.125 * t1 + 0.5 * t2 + 0.375 * t3], axis=0)

    def prepare(number, places, slots, whole=False, known={}):
        nodes = {x: known[x] if x in known else across(x, whole) for x in sorted({3 * (p // 2) + p % 2 + i for p in places for i in range(3)})}
        cells = []
        for p in places:
            x0, x1, x2 = (nodes[3 * (p // 2) + p % 2 + i] for i in range(3))
            cells.append(0.375 * x0 + 0.5 * x1 + 0.125 * x2 if p % 2 == 0 else 0.125 * x0 + 0.5 * x1 + 0.375 * x2)
        cells = jnp.concatenate(cells, axis=0).astype(BF16).astype(F32)

        count = (32 if whole else ACROSS) * len(places)
        tok, per = LEV * count, F // count
        turned = jnp.concatenate([cells] + [pltpu.roll(cells, F - NV * q, 1) for q in range(1, per)], axis=0).T
        variables = jnp.concatenate(
            [turned[NV * per * t : NV * per * t + NV] for t in range(LEV // per)], axis=1
        )
        level = iota((16, tok), 1) // count == iota((16, tok), 0)
        u = jnp.concatenate([variables, jnp.where(level, 1.0, 0.0).astype(F32)], axis=0)
        first = nn(left, u.astype(BF16))
        gram_u = first[0:KU] + first[KU : 2 * KU] + first[2 * KU : 3 * KU]
        squares = jnp.maximum(jnp.sum(gram_u * u, axis=0, keepdims=True), 0.0)
        scaled = u * lax.rsqrt(squares * F32(1.0 / 512) + F32(1e-5))
        high, low = split2(scaled)
        scaled2 = jnp.concatenate([high, low], axis=0)
        return dict(
            number=number,
            places=places,
            slots=slots,
            whole=whole,
            count=count,
            per=per,
            scaled2=scaled2,
            tokens=scaled2.astype(F32).T.astype(BF16),
            turns=[lane_turn(scaled[:24], count * k) for k in range(per)],
            total=first[3 * KU : 3 * KU + NV] + first[3 * KU + NV :],
            acc=None,
            atts={},
            sums={},
            spreads={},
        )

    def open_share(half, r):
        folded = msg[half["slots"][r], 0:32, 512:640]
        half["atts"][r] = tn(jnp.concatenate([folded, folded], axis=0), half["scaled2"])

    def hidden_units(half, r):
        slot = half["slots"][r]
        folded = msg[slot, 0:32, 0:512]
        folded2 = jnp.concatenate([folded, folded], axis=0)
        reads = msg[slot, 32:48, 0:512]
        for part in range(2):
            cut = slice(256 * part, 256 * part + 256)
            x = nn(half["tokens"], folded2[:, cut])
            kind = F32
            if half["whole"]:
                kind, x = BF16, x.astype(BF16)
            inner = x * (kind(math.sqrt(2 / math.pi)) + kind(math.sqrt(2 / math.pi) * 0.044715) * (x * x))
            hidden = (x + x * jnp.tanh(inner)).astype(BF16)
            term = nt(hidden, reads[:, cut])
            half["acc"] = term if half["acc"] is None else half["acc"] + term

    def scores(half, r):
        att, turns, per = half["atts"][r], half["turns"], half["per"]
        prods = []
        for h in range(2):
            for k in range(LEV):
                prod = att[24 * h : 24 * h + 24] * lane_turn(turns[k % per], F * (k // per))
                prods.append(prod[0:8] + prod[8:16] + prod[16:24])
        half["sums"][r] = nn(summing, jnp.concatenate(prods, axis=0).astype(BF16))

    def probabilities(half, r):
        expo = jnp.exp(half["sums"][r])
        prob = jnp.concatenate(
            [e / jnp.sum(e, axis=0, keepdims=True) for e in (expo[0:8], expo[8:16])], axis=0
        ).astype(BF16)
        half["spreads"][r] = nn(repeat, prob)

    def mix(half, r):
        att, spread, per = half["atts"][r], half["spreads"][r], half["per"]
        values = [lane_turn(att[48:80], half["count"] * k) for k in range(per)]
        mixed = None
        for k in range(LEV):
            term = spread[32 * k : 32 * k + 32] * lane_turn(values[k % per], F * (k // per))
            mixed = term if mixed is None else mixed + term
        half["total"] = half["total"] + mixed[0:16] + mixed[16:32]

    def shares(*pairs):
        for pair in pairs:
            open_share(*pair)
        stages = (scores, probabilities, mix)
        for i, pair in enumerate(pairs):
            hidden_units(*pair)
            for stage in stages[i : i + 1] if i < len(pairs) - 1 else stages[i:]:
                for other in pairs:
                    stage(*other)

    def turned_back(half):
        total, acc, count, per = half["total"], half["acc"], half["count"], half["per"]
        tiles = LEV // per
        pieces = []
        for t in range(tiles):
            pieces += [total[:, F * t : F * t + F], jnp.zeros((NV * (per - 1), F), F32)]
        turned = jnp.concatenate(pieces, axis=0).T
        wide = jnp.concatenate([acc, jnp.zeros((LEV * count, F - NV), F32)], axis=1)
        for t in range(tiles):
            block = wide[F * t : F * t + F]
            turned = turned + (block if t == 0 else pltpu.roll(block, NV * per * t, 1))
        result = turned[0:count]
        for q in range(1, per):
            result = result + pltpu.roll(turned[count * q : count * q + count], NV * q, 1)
        return result

    def finish(half, skip=0):
        live = jnp.concatenate([mask[ACROSS * p : ACROSS * p + ACROSS] for p in half["places"]], axis=0)
        buffer, n = tbufs[half["number"]], half["number"]
        buffer[0] = jnp.where(live > 0.5, turned_back(half), 0.0).astype(BF16)
        rows = pl.ds(ACROSS * skip, ACROSS * (len(half["places"]) - skip))
        half["sends"] = {}
        for r in (2, 3, 1):
            copy = pltpu.make_async_remote_copy(
                src_ref=buffer.at[0, rows], dst_ref=buffer.at[r, rows], send_sem=t_send.at[n, r], recv_sem=t_recv.at[n, r],
                device_id={"mp": peers[r]}, device_id_type=MESH,
            )
            copy.start()
            half["sends"][r] = copy

    def place_rows(half, skip=()):
        buffer = tbufs[half["number"]]
        for r, owner in ((0, core), (1, 1 - core)):
            if r:
                half["sends"][1].wait_recv()
            half["sends"][r + 2].wait_recv()
            block = buffer[r].astype(F32) + buffer[r + 2].astype(F32)
            for i, p in enumerate(half["places"]):
                for c in range(2):
                    if p not in skip:
                        at = ACROSS * i + 8 * c
                        tend[pl.ds(128 * owner + 8 * c + p, 8, stride=16), :] = block[at : at + 8]

    chip = (j, peers[1])
    inner = prepare(0, (1, 2, 3, 4), chip)
    shares((inner, 0))
    to_core.wait_recv()
    shares((inner, 1))
    finish(inner)

    to_chip.wait_recv()
    onward.start()
    send_f.wait_recv()
    for a, weight in enumerate((3 * KM[0, 3], 1.2 * KM[1, 3], 1.2 * KM[2, 3])):
        fresh[3, a] = fresh[3, a] - (d * F32(weight)) * f12[...]
    send_p.wait_recv()
    n12[...] = precv[...] - gown[pl.ds(first_row, 32)]
    eastern = prepare(1, (4, 5, 6, 7), chip)
    shares((eastern, 0), (eastern, 1))
    finish(eastern, skip=1)
    place_rows(inner)

    @pl.when(me == 0)
    def _():
        place_rows(eastern, skip=(4,))

    onward.wait_recv()

    @pl.when(me == 0)
    def _():
        pl.semaphore_wait(west_in, 1)
        send_f.start()
        send_p.start()

    for copy in (to_core, to_chip, onward, *inner["sends"].values()):
        copy.wait_send()

    @pl.when(core == 0)
    def _():
        send_g.wait_send()
        send_g_other.wait_send()

    known = {x: across(x, True) for x in (1, 2)}
    send_g.wait_recv()
    fresh[0, 0] = fresh[0, 0] - grecv[...].astype(F32)[0:Y]
    western = prepare(2, (0,), (0, 1, 2, 3), whole=True, known=known)
    western["total"] = western["total"] * 2.0
    shares((western, 0), (western, 1), (western, 2), (western, 3))
    result = jnp.where(mask[CELLS : CELLS + 32] > 0.5, turned_back(western), 0.0)
    for c in range(2):
        tend[pl.ds(8 * c, 16, stride=16), :] = result[16 * c : 16 * c + 16]

    @pl.when(me != 0)
    def _():
        place_rows(eastern, skip=(4,))

    for copy in (send_f, send_p, *eastern["sends"].values()):
        copy.wait_send()


def store(new, tend, new_out, tend_out, sem):
    first = pltpu.make_async_copy(new, new_out, sem.at[0])
    second = pltpu.make_async_copy(tend, tend_out, sem.at[1])
    first.start()
    second.start()
    first.wait()
    second.wait()


def local(elems, state_field, diffusion, stretch, w_in, lemb, w_qkv, w_out, w_up, w_down, w_read):
    state = jnp.transpose(state_field, (1, 0, 2)).reshape(4, 3, Y, F)
    operands = (
        state, diffusion.reshape(1, F), jnp.transpose(stretch), w_in, lemb,
        w_qkv, w_out, w_up, w_down, jnp.transpose(w_read),
    )
    vm = pltpu.VMEM
    dma = pltpu.SemaphoreType.DMA
    new, tend = pl.pallas_call(
        lambda *refs: kernel(elems, *refs),
        out_shape=(
            jax.ShapeDtypeStruct((4, 3, Y, F), F32),
            jax.ShapeDtypeStruct((256, F), F32),
        ),
        in_specs=[pl.BlockSpec(memory_space=pltpu.HBM)] * 10,
        out_specs=[pl.BlockSpec(memory_space=pltpu.VMEM)] * 2,
        scratch_shapes=[
            vm((4, 3, Y, F), F32),
            vm((4, 3, PAD + 64, F), F32),
            vm((7, ROWS, F), F32),
            vm((32, F), F32),
            vm((ROWS, F), F32),
            vm((Y, F), F32),
            vm((64, F), BF16),
            vm((64, F), BF16),
            vm((ROWS, F), F32),
            vm((32, F), F32),
            vm((1, F), F32),
            vm((8, 32), jnp.int32),
            vm((16, 512), BF16),
            vm((8, 512), BF16),
            vm((3, 512, 128), BF16),
            vm((128, 512), BF16),
            vm((512, 512), BF16),
            vm((512, 512), BF16),
            vm((16, 512), F32),
            vm((4, 48, 640), BF16),
            vm((CELLS + 32, F), F32),
            vm((4, 4 * ACROSS, F), BF16),
            vm((4, 4 * ACROSS, F), BF16),
            dma((11,)),
            dma((4,)),
            dma((3,)),
            dma((3,)),
            dma((3,)),
            dma((2, 4)),
            dma((2, 4)),
            pltpu.SemaphoreType.REGULAR,
            pltpu.SemaphoreType.REGULAR,
        ],
        compiler_params=pltpu.CompilerParams(
            collective_id=0, has_side_effects=True, vmem_limit_bytes=40 * 1024 * 1024
        ),
        name="step",
    )(*(pltpu.with_memory_space_constraint(x, pltpu.HBM) for x in operands))
    new, tend = (pltpu.with_memory_space_constraint(x, pltpu.VMEM) for x in (new, tend))
    new, tend = pl.pallas_call(
        store,
        out_shape=(jax.ShapeDtypeStruct(new.shape, F32), jax.ShapeDtypeStruct(tend.shape, F32)),
        in_specs=[pl.BlockSpec(memory_space=pltpu.VMEM)] * 2,
        out_specs=[pl.BlockSpec(memory_space=pltpu.HBM)] * 2,
        scratch_shapes=[dma((2,))],
        name="store",
    )(new, tend)
    return jnp.transpose(new.reshape(12, Y, F), (1, 0, 2)), tend.reshape(32, 8, F)


def solution(mesh):
    elems = mesh.shape["elem"]
    in_specs = (
        P(None, "elem", None),
        P(),
        P(None, "elem"),
        P(),
        P(),
        P(None, None, "mp"),
        P("mp", None),
        P(None, "mp"),
        P("mp", None),
        P(),
    )
    out_specs = (P(None, "elem", None), P(None, "elem", None))
    return jax.shard_map(
        lambda *args: local(elems, *args), mesh=mesh, in_specs=in_specs, out_specs=out_specs, check_vma=False
    )
```
